32 devices in a mesh: by: 4 (over z), bx: 8 (over y, x, core).
Axes of the slice: x: 2, y: 2, z: 4, core: 2. Of those that a mesh axis runs over, the one named last changes fastest.
Arguments:
- eastward_flow: float32 [62, 32, 2048], P(None, 'by', 'bx'), may hold values from -6 to 6
- northward_flow: float32 [62, 32, 2048], P(None, 'by', 'bx'), may hold values from -6 to 6
- heat_anomaly: float32 [62, 32, 2048], P(None, 'by', 'bx'), may hold values from -6 to 6
- salt_anomaly: float32 [62, 32, 2048], P(None, 'by', 'bx'), may hold values from -6 to 6
- air_stress_forcing: float32 [2, 32, 2048], P(None, 'by', 'bx'), may hold values from -6 to 6
- earlier_sea_height_load: float32 [32, 2048], P('by', 'bx'), may hold values from -6 to 6
- ocean_layer_depths: int32 [32, 2048], P('by', 'bx'), may hold values from 0 to 62, as said below
Outputs:
- east_new: float32 [62, 32, 2048], P(None, 'by', 'bx')
- north_new: float32 [62, 32, 2048], P(None, 'by', 'bx')
- temperature_new: float32 [62, 32, 2048], P(None, 'by', 'bx')
- salinity_new: float32 [62, 32, 2048], P(None, 'by', 'bx')
- surface_new: float32 [32, 2048], P('by', 'bx')
The draws below stay inside these ranges and needn't reach their ends.
Inputs may be any that keep to these rules, and one draw needn't show every extreme that they name: `ocean_layer_depths`: land (0) covers whole aligned tiles of 8 x 8 cells; every ocean column has 1 to 62 levels.
All inputs are finite; a program needn't handle non-finite values.
Results may differ from the reference program's by a relative error of at most 0.0003.
Values sent between devices are 32-bit elements; how exact they have to be, the bound alone decides.
No kernel may reach another device: no remote copies, remote signals or barrier semaphores. Data moves between devices by JAX's collectives and lax.ppermute only.
A program may use at most 192 MiB of HBM per device.

```python
import math
import jax
import jax.numpy as jnp

DEPTH_LAYERS = 62
ITERS = 4
NORTHWARD_CELLS = 32
EASTWARD_CELLS = 2048


def draw_ocean_layer_depths(key, part):
    key = jax.random.fold_in(key, 7)
    tile_key, level_key = jax.random.split(key)
    tiles = jax.random.randint(tile_key, (NORTHWARD_CELLS // 8 + 1, EASTWARD_CELLS // 8 + 1), 0, 5)
    land_cells = tiles[jnp.arange(NORTHWARD_CELLS) // 8][:, jnp.arange(EASTWARD_CELLS) // 8] == 0
    depth = jax.random.randint(level_key, (NORTHWARD_CELLS, EASTWARD_CELLS), 1, DEPTH_LAYERS + 1)
    return jnp.where(land_cells, 0, depth).astype(jnp.int32)


def steps_of(key, dims, cuts, least, high):
    factor_of = 1.0
    for dim, parts in cuts:
        steps = jax.random.uniform(jax.random.fold_in(jax.random.fold_in(key, 6), dim), (parts,), jnp.float32, least / len(cuts), high / len(cuts))
        factor_of = factor_of * jnp.repeat(jnp.exp(steps), dims[dim] // parts).reshape((-1,) + (1,) * (len(dims) - 1 - dim))
    return factor_of


def bell_draw(key, shape, deviation, limit, cuts=(), held_as=jnp.bfloat16):
    values = deviation * jax.random.normal(key, shape, jnp.float32)
    if cuts:
        values = values * steps_of(key, shape, cuts, -0.22, 0.18)
    return jnp.clip(values, -limit, limit).astype(held_as)


def setup_inputs(seed: int = 0) -> dict:
    keys = jax.random.split(jax.random.key(seed), 8)
    eastward_flow = bell_draw(keys[0], (DEPTH_LAYERS, NORTHWARD_CELLS, EASTWARD_CELLS), 1.0, 6.0, ((1, 4), (2, 8)), jnp.float32)
    northward_flow = bell_draw(keys[1], (DEPTH_LAYERS, NORTHWARD_CELLS, EASTWARD_CELLS), 1.0, 6.0, ((1, 4), (2, 8)), jnp.float32)
    heat_anomaly = bell_draw(keys[2], (DEPTH_LAYERS, NORTHWARD_CELLS, EASTWARD_CELLS), 1.0, 6.0, ((1, 4), (2, 8)), jnp.float32)
    salt_anomaly = bell_draw(keys[3], (DEPTH_LAYERS, NORTHWARD_CELLS, EASTWARD_CELLS), 1.0, 6.0, ((1, 4), (2, 8)), jnp.float32)
    air_stress_forcing = bell_draw(keys[4], (2, NORTHWARD_CELLS, EASTWARD_CELLS), 1.0, 6.0, ((1, 4), (2, 8)), jnp.float32)
    earlier_sea_height_load = bell_draw(keys[5], (NORTHWARD_CELLS, EASTWARD_CELLS), 1.0, 6.0, ((0, 4), (1, 8)), jnp.float32)
    ocean_layer_depths = draw_ocean_layer_depths(jax.random.fold_in(keys[7], 71), 0)
    return {"eastward_flow": eastward_flow, "northward_flow": northward_flow, "heat_anomaly": heat_anomaly, "salt_anomaly": salt_anomaly, "air_stress_forcing": air_stress_forcing, "earlier_sea_height_load": earlier_sea_height_load, "ocean_layer_depths": ocean_layer_depths}


KAPPA = 0.004
ADVECT = 0.25
PRESS = 0.1
WIND = 0.5
PHI = 0.5
DIVERGE = 2.0
LOWER = 0.2
UPPER = 2.0


def chebyshev_weights(count):
    middle = 0.5 * (UPPER + LOWER)
    half_span = 0.5 * (UPPER - LOWER)
    ratio_value = middle / half_span
    rho_now = 1.0 / ratio_value
    updates = []
    for index in range(count - 1):
        rho_next = 1.0 / (2.0 * ratio_value - rho_now)
        updates.append((rho_next * rho_now, 2.0 * rho_next / half_span))
        rho_now = rho_next
    return 1.0 / middle, updates


def shrink(field, width):
    return field[..., width:field.shape[-2] - width, width:field.shape[-1] - width]


def sides(field):
    return (field[..., 1:-1, 1:-1], field[..., 1:-1, 2:], field[..., 1:-1, :-2],
            field[..., 2:, 1:-1], field[..., :-2, 1:-1])


def laplacian(field, mask):
    cell_here, cell_east, cell_west, cell_north, cell_south = sides(field)
    mask_here, mask_east, mask_west, mask_north, mask_south = sides(mask)
    return (mask_here * mask_east * (cell_east - cell_here) + mask_here * mask_west * (cell_west - cell_here)
            + mask_here * mask_north * (cell_north - cell_here) + mask_here * mask_south * (cell_south - cell_here))


def gradients(field, mask):
    cell_here, cell_east, cell_west, cell_north, cell_south = sides(field)
    mask_here, mask_east, mask_west, mask_north, mask_south = sides(mask)
    along_x = 0.5 * (mask_here * mask_east * (cell_east - cell_here) + mask_here * mask_west * (cell_here - cell_west))
    along_y = 0.5 * (mask_here * mask_north * (cell_north - cell_here) + mask_here * mask_south * (cell_here - cell_south))
    return along_x, along_y


def wet_levels(depth, levels):
    return jnp.where(jnp.arange(levels)[:, None, None] < depth[None], 1.0, 0.0).astype(jnp.float32)


def coriolis_rows(first_row, count, total_rows):
    rows_float = (first_row + jnp.arange(count)).astype(jnp.float32)
    return (1.2 * jnp.sin(0.9 * math.pi * ((rows_float + 0.5) / total_rows - 0.5)))[:, None]


def tendency(ocean_state_arrays, wind, wet, coriolis):
    east_vel, north_vel, temper, saline = ocean_state_arrays
    inner = shrink(wet, 2)
    rotate = coriolis[2:coriolis.shape[0] - 2]
    density = (-0.8 * temper + 0.6 * saline) * wet
    pressure = PRESS * jnp.cumsum(density, axis=0)
    press_x, press_y = gradients(pressure, wet)
    press_x = shrink(press_x, 1)
    press_y = shrink(press_y, 1)
    east_in = shrink(east_vel, 2)
    north_in = shrink(north_vel, 2)
    inner_mask = shrink(wet, 1)

    def mixing(field):
        slope_x, slope_y = gradients(field, wet)
        carried = east_in * shrink(slope_x, 1) + north_in * shrink(slope_y, 1)
        smoothed = laplacian(laplacian(field, wet), inner_mask)
        return -ADVECT * carried - KAPPA * smoothed

    east_tend = inner * (rotate * north_in - press_x + mixing(east_vel))
    north_tend = inner * (-rotate * east_in - press_y + mixing(north_vel))
    east_top = east_tend[:1] + WIND * inner[:1] * shrink(wind[0:1], 2)
    north_top = north_tend[:1] + WIND * inner[:1] * shrink(wind[1:2], 2)
    east_tend = jnp.concatenate([east_top, east_tend[1:]], axis=0)
    north_tend = jnp.concatenate([north_top, north_tend[1:]], axis=0)
    return east_tend, north_tend, inner * mixing(temper), inner * mixing(saline)


def corner_depth(depth, levels):
    smallest = jnp.minimum(jnp.minimum(depth[:-1, :-1], depth[:-1, 1:]), jnp.minimum(depth[1:, :-1], depth[1:, 1:]))
    return smallest.astype(jnp.float32) / levels


def diagonal_of(depth):
    return PHI + 0.5 * (depth[1:, 1:] + depth[1:, :-1] + depth[:-1, 1:] + depth[:-1, :-1])


def apply_operator(field, depth):
    low_left = field[:-1, :-1]
    low_right = field[:-1, 1:]
    up_left = field[1:, :-1]
    up_right = field[1:, 1:]
    slope_x = 0.5 * (low_right + up_right - low_left - up_left)
    slope_y = 0.5 * (up_left + up_right - low_left - low_right)
    flux_x = depth * slope_x
    flux_y = depth * slope_y
    spread = 0.5 * ((flux_x[1:, 1:] + flux_x[:-1, 1:]) - (flux_x[1:, :-1] + flux_x[:-1, :-1])
                    + (flux_y[1:, 1:] + flux_y[1:, :-1]) - (flux_y[:-1, 1:] + flux_y[:-1, :-1]))
    return PHI * field[1:-1, 1:-1] - spread


def pad_global(field, width):
    wrapped = jnp.concatenate([field[..., -width:], field, field[..., :width]], axis=-1)
    padding = [(0, 0)] * (field.ndim - 2) + [(width, width), (0, 0)]
    return jnp.pad(wrapped, padding)


def region(field, width):
    return field[4 - width:field.shape[0] - 4 + width, 4 - width:field.shape[1] - 4 + width]


def reference(eastward_flow, northward_flow, heat_anomaly, salt_anomaly, air_stress_forcing, earlier_sea_height_load, ocean_layer_depths):
    depth_pad = pad_global(ocean_layer_depths, 4)
    ocean_state_arrays = (eastward_flow, northward_flow, heat_anomaly, salt_anomaly)
    wet_two = wet_levels(region(depth_pad, 2), DEPTH_LAYERS)
    coriolis = coriolis_rows(-2, NORTHWARD_CELLS + 4, NORTHWARD_CELLS)
    wind_pad = pad_global(air_stress_forcing, 2)
    first = tendency(tuple(pad_global(item, 2) for item in ocean_state_arrays), wind_pad, wet_two, coriolis)
    provisional = tuple(item + extra for item, extra in zip(ocean_state_arrays, first))
    second = tendency(tuple(pad_global(item, 2) for item in provisional), wind_pad, wet_two, coriolis)
    updated = tuple(item + 0.5 * (term_first + term_second) for item, term_first, term_second in zip(ocean_state_arrays, first, second))
    wet_in = shrink(wet_two, 2)
    transport_east = jnp.sum(wet_in * updated[0], axis=0) / DEPTH_LAYERS
    transport_north = jnp.sum(wet_in * updated[1], axis=0) / DEPTH_LAYERS
    column_one = jnp.where(region(depth_pad, 1) > 0, 1.0, 0.0).astype(jnp.float32)
    slope_x = gradients(pad_global(transport_east, 1), column_one)[0]
    slope_y = gradients(pad_global(transport_north, 1), column_one)[1]
    forcing = shrink(column_one, 1) * (PHI * earlier_sea_height_load - DIVERGE * (slope_x + slope_y))
    depth_one = corner_depth(region(depth_pad, 1), DEPTH_LAYERS)
    diagonal = diagonal_of(depth_one)
    opening, updates = chebyshev_weights(ITERS)
    residual = forcing - apply_operator(pad_global(earlier_sea_height_load, 1), depth_one)
    direction = opening * (residual / diagonal)
    solution = earlier_sea_height_load
    for index in range(ITERS):
        solution = solution + direction
        if index + 1 < ITERS:
            residual = residual - apply_operator(pad_global(direction, 1), depth_one)
            keep, push = updates[index]
            direction = keep * direction + push * (residual / diagonal)
    return updated[0], updated[1], updated[2], updated[3], solution
```

```python
import functools
import math

import jax
import jax.numpy as jnp
from jax import lax
from jax.experimental import pallas as pl
from jax.experimental.pallas import tpu as pltpu
from jax.sharding import PartitionSpec as P

ITERS = 4
KAPPA = 0.004
ADVECT = 0.25
PRESS = 0.1
WIND = 0.5
PHI = 0.5
DIVERGE = 2.0
LOWER = 0.2
UPPER = 2.0

SUB = 8
LANES = 128
FIELDS = 4
RIM = 4
EDGE = 8
EXTRA = 2
CHUNKS = (2, 2, 2, 2)
FAR = 1000000
F32 = jnp.float32


def chebyshev_weights(count):
    middle = 0.5 * (UPPER + LOWER)
    half_span = 0.5 * (UPPER - LOWER)
    ratio_value = middle / half_span
    rho_now = 1.0 / ratio_value
    updates = []
    for index in range(count - 1):
        rho_next = 1.0 / (2.0 * ratio_value - rho_now)
        updates.append((rho_next * rho_now, 2.0 * rho_next / half_span))
        rho_now = rho_next
    return (1.0 / middle, updates)


def first_level(chunk):
    return SUB * sum(CHUNKS[:chunk]) - (EXTRA if chunk else 0)


def chunk_levels(chunk):
    return SUB * CHUNKS[chunk] - (0 if chunk else EXTRA)


def pack_kernel(rows, *refs):
    count = len(CHUNKS)
    fields = refs[:FIELDS]
    wind, surface, depth = refs[FIELDS : FIELDS + 3]
    outs = refs[FIELDS + 3 :]
    halves = [(outs[2 * c], outs[2 * c + 1]) for c in range(count)]
    to_west, to_east = outs[2 * count : 2 * count + 2]
    held, sems = outs[2 * count + 2 :]

    def copy(f, lane):
        return pltpu.make_async_copy(
            fields[f].at[:, pl.ds(lane * LANES, LANES)], held.at[f, lane], sems.at[f, lane]
        )

    for f in range(FIELDS):
        for lane in range(2):
            copy(f, lane).start()
    flat = (
        (depth[...].astype(F32), surface[...]),
        (wind[0], wind[1]),
    )
    for f in range(FIELDS):
        for lane in range(2):
            copy(f, lane).wait()
        for c in range(count):
            for t in range(CHUNKS[c]):
                used = min(SUB, chunk_levels(c) - SUB * t)
                base = (first_level(c) + SUB * t) * rows
                for r in range(rows):
                    half = halves[c][r // RIM]
                    for lane in range(2):
                        span = pl.ds(lane * LANES, LANES)
                        half[f, r % RIM, t, pl.ds(0, used), span] = held[
                            f, lane, pl.ds(base + r, used, stride=rows), :
                        ]
                    for extra in range(SUB - used):
                        if f < len(flat):
                            line = flat[f][extra][r : r + 1, :]
                        else:
                            line = jnp.zeros((1, 2 * LANES), F32)
                        half[f, r % RIM, t, pl.ds(used + extra, 1), :] = line
    lanes = lax.broadcasted_iota(jnp.int32, (SUB, LANES), 1)
    slot = 0
    for c in range(count):
        for t in range(CHUNKS[c]):
            for group in range(2):
                west = jnp.zeros((SUB, LANES), F32)
                east = jnp.zeros((SUB, LANES), F32)
                for q in range(RIM):
                    for f in range(FIELDS):
                        place = (q * FIELDS + f) * EDGE
                        other = (place - EDGE) % LANES
                        block = halves[c][group][f, q, t]
                        low = block[:, :LANES]
                        high = block[:, LANES:]
                        if place:
                            low = pltpu.roll(low, place, 1)
                            high = pltpu.roll(high, place, 1)
                        west = jnp.where((lanes >= place) & (lanes < place + EDGE), low, west)
                        east = jnp.where((lanes >= other) & (lanes < other + EDGE), high, east)
                to_west[group, slot] = west
                to_east[group, slot] = east
            slot += 1


def pack(fields, wind, surface, depth):
    levels, rows, columns = fields[0].shape
    flat = [item.reshape(levels * rows, columns) for item in fields]
    total = sum(CHUNKS)
    shapes = []
    for tiles in CHUNKS:
        shapes += [jax.ShapeDtypeStruct((FIELDS, RIM, tiles, SUB, columns), F32)] * 2
    shapes += [jax.ShapeDtypeStruct((2, total, SUB, LANES), F32)] * 2
    outs = pl.pallas_call(
        functools.partial(pack_kernel, rows),
        out_shape=shapes,
        in_specs=[pl.BlockSpec(memory_space=pltpu.HBM)] * FIELDS
        + [pl.BlockSpec(memory_space=pltpu.VMEM)] * 3,
        out_specs=[pl.BlockSpec(memory_space=pltpu.VMEM)] * len(shapes),
        scratch_shapes=[
            pltpu.VMEM((FIELDS, 2, levels * rows, LANES), F32),
            pltpu.SemaphoreType.DMA((FIELDS, 2)),
        ],
        compiler_params=pltpu.CompilerParams(vmem_limit_bytes=12 * 1024 * 1024),
        name="pack",
    )(*flat, wind, surface, depth)
    halves = [(outs[2 * c], outs[2 * c + 1]) for c in range(len(CHUNKS))]
    return halves, outs[-2], outs[-1]


def east_of(value):
    return pltpu.roll(value, value.shape[-1] - 1, value.ndim - 1)


def west_of(value):
    return pltpu.roll(value, 1, value.ndim - 1)


def step_kernel(chunk, rows, *refs):
    first = chunk == 0
    last = chunk == len(CHUNKS) - 1
    tiles = CHUNKS[chunk]
    levels = chunk_levels(chunk)
    tall = rows + 2 * RIM
    refs = list(refs)

    def take(count):
        taken = refs[:count]
        del refs[:count]
        return taken

    rotate = take(1)[0]
    south, low, high, north = take(4)
    sides = take(4)
    if not first:
        depth_in, carry_in, sums_in = take(3)
        take(FIELDS)
    outs = take(FIELDS)
    if first:
        depth_out, surface_out = take(2)
    if last:
        sums_low, sums_high = take(2)
    else:
        carry_out, sums_out = take(2)
    cur, wets, wets_x, wets_w, wets_y, press, press_x, press_y, laps, mixes, between, held = take(12)
    if last:
        carry, sums = take(2)
    else:
        carry, sums = carry_out, sums_out
    deep = depth_out if first else depth_in
    (sems,) = take(1)

    if first:
        carry[...] = jnp.zeros(carry.shape, F32)
        sums[...] = jnp.zeros(sums.shape, F32)
    else:
        carry[...] = carry_in[...]
        sums[...] = sums_in[...]

    lanes = lax.broadcasted_iota(jnp.int32, (SUB, LANES), 1)
    start = sum(CHUNKS[:chunk])
    blocks = (south, low, high, north)
    wide = low.shape[-1] + LANES
    own = low.shape[-1]
    every = range(FIELDS)

    def rim_of(f, a, t):
        group, q = a // RIM, a % RIM
        if group == 0:
            from_east, from_west = sides[2][0, start + t], sides[2][1, start + t]
        elif group == 3:
            from_east, from_west = sides[3][0, start + t], sides[3][1, start + t]
        else:
            from_east, from_west = sides[0][group - 1, start + t], sides[1][group - 1, start + t]
        place = (q * FIELDS + f) * EDGE
        both = jnp.where((lanes >= place) & (lanes < place + EDGE), from_east, from_west)
        return pltpu.roll(both, LANES - place, 1) if place else both

    if first:
        for a in range(tall):
            for extra, ref in ((0, depth_out), (1, surface_out)):
                slot = SUB - EXTRA + extra
                line = blocks[a // RIM][0, a % RIM, tiles - 1]
                ref[pl.ds(a, 1), pl.ds(0, own)] = line[slot : slot + 1, :]
                line = rim_of(0, a, tiles - 1)
                ref[pl.ds(a, 1), pl.ds(own, LANES)] = line[slot : slot + 1, :]

    subs = lax.broadcasted_iota(jnp.int32, (SUB, wide), 0)

    def pressure(get, lowest, highest, carry_at):
        rows_p = range(lowest - 1, highest + 2)
        sums_p = [((-0.8 * PRESS) * get(2, a) + (0.6 * PRESS) * get(3, a)) * wets[a] for a in rows_p]
        for shift in (1, 2, 4):
            moved = [pltpu.roll(value, shift, 0) for value in sums_p]
            sums_p = [
                value + jnp.where(subs >= shift, other, 0.0) for value, other in zip(sums_p, moved)
            ]
        before = [carry[carry_at + k] for k in range(len(sums_p))]
        sums_p = [value + other for value, other in zip(sums_p, before)]
        ends = [jnp.broadcast_to(value[SUB - 1 : SUB, :], value.shape) for value in sums_p]
        for k, a in enumerate(rows_p):
            press[a] = sums_p[k]
            carry[carry_at + k] = ends[k]
        slope = wets_y[lowest - 1] * (press[lowest] - press[lowest - 1])
        for a in range(lowest, highest + 1):
            here = press[a]
            east, west = east_of(here), west_of(here)
            slope_before = slope
            slope = wets_y[a] * (press[a + 1] - here)
            press_x[a] = 0.5 * (wets_x[a] * (east - here) + wets_w[a] * (here - west))
            press_y[a] = 0.5 * (slope + slope_before)

    def tendency(get, lowest, highest, carry_at, emit):
        pressure(get, lowest, highest, carry_at)

        def turned(get_row):
            values = [get_row(f) for f in every]
            return values, [east_of(x) for x in values], [west_of(x) for x in values]

        below = [get(f, lowest - 2) for f in every]
        here, east, west = turned(lambda f: get(f, lowest - 1))
        face = wets_y[lowest - 2]
        up = [face * (x - y) for x, y in zip(here, below)]
        for a in range(lowest - 1, highest + 2):
            if a <= highest:
                after, east_after, west_after = turned(lambda f: get(f, a + 1))
            else:
                after = [get(f, a + 1) for f in every]
            face, side_x, side_w = wets_y[a], wets_x[a], wets_w[a]
            up_before = up
            up = [face * (x - y) for x, y in zip(after, here)]
            right = [side_x * (x - y) for x, y in zip(east, here)]
            left = [side_w * (x - y) for x, y in zip(here, west)]
            lap = [(right[f] - left[f]) + (up[f] - up_before[f]) for f in every]
            if lowest <= a <= highest:
                u, v = (-0.5 * ADVECT) * here[0], (-0.5 * ADVECT) * here[1]
                mixed = [u * (right[f] + left[f]) + v * (up[f] + up_before[f]) for f in every]
                turn = rotate[a] * wets[a]
                mixed[0] = mixed[0] + (turn * here[1] - press_x[a])
                mixed[1] = mixed[1] - (turn * here[0] + press_y[a])
                for f in every:
                    mixes[f, a] = mixed[f]
            for f in every:
                laps[f, a] = lap[f]
            if a <= highest:
                here, east, west = after, east_after, west_after

        below = [laps[f, lowest - 1] for f in every]
        here, east, west = turned(lambda f: laps[f, lowest])
        face = wets_y[lowest - 1]
        up = [face * (x - y) for x, y in zip(here, below)]
        for a in range(lowest, highest + 1):
            if a < highest:
                after, east_after, west_after = turned(lambda f: laps[f, a + 1])
            else:
                after = [laps[f, a + 1] for f in every]
            face, side_x, side_w = wets_y[a], wets_x[a], wets_w[a]
            up_before = up
            up = [face * (x - y) for x, y in zip(after, here)]
            smooth = [
                (side_x * (east[f] - here[f]) - side_w * (here[f] - west[f]))
                + (up[f] - up_before[f])
                for f in every
            ]
            emit(a, [mixes[f, a] - KAPPA * smooth[f] for f in every])
            if a < highest:
                here, east, west = after, east_after, west_after

    def tile(t, _):
        for a in range(tall):
            for f in every:
                cur[f, a, :, pl.ds(0, own)] = blocks[a // RIM][f, a % RIM, t]
                cur[f, a, :, pl.ds(own, LANES)] = rim_of(f, a, t)
        level = subs + (first_level(chunk) + SUB * t)
        if first:
            level = jnp.where(level >= levels, FAR, level)
        level = level.astype(F32)
        top = jnp.where(level == 0.0, WIND, 0.0)
        deeps = [deep[pl.ds(a, 1), :] for a in range(tall)]
        for a in range(tall):
            wets[a] = jnp.where(level < deeps[a], 1.0, 0.0)
            wets_x[a] = jnp.where(level < jnp.minimum(deeps[a], east_of(deeps[a])), 1.0, 0.0)
            wets_w[a] = jnp.where(level < jnp.minimum(deeps[a], west_of(deeps[a])), 1.0, 0.0)
            if a + 1 < tall:
                wets_y[a] = jnp.where(level < jnp.minimum(deeps[a], deeps[a + 1]), 1.0, 0.0)

        def winded(a, values):
            if not first:
                return values
            windy = top * wets[a]
            values = list(values)
            for f in range(2):
                slot = SUB - EXTRA + f
                line = jnp.concatenate(
                    [
                        blocks[a // RIM][1, a % RIM, tiles - 1][slot : slot + 1, :],
                        rim_of(1, a, tiles - 1)[slot : slot + 1, :],
                    ],
                    axis=1,
                )
                values[f] = values[f] + windy * line
            return values

        def emit_first(a, values):
            values = winded(a, values)
            values = [cur[f, a] + values[f] for f in every]
            for f in every:
                between[f, a] = values[f]

        tendency(lambda f, a: cur[f, a], 2, tall - 3, 0, emit_first)

        def emit_second(a, values):
            values = winded(a, values)
            news = [0.5 * ((cur[f, a] + between[f, a]) + values[f]) for f in every]
            r = a - RIM
            adds = [sums[f, r] + wets[a] * news[f] for f in range(2)]
            for f in range(2):
                sums[f, r] = adds[f]
            for f in every:
                for lane in range(2):
                    held[f, lane, pl.ds(t * (SUB * rows) + r, SUB, stride=rows), :] = news[f][
                        :, lane * LANES : (lane + 1) * LANES
                    ]

        tendency(lambda f, a: between[f, a], RIM, tall - RIM - 1, tall - 2, emit_second)
        return 0

    lax.fori_loop(0, tiles, tile, 0)

    def copy(f, lane):
        return pltpu.make_async_copy(
            held.at[f, lane, pl.ds(0, levels * rows)],
            outs[f].at[pl.ds(first_level(chunk) * rows, levels * rows), pl.ds(lane * LANES, LANES)],
            sems.at[f, lane],
        )

    for f in range(FIELDS):
        for lane in range(2):
            copy(f, lane).start()
    if last:
        depth_levels = first_level(chunk) + levels
        for f in range(2):
            for r in range(rows):
                line = jnp.sum(sums[f, r], axis=0, keepdims=True) / depth_levels
                if r < RIM:
                    sums_low[f, pl.ds(r, 1), :] = line
                else:
                    sums_high[f, pl.ds(r - RIM, 1), :] = line
    for f in range(FIELDS):
        for lane in range(2):
            copy(f, lane).wait()


def step(chunk, rows, levels, columns, rotate, blocks, sides, kept, news):
    first = chunk == 0
    last = chunk == len(CHUNKS) - 1
    tiles = CHUNKS[chunk]
    wide = columns + LANES
    tall = rows + 2 * RIM
    vmem = pl.BlockSpec(memory_space=pltpu.VMEM)
    hbm = pl.BlockSpec(memory_space=pl.ANY)
    operands = [rotate, *blocks, *sides]
    in_specs = [pl.BlockSpec(memory_space=pltpu.SMEM)] + [vmem] * 8
    if not first:
        operands += [*kept, *news]
        in_specs += [vmem] * 3 + [hbm] * FIELDS
    carry = (tall - 2 + rows + 2, SUB, wide)
    sums = (2, rows, SUB, wide)
    shapes = [jax.ShapeDtypeStruct((levels * rows, columns), F32)] * FIELDS
    out_specs = [hbm] * FIELDS
    row = pltpu.VMEM((tall, SUB, wide), F32)
    fields = pltpu.VMEM((FIELDS, tall, SUB, wide), F32)
    scratch = [fields] + [row] * 7 + [fields] * 3
    scratch += [pltpu.VMEM((FIELDS, 2, tiles * SUB * rows, LANES), F32)]
    if first:
        shapes += [jax.ShapeDtypeStruct((tall, wide), F32)] * 2
    if last:
        shapes += [jax.ShapeDtypeStruct((2, RIM, wide), F32)] * 2
        scratch += [pltpu.VMEM(carry, F32), pltpu.VMEM(sums, F32)]
    else:
        shapes += [jax.ShapeDtypeStruct(carry, F32), jax.ShapeDtypeStruct(sums, F32)]
    out_specs += [vmem] * (len(shapes) - FIELDS)
    scratch += [pltpu.SemaphoreType.DMA((FIELDS, 2))]
    aliases = {} if first else {len(operands) - FIELDS + f: f for f in range(FIELDS)}
    return pl.pallas_call(
        functools.partial(step_kernel, chunk, rows),
        out_shape=shapes,
        in_specs=in_specs,
        out_specs=out_specs,
        scratch_shapes=scratch,
        input_output_aliases=aliases,
        compiler_params=pltpu.CompilerParams(vmem_limit_bytes=16 * 1024 * 1024),
        name="step",
    )(*operands)


def solve_kernel(levels, rows, deep_ref, surface_ref, south, low, high, north, out):
    deep = deep_ref[...]
    surface = surface_ref[...]
    flows = [
        jnp.concatenate([south[f], low[f], high[f], north[f]], axis=0) for f in range(2)
    ]
    tall = deep.shape[0]

    def east(x):
        return pltpu.roll(x, x.shape[1] - 1, 1)

    def west(x):
        return pltpu.roll(x, 1, 1)

    def up(x):
        return pltpu.roll(x, tall - 1, 0)

    def down(x):
        return pltpu.roll(x, 1, 0)

    ocean = jnp.where(deep > 0.0, 1.0, 0.0)
    across = ocean * east(ocean) * (east(flows[0]) - flows[0])
    along = ocean * up(ocean) * (up(flows[1]) - flows[1])
    slope = 0.5 * (across + west(across)) + 0.5 * (along + down(along))
    forcing = ocean * (PHI * surface - DIVERGE * slope)
    pair = jnp.minimum(deep, east(deep))
    corner = jnp.minimum(pair, up(pair)) / levels
    column = corner + down(corner)
    diagonal = PHI + 0.5 * (column + west(column))

    def operator(e):
        plus = e + up(e)
        minus = up(e) - e
        flux_x = corner * (0.5 * (east(plus) - plus))
        flux_y = corner * (0.5 * (east(minus) + minus))
        fx = flux_x + down(flux_x)
        fy = flux_y + west(flux_y)
        spread = 0.5 * ((fx - west(fx)) + (fy - down(fy)))
        return PHI * e - spread

    opening, updates = chebyshev_weights(ITERS)
    residual = forcing - operator(surface)
    direction = opening * (residual / diagonal)
    total = surface
    for index in range(ITERS):
        total = total + direction
        if index + 1 < ITERS:
            residual = residual - operator(direction)
            keep, push = updates[index]
            direction = keep * direction + push * (residual / diagonal)
    out[...] = total[RIM : RIM + rows, : out.shape[1]]


def body(
    eastward_flow,
    northward_flow,
    heat_anomaly,
    salt_anomaly,
    air_stress_forcing,
    earlier_sea_height_load,
    ocean_layer_depths,
):
    levels, rows, columns = eastward_flow.shape
    assert rows == 2 * RIM and columns == 2 * LANES and levels + EXTRA == SUB * sum(CHUNKS)
    along_y, along_x = lax.axis_size("by"), lax.axis_size("bx")
    to_north = [(i, i + 1) for i in range(along_y - 1)]
    to_south = [(i + 1, i) for i in range(along_y - 1)]
    to_east = [(i, (i + 1) % along_x) for i in range(along_x)]
    to_west = [((i + 1) % along_x, i) for i in range(along_x)]

    row_index = lax.axis_index("by") * rows - RIM + jnp.arange(rows + 2 * RIM)
    rotate = 1.2 * jnp.sin(
        0.9 * math.pi * ((row_index.astype(F32) + 0.5) / (rows * along_y) - 0.5)
    )

    fields = (eastward_flow, northward_flow, heat_anomaly, salt_anomaly)
    halves, west_edge, east_edge = pack(
        fields, air_stress_forcing, earlier_sea_height_load, ocean_layer_depths
    )
    from_east = lax.ppermute(west_edge, "bx", to_west)
    from_west = lax.ppermute(east_edge, "bx", to_east)

    def send(low, high):
        return lax.ppermute(high, "by", to_north), lax.ppermute(low, "by", to_south)

    rims = [send(*halves[0])]
    corner_south = lax.ppermute(jnp.stack([from_east[1], from_west[1]]), "by", to_north)
    corner_north = lax.ppermute(jnp.stack([from_east[0], from_west[0]]), "by", to_south)
    *rims[0], corner_south, corner_north, low, high = lax.optimization_barrier(
        (*rims[0], corner_south, corner_north, *halves[1])
    )
    halves[1] = (low, high)
    rims.append(send(low, high))
    sides = (from_east, from_west, corner_south, corner_north)

    kept, news = None, None
    for chunk in range(len(CHUNKS)):
        low, high = halves[chunk]
        south, north = rims[chunk]
        outs = step(
            chunk, rows, levels, columns, rotate, (south, low, high, north), sides, kept, news
        )
        news, rest = outs[:FIELDS], outs[FIELDS:]
        if chunk == 0:
            deep, surface = rest[:2]
            rest = rest[2:]
        if chunk + 2 < len(CHUNKS):
            low, high, *rest = lax.optimization_barrier((*halves[chunk + 2], *rest))
            halves[chunk + 2] = (low, high)
            rims.append(send(low, high))
        kept = (deep, *rest)
    low, high = rest
    south = lax.ppermute(high, "by", to_north)
    north = lax.ppermute(low, "by", to_south)
    surface_new = pl.pallas_call(
        functools.partial(solve_kernel, levels, rows),
        out_shape=jax.ShapeDtypeStruct((rows, columns), F32),
        in_specs=[pl.BlockSpec(memory_space=pltpu.VMEM)] * 6,
        out_specs=pl.BlockSpec(memory_space=pltpu.VMEM),
        name="solve",
    )(deep, surface, south, low, high, north)
    shaped = [item.reshape(levels, rows, columns) for item in news]
    return (*shaped, surface_new)


def solution(mesh):
    return jax.shard_map(
        body,
        mesh=mesh,
        in_specs=(P(None, "by", "bx"),) * 5 + (P("by", "bx"),) * 2,
        out_specs=(P(None, "by", "bx"),) * 4 + (P("by", "bx"),),
        check_vma=False,
    )
```

```python
import functools
import math

import jax
import jax.numpy as jnp
from jax import lax
from jax.experimental import pallas as pl
from jax.experimental.pallas import tpu as pltpu
from jax.sharding import PartitionSpec as P

ITERS = 4
KAPPA = 0.004
ADVECT = 0.25
PRESS = 0.1
WIND = 0.5
PHI = 0.5
DIVERGE = 2.0
LOWER = 0.2
UPPER = 2.0

SUB = 8
LANES = 128
FIELDS = 4
RIM = 4
EDGE = 8
EXTRA = 2
CHUNKS = (2, 2, 2, 2)
AHEAD = 3
FAR = 1000000
BATCH = 4
GROUPS = ((0, 1), (2, 3))
SMALL_VMEM = 4 * 1024 * 1024
PACK_VMEM = 103 * 512 * 1024
F32 = jnp.float32


def chebyshev_weights(count):
    middle = 0.5 * (UPPER + LOWER)
    half_span = 0.5 * (UPPER - LOWER)
    ratio_value = middle / half_span
    rho_now = 1.0 / ratio_value
    updates = []
    for index in range(count - 1):
        rho_next = 1.0 / (2.0 * ratio_value - rho_now)
        updates.append((rho_next * rho_now, 2.0 * rho_next / half_span))
        rho_now = rho_next
    return (1.0 / middle, updates)


def swaps(count, first, ring):
    pairs = []
    for i in range(first, count if ring else count - 1, 2):
        j = (i + 1) % count
        pairs += [(i, j), (j, i)]
    return pairs


def first_level(chunk):
    return SUB * sum(CHUNKS[:chunk]) - (EXTRA if chunk else 0)


def chunk_levels(chunk):
    return SUB * CHUNKS[chunk] - (0 if chunk else EXTRA)


def parities():
    return lax.axis_index("by") & 1, lax.axis_index("bx") & 1


def first_rows():
    odd = lax.axis_index("by") & 1
    return (1 - odd) * RIM, odd * RIM


def place_tile(half, held, rows, group, f, chunk, t, line):
    used = min(SUB, chunk_levels(chunk) - SUB * t)
    base = (first_level(chunk) + SUB * t) * rows
    first = first_rows()[group]
    for q in range(RIM):
        for lane in range(2):
            half[f * RIM + q, t, pl.ds(0, used), pl.ds(lane * LANES, LANES)] = held[
                f, lane, pl.ds(base + first + q, used, stride=rows), :
            ]
        for extra in range(SUB - used):
            half[f * RIM + q, t, pl.ds(used + extra, 1), :] = line(f, extra, first + q)


def pack_kernel(rows, *refs):
    fields = refs[:FIELDS]
    flat = refs[FIELDS]
    *halves, across_a, across_b, held, sems = refs[FIELDS + 1 :]

    def copy(f, lane):
        return pltpu.make_async_copy(
            fields[f].at[:, pl.ds(lane * LANES, LANES)], held.at[f, lane], sems.at[f, lane]
        )

    for f in range(FIELDS):
        for lane in range(2):
            copy(f, lane).start()

    def line(f, extra, row):
        if f < 2:
            return flat[EXTRA * f + extra, pl.ds(row, 1), :]
        return jnp.zeros((1, 2 * LANES), F32)

    for f in range(FIELDS):
        for lane in range(2):
            copy(f, lane).wait()
        for c in range(len(CHUNKS)):
            for t in range(CHUNKS[c]):
                for group in range(2):
                    place_tile(halves[2 * c + group], held, rows, group, f, c, t, line)
    lanes = lax.broadcasted_iota(jnp.int32, (SUB, LANES), 1)
    odd = jnp.broadcast_to(lax.axis_index("bx") & 1, (SUB, LANES)) == 1
    slot = 0
    for c in range(len(CHUNKS)):
        for t in range(CHUNKS[c]):
            for group in range(2):
                west = jnp.zeros((SUB, LANES), F32)
                east = jnp.zeros((SUB, LANES), F32)
                for q in range(RIM):
                    for f in range(FIELDS):
                        place = (q * FIELDS + f) * EDGE
                        other = (place - EDGE) % LANES
                        block = halves[2 * c + group][f * RIM + q, t]
                        low = block[:, :LANES]
                        high = block[:, LANES:]
                        if place:
                            low = pltpu.roll(low, place, 1)
                            high = pltpu.roll(high, place, 1)
                        west = jnp.where((lanes >= place) & (lanes < place + EDGE), low, west)
                        east = jnp.where((lanes >= other) & (lanes < other + EDGE), high, east)
                across_a[group, slot] = jnp.where(odd, west, east)
                across_b[group, slot] = jnp.where(odd, east, west)
            slot += 1


def half_shapes(columns):
    return [
        jax.ShapeDtypeStruct((FIELDS * RIM + 1, tiles, SUB, columns), F32)
        for tiles in CHUNKS
        for _ in range(2)
    ]


def pack(fields, lines):
    levels, rows, columns = fields[0].shape
    flat = [item.reshape(levels * rows, columns) for item in fields]
    shapes = half_shapes(columns)
    shapes += [jax.ShapeDtypeStruct((2, sum(CHUNKS), SUB, LANES), F32)] * 2
    *halves, across_a, across_b = pl.pallas_call(
        functools.partial(pack_kernel, rows),
        out_shape=shapes,
        in_specs=[pl.BlockSpec(memory_space=pltpu.HBM)] * FIELDS
        + [pl.BlockSpec(memory_space=pltpu.VMEM)],
        out_specs=[pl.BlockSpec(memory_space=pltpu.VMEM)] * len(shapes),
        scratch_shapes=[
            pltpu.VMEM((FIELDS, 2, levels * rows, LANES), F32),
            pltpu.SemaphoreType.DMA((FIELDS, 2)),
        ],
        compiler_params=pltpu.CompilerParams(vmem_limit_bytes=PACK_VMEM),
        name="pack",
    )(*flat, lines)
    return halves, across_a, across_b


def rims_kernel(across_a, across_b, *refs):
    count = 2 * len(CHUNKS)
    halves, sems = refs[count : 2 * count], refs[2 * count]
    copies = []
    for k, half in enumerate(halves):
        slots = pl.ds(sum(CHUNKS[: k // 2]), CHUNKS[k // 2])
        for lane, across in enumerate((across_a, across_b)):
            copies.append(
                pltpu.make_async_copy(
                    across.at[k % 2, slots],
                    half.at[FIELDS * RIM, :, :, pl.ds(lane * LANES, LANES)],
                    sems.at[k, lane],
                )
            )
    for copy in copies:
        copy.start()
    for copy in copies:
        copy.wait()


def put_rims(halves, across_a, across_b):
    count = len(halves)
    anywhere = pl.BlockSpec(memory_space=pl.ANY)
    outs = pl.pallas_call(
        rims_kernel,
        out_shape=[jax.ShapeDtypeStruct(item.shape, F32) for item in halves],
        in_specs=[anywhere] * (count + 2),
        out_specs=[anywhere] * count,
        scratch_shapes=[pltpu.SemaphoreType.DMA((count, 2))],
        input_output_aliases={2 + k: k for k in range(count)},
        compiler_params=pltpu.CompilerParams(vmem_limit_bytes=SMALL_VMEM),
        name="rims",
    )(across_a, across_b, *halves)
    return [list(outs[k : k + 2]) for k in range(0, count, 2)]


def east_of(value):
    return pltpu.roll(value, value.shape[-1] - 1, value.ndim - 1)


def west_of(value):
    return pltpu.roll(value, 1, value.ndim - 1)


def step_kernel(chunk, rows, *refs):
    first = chunk == 0
    last = chunk == len(CHUNKS) - 1
    tiles = CHUNKS[chunk]
    levels = chunk_levels(chunk)
    tall = rows + 2 * RIM
    refs = list(refs)

    def take(count):
        taken = refs[:count]
        del refs[:count]
        return taken

    (rotate,) = take(1)
    met_a, own_a, own_b, met_b = blocks = take(4)
    if not first:
        deeps_in, carry_in, sums_in = take(3)
        take(FIELDS)
    outs = take(FIELDS)
    if first:
        deeps, depth_out, surface_out = take(3)
    else:
        deeps = deeps_in
    if last:
        sums_a, sums_b = take(2)
    else:
        carry_out, sums_out = take(2)
    cur, wets, wets_x, wets_w, wets_y, press, press_x, press_y, laps, mixes, between, held = take(12)
    if first:
        (winds,) = take(1)
    if last:
        carry, sums = take(2)
    else:
        carry, sums = carry_out, sums_out
    (sems,) = take(1)

    if first:
        carry[...] = jnp.zeros(carry.shape, F32)
        sums[...] = jnp.zeros(sums.shape, F32)
    else:
        carry[...] = carry_in[...]
        sums[...] = sums_in[...]

    lanes = lax.broadcasted_iota(jnp.int32, (SUB, LANES), 1)
    own = own_a.shape[-1]
    wide = own + LANES
    every = range(FIELDS)
    odd_y, odd_x = parities()
    bases = [odd_y * (RIM * k) + (1 - odd_y) * (RIM * (3 - k)) for k in range(4)]
    swapped = ((lanes // EDGE) & 1) != 1 - odd_x

    def rims_of(k, t):
        both = blocks[k][FIELDS * RIM, t]
        one, two = both[:, :LANES], both[:, LANES:]
        mixed = (jnp.where(swapped, one, two), jnp.where(swapped, two, one))

        def rim(f, q):
            place = (q * FIELDS + f) * EDGE
            return pltpu.roll(mixed[f % 2], LANES - place, 1) if place else mixed[f % 2]

        return rim

    if first:
        for k in range(4):
            rim = rims_of(k, tiles - 1)
            for q in range(RIM):
                block = [
                    jnp.concatenate([blocks[k][f * RIM + q, tiles - 1], rim(f, q)], axis=1)
                    for f in range(2)
                ]
                for f, extra, ref in (
                    (0, 0, deeps.at[0]),
                    (0, 1, deeps.at[1]),
                    (1, 0, winds.at[0]),
                    (1, 1, winds.at[1]),
                ):
                    slot = SUB - EXTRA + extra
                    ref[bases[k] + q] = jnp.broadcast_to(block[f][slot : slot + 1, :], (SUB, wide))
        for a in range(tall):
            surface_out[pl.ds(a, 1), :] = deeps[1, a, pl.ds(0, 1), :]
            depth_out[pl.ds(a, 1), :] = deeps[0, a, pl.ds(0, 1), :]
        for a in range(tall):
            here = deeps[0, a]
            deeps[1, a] = jnp.minimum(here, east_of(here))
            deeps[2, a] = jnp.minimum(here, west_of(here))
            deeps[3, a] = jnp.minimum(here, deeps[0, min(a + 1, tall - 1)])

    subs = lax.broadcasted_iota(jnp.int32, (SUB, wide), 0)

    def pressure(get, lowest, highest, carry_at):
        for first_row in range(lowest - 1, highest + 2, BATCH):
            rows_p = range(first_row, min(first_row + BATCH, highest + 2))
            sums_p = [
                ((-0.4 * PRESS) * get(2, a) + (0.3 * PRESS) * get(3, a)) * wets[a] for a in rows_p
            ]
            for shift in (1, 2, 4):
                moved = [pltpu.roll(value, shift, 0) for value in sums_p]
                sums_p = [
                    value + jnp.where(subs >= shift, other, 0.0)
                    for value, other in zip(sums_p, moved)
                ]
            places = [carry_at + a - (lowest - 1) for a in rows_p]
            sums_p = [value + carry[place] for value, place in zip(sums_p, places)]
            ends = [jnp.broadcast_to(value[SUB - 1 : SUB, :], value.shape) for value in sums_p]
            for k, a in enumerate(rows_p):
                press[a] = sums_p[k]
                carry[places[k]] = ends[k]
        slope = wets_y[lowest - 1] * (press[lowest] - press[lowest - 1])
        for first_row in range(lowest, highest + 1, BATCH):
            rows_p = range(first_row, min(first_row + BATCH, highest + 1))
            here = [press[a] for a in rows_p]
            east = [east_of(x) for x in here]
            west = [west_of(x) for x in here]
            across = [
                wets_x[a] * (east[k] - here[k]) + wets_w[a] * (here[k] - west[k])
                for k, a in enumerate(rows_p)
            ]
            here.append(press[rows_p[-1] + 1])
            slopes = [slope] + [
                wets_y[a] * (here[k + 1] - here[k]) for k, a in enumerate(rows_p)
            ]
            slope = slopes[-1]
            for k, a in enumerate(rows_p):
                press_x[a] = across[k]
                press_y[a] = slopes[k + 1] + slopes[k]

    def tendency(get, lowest, highest, carry_at, emit):
        pressure(get, lowest, highest, carry_at)
        for group in GROUPS:
            first_pass(get, lowest, highest, group)
        for group in GROUPS:
            second_pass(lowest, highest, group, emit)

    def turned(get, group, a):
        values = [get(f, a) for f in group]
        return values, [east_of(x) for x in values], [west_of(x) for x in values]

    def first_pass(get, lowest, highest, group):
        span = range(len(group))
        below = [get(f, lowest - 2) for f in group]
        here, east, west = turned(get, group, lowest - 1)
        face = wets_y[lowest - 2]
        up = [face * (x - y) for x, y in zip(here, below)]
        for a in range(lowest - 1, highest + 2):
            if a <= highest:
                after, east_after, west_after = turned(get, group, a + 1)
            else:
                after = [get(f, a + 1) for f in group]
            face, side_x, side_w = wets_y[a], wets_x[a], wets_w[a]
            up_before = up
            up = [face * (x - y) for x, y in zip(after, here)]
            right = [side_x * (x - y) for x, y in zip(east, here)]
            left = [side_w * (x - y) for x, y in zip(here, west)]
            lap = [(right[i] - left[i]) + (up[i] - up_before[i]) for i in span]
            if lowest <= a <= highest:
                flows = here if group[0] == 0 else [get(0, a), get(1, a)]
                u, v = (-0.5 * ADVECT) * flows[0], (-0.5 * ADVECT) * flows[1]
                mixed = [u * (right[i] + left[i]) + v * (up[i] + up_before[i]) for i in span]
                if group[0] == 0:
                    turn = rotate[pl.ds(a, 1), :] * wets[a]
                    mixed[0] = mixed[0] + (turn * here[1] - press_x[a])
                    mixed[1] = mixed[1] - (turn * here[0] + press_y[a])
                for i, f in enumerate(group):
                    mixes[f, a] = mixed[i]
            for i, f in enumerate(group):
                laps[f, a] = lap[i]
            if a <= highest:
                here, east, west = after, east_after, west_after

    def second_pass(lowest, highest, group, emit):
        span = range(len(group))

        def get(f, a):
            return laps[f, a]

        below = [get(f, lowest - 1) for f in group]
        here, east, west = turned(get, group, lowest)
        face = wets_y[lowest - 1]
        up = [face * (x - y) for x, y in zip(here, below)]
        for a in range(lowest, highest + 1):
            if a < highest:
                after, east_after, west_after = turned(get, group, a + 1)
            else:
                after = [get(f, a + 1) for f in group]
            face, side_x, side_w = wets_y[a], wets_x[a], wets_w[a]
            up_before = up
            up = [face * (x - y) for x, y in zip(after, here)]
            smooth = [
                (side_x * (east[i] - here[i]) - side_w * (here[i] - west[i]))
                + (up[i] - up_before[i])
                for i in span
            ]
            emit(a, group, [mixes[f, a] - KAPPA * smooth[i] for i, f in enumerate(group)])
            if a < highest:
                here, east, west = after, east_after, west_after

    def tile(t, _):
        for k in range(4):
            rim = rims_of(k, t)
            for q in range(RIM):
                for f in every:
                    cur[f, bases[k] + q, :, pl.ds(0, own)] = blocks[k][f * RIM + q, t]
                    cur[f, bases[k] + q, :, pl.ds(own, LANES)] = rim(f, q)
        level = subs + (first_level(chunk) + SUB * t)
        if first:
            level = jnp.where(level >= levels, FAR, level)
        level = level.astype(F32)
        top = jnp.where(level == 0.0, WIND, 0.0)
        for a in range(tall):
            for k, ref in enumerate((wets, wets_x, wets_w, wets_y)):
                ref[a] = jnp.where(level < deeps[k, a], 1.0, 0.0)

        def winded(a, group, values):
            if not first or group[0] != 0:
                return values
            windy = top * wets[a]
            return [values[f] + windy * winds[f, a] for f in range(2)] + values[2:]

        def emit_first(a, group, values):
            values = winded(a, group, values)
            values = [cur[f, a] + value for f, value in zip(group, values)]
            for f, value in zip(group, values):
                between[f, a] = value

        tendency(lambda f, a: cur[f, a], 2, tall - 3, 0, emit_first)

        def emit_second(a, group, values):
            values = winded(a, group, values)
            news = [0.5 * ((cur[f, a] + between[f, a]) + value) for f, value in zip(group, values)]
            r = a - RIM
            if group[0] == 0:
                adds = [sums[f, r] + wets[a] * news[f] for f in range(2)]
                for f in range(2):
                    sums[f, r] = adds[f]
            for f, new in zip(group, news):
                for lane in range(2):
                    held[f, lane, pl.ds(t * (SUB * rows) + r, SUB, stride=rows), :] = new[
                        :, lane * LANES : (lane + 1) * LANES
                    ]

        tendency(lambda f, a: between[f, a], RIM, tall - RIM - 1, tall - 2, emit_second)

        @pl.when(t < tiles - 1)
        def _():
            for f in every:
                for lane in range(2):
                    copy(f, lane, t, SUB).start()

        return 0

    def copy(f, lane, t, count):
        size = count * rows
        at = (first_level(chunk) + SUB * t) * rows
        return pltpu.make_async_copy(
            held.at[f, lane, pl.ds(t * (SUB * rows), size)],
            outs[f].at[pl.ds(at, size), pl.ds(lane * LANES, LANES)],
            sems.at[t, f, lane],
        )

    lax.fori_loop(0, tiles, tile, 0)
    final = levels - SUB * (tiles - 1)
    for f in every:
        for lane in range(2):
            copy(f, lane, tiles - 1, final).start()
    if last:
        depth_levels = first_level(chunk) + levels
        for f in range(2):
            for ref, at in ((sums_a, (1 - odd_y) * RIM), (sums_b, odd_y * RIM)):
                for q in range(RIM):
                    line = jnp.sum(sums[f, at + q], axis=0, keepdims=True) / depth_levels
                    ref[f, pl.ds(q, 1), :] = line
    for t in range(tiles):
        for f in every:
            for lane in range(2):
                copy(f, lane, t, final if t == tiles - 1 else SUB).wait()


def step(chunk, rows, levels, columns, rotate, blocks, kept, news):
    first = chunk == 0
    last = chunk == len(CHUNKS) - 1
    tiles = CHUNKS[chunk]
    wide = columns + LANES
    tall = rows + 2 * RIM
    vmem = pl.BlockSpec(memory_space=pltpu.VMEM)
    hbm = pl.BlockSpec(memory_space=pl.ANY)
    operands = [rotate, *blocks]
    in_specs = [vmem] * 5
    if not first:
        operands += [*kept, *news]
        in_specs += [vmem] * 3 + [hbm] * FIELDS
    carry = (tall - 2 + rows + 2, SUB, wide)
    sums = (2, rows, SUB, wide)
    shapes = [jax.ShapeDtypeStruct((levels * rows, columns), F32)] * FIELDS
    out_specs = [hbm] * FIELDS
    row = pltpu.VMEM((tall, SUB, wide), F32)
    fields = pltpu.VMEM((FIELDS, tall, SUB, wide), F32)
    scratch = [fields] + [row] * 7 + [fields] * 3
    scratch += [pltpu.VMEM((FIELDS, 2, tiles * SUB * rows, LANES), F32)]
    if first:
        shapes += [jax.ShapeDtypeStruct((4, tall, SUB, wide), F32)]
        shapes += [jax.ShapeDtypeStruct((tall, wide), F32)] * 2
        scratch += [pltpu.VMEM((2, tall, SUB, wide), F32)]
    if last:
        shapes += [jax.ShapeDtypeStruct((2, RIM, wide), F32)] * 2
        scratch += [pltpu.VMEM(carry, F32), pltpu.VMEM(sums, F32)]
    else:
        shapes += [jax.ShapeDtypeStruct(carry, F32), jax.ShapeDtypeStruct(sums, F32)]
    out_specs += [vmem] * (len(shapes) - FIELDS)
    scratch += [pltpu.SemaphoreType.DMA((tiles, FIELDS, 2))]
    aliases = {} if first else {len(operands) - FIELDS + f: f for f in range(FIELDS)}
    return pl.pallas_call(
        functools.partial(step_kernel, chunk, rows),
        out_shape=shapes,
        in_specs=in_specs,
        out_specs=out_specs,
        scratch_shapes=scratch,
        input_output_aliases=aliases,
        compiler_params=pltpu.CompilerParams(vmem_limit_bytes=16 * 1024 * 1024),
        name="step",
    )(*operands)


def shift_rows(x, count):
    return pltpu.roll(x, count % x.shape[0], 0)


def weighed(weights, e):
    east, west = east_of(e), west_of(e)
    return (
        weights[0] * shift_rows(east, -1) + weights[1] * shift_rows(west, -1)
    ) + (weights[2] * shift_rows(east, 1) + weights[3] * shift_rows(west, 1))


def prepare_kernel(levels, deep_ref, surface_ref, out):
    deep = deep_ref[...]
    surface = surface_ref[...]
    ocean = jnp.where(deep > 0.0, 1.0, 0.0)
    pair = jnp.minimum(deep, east_of(deep))
    north_east = jnp.minimum(pair, shift_rows(pair, -1)) / levels
    north_west = west_of(north_east)
    corners = (north_east, north_west, shift_rows(north_east, 1), shift_rows(north_west, 1))
    share = 1.0 / (PHI + 0.5 * ((corners[0] + corners[1]) + (corners[2] + corners[3])))
    weights = [(0.5 * share) * corner for corner in corners]
    for k in range(4):
        out[k] = weights[k]
    out[4] = (PHI * ocean * share) * surface - (surface - weighed(weights, surface))
    across = ocean * east_of(ocean)
    along = ocean * shift_rows(ocean, -1)
    scale = (-0.5 * DIVERGE) * share
    out[5] = scale * across
    out[6] = scale * west_of(across)
    out[7] = scale * along
    out[8] = scale * shift_rows(along, 1)
    out[9] = surface


def solve_kernel(rows, ready, met_a, own_a, own_b, met_b, out):
    odd = jnp.broadcast_to(parities()[0], ready.shape[1:]) == 1
    flows = []
    for f in range(2):
        lines = [ref[f] for ref in (met_a, own_a, own_b, met_b)]
        flows.append(
            jnp.where(odd, jnp.concatenate(lines, axis=0), jnp.concatenate(lines[::-1], axis=0))
        )
    weights = [ready[k] for k in range(4)]
    east, north = flows
    scaled = ready[4] + (
        (ready[5] * (east_of(east) - east) + ready[6] * (east - west_of(east)))
        + (
            ready[7] * (shift_rows(north, -1) - north)
            + ready[8] * (north - shift_rows(north, 1))
        )
    )
    opening, updates = chebyshev_weights(ITERS)
    direction = opening * scaled
    total = ready[9]
    for index in range(ITERS):
        total = total + direction
        if index + 1 < ITERS:
            scaled = scaled - (direction - weighed(weights, direction))
            keep, push = updates[index]
            direction = keep * direction + push * scaled
    out[...] = total[RIM : RIM + rows, : out.shape[1]]


def body(
    eastward_flow,
    northward_flow,
    heat_anomaly,
    salt_anomaly,
    air_stress_forcing,
    earlier_sea_height_load,
    ocean_layer_depths,
):
    levels, rows, columns = eastward_flow.shape
    assert rows == 2 * RIM and columns == 2 * LANES and levels + EXTRA == SUB * sum(CHUNKS)
    along_y, along_x = lax.axis_size("by"), lax.axis_size("bx")
    pairs_y = (swaps(along_y, 0, False), swaps(along_y, 1, False))
    pairs_x = (swaps(along_x, 0, True), swaps(along_x, 1, True))
    row_index = lax.axis_index("by") * rows - RIM + jnp.arange(rows + 2 * RIM)
    rotate = 1.2 * jnp.sin(
        0.9 * math.pi * ((row_index.astype(F32) + 0.5) / (rows * along_y) - 0.5)
    )
    rotate = jnp.broadcast_to(rotate[:, None], (rows + 2 * RIM, columns + LANES))

    fields = (eastward_flow, northward_flow, heat_anomaly, salt_anomaly)
    lines = jnp.concatenate(
        [
            jnp.stack([ocean_layer_depths.astype(F32), earlier_sea_height_load]),
            air_stress_forcing,
        ]
    )
    halves, edge_a, edge_b = pack(fields, lines)
    across_a = lax.ppermute(edge_a, "bx", pairs_x[0])
    across_b = lax.ppermute(edge_b, "bx", pairs_x[1])
    halves = put_rims(halves, across_a, across_b)

    def send(own):
        return [lax.ppermute(item, "by", pairs) for item, pairs in zip(own, pairs_y)]

    rims = [send(halves[chunk]) for chunk in range(AHEAD)]
    kept, news = None, None
    for chunk in range(len(CHUNKS)):
        own_a, own_b = halves[chunk]
        met_a, met_b = rims[chunk]
        blocks = (met_a, own_a, own_b, met_b)
        outs = step(chunk, rows, levels, columns, rotate, blocks, kept, news)
        news, rest = outs[:FIELDS], outs[FIELDS:]
        if chunk == 0:
            deeps, depth_wide, surface_wide = rest[:3]
            rest = rest[3:]
        later = chunk + AHEAD
        if later < len(CHUNKS):
            *halves[later], one, two = lax.optimization_barrier((*halves[later], *rest))
            rest = (one, two)
            rims.append(send(halves[later]))
        kept = (deeps, *rest)
    own_a, own_b = rest
    depth_wide, surface_wide, own_a, own_b = lax.optimization_barrier(
        (depth_wide, surface_wide, own_a, own_b)
    )
    met_a, met_b = send((own_a, own_b))
    vmem = pl.BlockSpec(memory_space=pltpu.VMEM)
    ready = pl.pallas_call(
        functools.partial(prepare_kernel, levels),
        out_shape=jax.ShapeDtypeStruct((10, *depth_wide.shape), F32),
        in_specs=[vmem] * 2,
        out_specs=vmem,
        compiler_params=pltpu.CompilerParams(vmem_limit_bytes=SMALL_VMEM),
        name="prepare",
    )(depth_wide, surface_wide)
    surface_new = pl.pallas_call(
        functools.partial(solve_kernel, rows),
        out_shape=jax.ShapeDtypeStruct((rows, columns), F32),
        in_specs=[vmem] * 5,
        out_specs=vmem,
        compiler_params=pltpu.CompilerParams(vmem_limit_bytes=SMALL_VMEM),
        name="solve",
    )(ready, met_a, own_a, own_b, met_b)
    shaped = [item.reshape(levels, rows, columns) for item in news]
    return (*shaped, surface_new)


def solution(mesh):
    return jax.shard_map(
        body,
        mesh=mesh,
        in_specs=(P(None, "by", "bx"),) * 5 + (P("by", "bx"),) * 2,
        out_specs=(P(None, "by", "bx"),) * 4 + (P("by", "bx"),),
        check_vma=False,
    )
```

```python
import functools
import math

import jax
import jax.numpy as jnp
from jax import lax
from jax.experimental import pallas as pl
from jax.experimental.pallas import tpu as pltpu
from jax.sharding import PartitionSpec as P

ITERS = 4
KAPPA = 0.004
ADVECT = 0.25
PRESS = 0.1
WIND = 0.5
PHI = 0.5
DIVERGE = 2.0
LOWER = 0.2
UPPER = 2.0

SUB = 8
LANES = 128
FIELDS = 4
RIM = 4
EDGE = 8
EXTRA = 2
CHUNKS = (2, 2, 2, 2)
AHEAD = 3
FAR = 1000000
BATCH = 4
GROUPS = ((0,), (1,), (2,), (3,))
SMALL_VMEM = 4 * 1024 * 1024
PACK_VMEM = 8 * 1024 * 1024
F32 = jnp.float32


def chebyshev_weights(count):
    middle = 0.5 * (UPPER + LOWER)
    half_span = 0.5 * (UPPER - LOWER)
    ratio_value = middle / half_span
    rho_now = 1.0 / ratio_value
    updates = []
    for index in range(count - 1):
        rho_next = 1.0 / (2.0 * ratio_value - rho_now)
        updates.append((rho_next * rho_now, 2.0 * rho_next / half_span))
        rho_now = rho_next
    return (1.0 / middle, updates)


def swaps(count, first, ring):
    pairs = []
    for i in range(first, count if ring else count - 1, 2):
        j = (i + 1) % count
        pairs += [(i, j), (j, i)]
    return pairs


def first_level(chunk):
    return SUB * sum(CHUNKS[:chunk]) - (EXTRA if chunk else 0)


def chunk_levels(chunk):
    return SUB * CHUNKS[chunk] - (0 if chunk else EXTRA)


def parities():
    return lax.axis_index("by") & 1, lax.axis_index("bx") & 1


def first_rows():
    odd = lax.axis_index("by") & 1
    return (1 - odd) * RIM, odd * RIM


def place_tile(half, held, rows, group, f, chunk, t, line):
    used = min(SUB, chunk_levels(chunk) - SUB * t)
    base = (first_level(chunk) + SUB * t) * rows
    first = first_rows()[group]
    for q in range(RIM):
        for lane in range(2):
            half[f * RIM + q, t, pl.ds(0, used), pl.ds(lane * LANES, LANES)] = held[
                f, lane, pl.ds(base + first + q, used, stride=rows), :
            ]
        for extra in range(SUB - used):
            half[f * RIM + q, t, pl.ds(used + extra, 1), :] = line(f, extra, first + q)


def pack_kernel(rows, *refs):
    fields = refs[:FIELDS]
    sources = refs[FIELDS : FIELDS + 3]
    *halves, across_a, across_b, held, sems, flat, depth, sems_flat = refs[FIELDS + 3 :]
    small = [
        pltpu.make_async_copy(source, into, sems_flat.at[k])
        for k, (source, into) in enumerate(
            zip(sources, (flat.at[pl.ds(EXTRA, EXTRA)], flat.at[1], depth))
        )
    ]

    def copy(f, lane):
        return pltpu.make_async_copy(
            fields[f].at[:, pl.ds(lane * LANES, LANES)], held.at[f, lane], sems.at[f, lane]
        )

    for f in range(FIELDS):
        for lane in range(2):
            copy(f, lane).start()
    for item in small:
        item.start()
    for item in small:
        item.wait()
    flat[0] = depth[...].astype(F32)

    def line(f, extra, row):
        if f < 2:
            return flat[EXTRA * f + extra, pl.ds(row, 1), :]
        return jnp.zeros((1, 2 * LANES), F32)

    for f in range(FIELDS):
        for lane in range(2):
            copy(f, lane).wait()
        for c in range(len(CHUNKS)):
            for t in range(CHUNKS[c]):
                for group in range(2):
                    place_tile(halves[2 * c + group], held, rows, group, f, c, t, line)
    lanes = lax.broadcasted_iota(jnp.int32, (SUB, LANES), 1)
    odd = jnp.broadcast_to(lax.axis_index("bx") & 1, (SUB, LANES)) == 1
    slot = 0
    for c in range(len(CHUNKS)):
        for t in range(CHUNKS[c]):
            for group in range(2):
                west = jnp.zeros((SUB, LANES), F32)
                east = jnp.zeros((SUB, LANES), F32)
                for q in range(RIM):
                    for f in range(FIELDS):
                        place = (q * FIELDS + f) * EDGE
                        other = (place - EDGE) % LANES
                        block = halves[2 * c + group][f * RIM + q, t]
                        low = block[:, :LANES]
                        high = block[:, LANES:]
                        if place:
                            low = pltpu.roll(low, place, 1)
                            high = pltpu.roll(high, place, 1)
                        west = jnp.where((lanes >= place) & (lanes < place + EDGE), low, west)
                        east = jnp.where((lanes >= other) & (lanes < other + EDGE), high, east)
                across_a[group, slot] = jnp.where(odd, west, east)
                across_b[group, slot] = jnp.where(odd, east, west)
            slot += 1


def half_shapes(columns):
    return [
        jax.ShapeDtypeStruct((FIELDS * RIM + 1, tiles, SUB, columns), F32)
        for tiles in CHUNKS
        for _ in range(2)
    ]


def pack(fields, lines):
    levels, rows, columns = fields[0].shape
    flat = [item.reshape(levels * rows, columns) for item in fields]
    shapes = half_shapes(columns)
    shapes += [jax.ShapeDtypeStruct((2, sum(CHUNKS), SUB, LANES), F32)] * 2
    *halves, across_a, across_b = pl.pallas_call(
        functools.partial(pack_kernel, rows),
        out_shape=shapes,
        in_specs=[pl.BlockSpec(memory_space=pltpu.HBM)] * (FIELDS + 3),
        out_specs=[pl.BlockSpec(memory_space=pltpu.VMEM)] * len(shapes),
        scratch_shapes=[
            pltpu.VMEM((FIELDS, 2, levels * rows, LANES), F32),
            pltpu.SemaphoreType.DMA((FIELDS, 2)),
            pltpu.VMEM((2 * EXTRA, rows, columns), F32),
            pltpu.VMEM((rows, columns), jnp.int32),
            pltpu.SemaphoreType.DMA((3,)),
        ],
        compiler_params=pltpu.CompilerParams(vmem_limit_bytes=PACK_VMEM),
        name="pack",
    )(*[pltpu.with_memory_space_constraint(item, pltpu.HBM) for item in (*flat, *lines)])
    return halves, across_a, across_b


def rims_kernel(across_a, across_b, *refs):
    count = 2 * len(CHUNKS)
    halves, sems = refs[count : 2 * count], refs[2 * count]
    copies = []
    for k, half in enumerate(halves):
        slots = pl.ds(sum(CHUNKS[: k // 2]), CHUNKS[k // 2])
        for lane, across in enumerate((across_a, across_b)):
            copies.append(
                pltpu.make_async_copy(
                    across.at[k % 2, slots],
                    half.at[FIELDS * RIM, :, :, pl.ds(lane * LANES, LANES)],
                    sems.at[k, lane],
                )
            )
    for copy in copies:
        copy.start()
    for copy in copies:
        copy.wait()


def put_rims(halves, across_a, across_b):
    count = len(halves)
    anywhere = pl.BlockSpec(memory_space=pl.ANY)
    outs = pl.pallas_call(
        rims_kernel,
        out_shape=[jax.ShapeDtypeStruct(item.shape, F32) for item in halves],
        in_specs=[anywhere] * (count + 2),
        out_specs=[anywhere] * count,
        scratch_shapes=[pltpu.SemaphoreType.DMA((count, 2))],
        input_output_aliases={2 + k: k for k in range(count)},
        compiler_params=pltpu.CompilerParams(vmem_limit_bytes=SMALL_VMEM),
        name="rims",
    )(across_a, across_b, *halves)
    return [list(outs[k : k + 2]) for k in range(0, count, 2)]


def east_of(value):
    return pltpu.roll(value, value.shape[-1] - 1, value.ndim - 1)


def west_of(value):
    return pltpu.roll(value, 1, value.ndim - 1)


def step_kernel(chunk, rows, *refs):
    first = chunk == 0
    last = chunk == len(CHUNKS) - 1
    tiles = CHUNKS[chunk]
    levels = chunk_levels(chunk)
    tall = rows + 2 * RIM
    refs = list(refs)

    def take(count):
        taken = refs[:count]
        del refs[:count]
        return taken

    (rotate,) = take(1)
    met_a, own_a, own_b, met_b = blocks = take(4)
    if not first:
        deeps_in, carry_in, sums_in = take(3)
        take(FIELDS)
    outs = take(FIELDS)
    if first:
        deeps, depth_out, surface_out = take(3)
    else:
        deeps = deeps_in
    if last:
        sums_a, sums_b = take(2)
    else:
        carry_out, sums_out = take(2)
    cur, wets, wets_x, wets_w, wets_y, press, press_x, press_y, laps, mixes, between, held = take(12)
    if first:
        (winds,) = take(1)
    if last:
        carry, sums = take(2)
    else:
        carry, sums = carry_out, sums_out
    (sems,) = take(1)

    if first:
        carry[...] = jnp.zeros(carry.shape, F32)
        sums[...] = jnp.zeros(sums.shape, F32)
    else:
        carry[...] = carry_in[...]
        sums[...] = sums_in[...]

    lanes = lax.broadcasted_iota(jnp.int32, (SUB, LANES), 1)
    own = own_a.shape[-1]
    wide = own + LANES
    every = range(FIELDS)
    odd_y, odd_x = parities()
    bases = [odd_y * (RIM * k) + (1 - odd_y) * (RIM * (3 - k)) for k in range(4)]
    swapped = ((lanes // EDGE) & 1) != 1 - odd_x

    def rims_of(k, t):
        both = blocks[k][FIELDS * RIM, t]
        one, two = both[:, :LANES], both[:, LANES:]
        mixed = (jnp.where(swapped, one, two), jnp.where(swapped, two, one))

        def rim(f, q):
            place = (q * FIELDS + f) * EDGE
            return pltpu.roll(mixed[f % 2], LANES - place, 1) if place else mixed[f % 2]

        return rim

    if first:
        for k in range(4):
            rim = rims_of(k, tiles - 1)
            for q in range(RIM):
                block = [
                    jnp.concatenate([blocks[k][f * RIM + q, tiles - 1], rim(f, q)], axis=1)
                    for f in range(2)
                ]
                for f, extra, ref in (
                    (0, 0, deeps.at[0]),
                    (0, 1, deeps.at[1]),
                    (1, 0, winds.at[0]),
                    (1, 1, winds.at[1]),
                ):
                    slot = SUB - EXTRA + extra
                    ref[bases[k] + q] = jnp.broadcast_to(block[f][slot : slot + 1, :], (SUB, wide))
        for a in range(tall):
            surface_out[pl.ds(a, 1), :] = deeps[1, a, pl.ds(0, 1), :]
            depth_out[pl.ds(a, 1), :] = deeps[0, a, pl.ds(0, 1), :]
        for a in range(tall):
            here = deeps[0, a]
            deeps[1, a] = jnp.minimum(here, east_of(here))
            deeps[2, a] = jnp.minimum(here, west_of(here))
            deeps[3, a] = jnp.minimum(here, deeps[0, min(a + 1, tall - 1)])

    subs = lax.broadcasted_iota(jnp.int32, (SUB, wide), 0)

    def pressure(get, lowest, highest, carry_at):
        for first_row in range(lowest - 1, highest + 2, BATCH):
            rows_p = range(first_row, min(first_row + BATCH, highest + 2))
            sums_p = [
                ((-0.4 * PRESS) * get(2, a) + (0.3 * PRESS) * get(3, a)) * wets[a] for a in rows_p
            ]
            for shift in (1, 2, 4):
                moved = [pltpu.roll(value, shift, 0) for value in sums_p]
                sums_p = [
                    value + jnp.where(subs >= shift, other, 0.0)
                    for value, other in zip(sums_p, moved)
                ]
            places = [carry_at + a - (lowest - 1) for a in rows_p]
            sums_p = [value + carry[place] for value, place in zip(sums_p, places)]
            ends = [jnp.broadcast_to(value[SUB - 1 : SUB, :], value.shape) for value in sums_p]
            for k, a in enumerate(rows_p):
                press[a] = sums_p[k]
                carry[places[k]] = ends[k]
        slope = wets_y[lowest - 1] * (press[lowest] - press[lowest - 1])
        for first_row in range(lowest, highest + 1, BATCH):
            rows_p = range(first_row, min(first_row + BATCH, highest + 1))
            here = [press[a] for a in rows_p]
            east = [east_of(x) for x in here]
            west = [west_of(x) for x in here]
            across = [
                wets_x[a] * (east[k] - here[k]) + wets_w[a] * (here[k] - west[k])
                for k, a in enumerate(rows_p)
            ]
            here.append(press[rows_p[-1] + 1])
            slopes = [slope] + [
                wets_y[a] * (here[k + 1] - here[k]) for k, a in enumerate(rows_p)
            ]
            slope = slopes[-1]
            for k, a in enumerate(rows_p):
                press_x[a] = across[k]
                press_y[a] = slopes[k + 1] + slopes[k]

    def tendency(get, lowest, highest, carry_at, emit, finish=None):
        pressure(get, lowest, highest, carry_at)
        for group in GROUPS:
            first_pass(get, lowest, highest, group)
        for group in GROUPS:
            second_pass(lowest, highest, group, emit)
            if finish is not None:
                finish(group)

    def turned(get, group, a):
        values = [get(f, a) for f in group]
        return values, [east_of(x) for x in values], [west_of(x) for x in values]

    def first_pass(get, lowest, highest, group):
        span = range(len(group))
        below = [get(f, lowest - 2) for f in group]
        here, east, west = turned(get, group, lowest - 1)
        face = wets_y[lowest - 2]
        up = [face * (x - y) for x, y in zip(here, below)]
        for a in range(lowest - 1, highest + 2):
            if a <= highest:
                after, east_after, west_after = turned(get, group, a + 1)
            else:
                after = [get(f, a + 1) for f in group]
            face, side_x, side_w = wets_y[a], wets_x[a], wets_w[a]
            up_before = up
            up = [face * (x - y) for x, y in zip(after, here)]
            right = [side_x * (x - y) for x, y in zip(east, here)]
            left = [side_w * (x - y) for x, y in zip(here, west)]
            lap = [(right[i] - left[i]) + (up[i] - up_before[i]) for i in span]
            if lowest <= a <= highest:
                flows = [here[group.index(f)] if f in group else get(f, a) for f in range(2)]
                u, v = (-0.5 * ADVECT) * flows[0], (-0.5 * ADVECT) * flows[1]
                mixed = [u * (right[i] + left[i]) + v * (up[i] + up_before[i]) for i in span]
                for i, f in enumerate(group):
                    if f < 2:
                        turn = rotate[pl.ds(a, 1), :] * wets[a]
                    if f == 0:
                        mixed[i] = mixed[i] + (turn * flows[1] - press_x[a])
                    if f == 1:
                        mixed[i] = mixed[i] - (turn * flows[0] + press_y[a])
                for i, f in enumerate(group):
                    mixes[f, a] = mixed[i]
            for i, f in enumerate(group):
                laps[f, a] = lap[i]
            if a <= highest:
                here, east, west = after, east_after, west_after

    def second_pass(lowest, highest, group, emit):
        span = range(len(group))

        def get(f, a):
            return laps[f, a]

        below = [get(f, lowest - 1) for f in group]
        here, east, west = turned(get, group, lowest)
        face = wets_y[lowest - 1]
        up = [face * (x - y) for x, y in zip(here, below)]
        for a in range(lowest, highest + 1):
            if a < highest:
                after, east_after, west_after = turned(get, group, a + 1)
            else:
                after = [get(f, a + 1) for f in group]
            face, side_x, side_w = wets_y[a], wets_x[a], wets_w[a]
            up_before = up
            up = [face * (x - y) for x, y in zip(after, here)]
            smooth = [
                (side_x * (east[i] - here[i]) - side_w * (here[i] - west[i]))
                + (up[i] - up_before[i])
                for i in span
            ]
            emit(a, group, [mixes[f, a] - KAPPA * smooth[i] for i, f in enumerate(group)])
            if a < highest:
                here, east, west = after, east_after, west_after

    def tile(t, _):
        for k in range(4):
            rim = rims_of(k, t)
            for q in range(RIM):
                for f in every:
                    cur[f, bases[k] + q, :, pl.ds(0, own)] = blocks[k][f * RIM + q, t]
                    cur[f, bases[k] + q, :, pl.ds(own, LANES)] = rim(f, q)
        level = subs + (first_level(chunk) + SUB * t)
        if first:
            level = jnp.where(level >= levels, FAR, level)
        level = level.astype(F32)
        top = jnp.where(level == 0.0, WIND, 0.0)
        for a in range(tall):
            for k, ref in enumerate((wets, wets_x, wets_w, wets_y)):
                ref[a] = jnp.where(level < deeps[k, a], 1.0, 0.0)

        def winded(a, group, values):
            if not first:
                return values
            return [
                value + (top * wets[a]) * winds[f, a] if f < 2 else value
                for f, value in zip(group, values)
            ]

        def emit_first(a, group, values):
            values = winded(a, group, values)
            values = [cur[f, a] + value for f, value in zip(group, values)]
            for f, value in zip(group, values):
                between[f, a] = value

        tendency(lambda f, a: cur[f, a], 2, tall - 3, 0, emit_first)

        def emit_second(a, group, values):
            values = winded(a, group, values)
            news = [0.5 * ((cur[f, a] + between[f, a]) + value) for f, value in zip(group, values)]
            r = a - RIM
            adds = [sums[f, r] + wets[a] * new for f, new in zip(group, news) if f < 2]
            for f, add in zip(group, adds):
                sums[f, r] = add
            for f, new in zip(group, news):
                for lane in range(2):
                    held[f, lane, pl.ds(t * (SUB * rows) + r, SUB, stride=rows), :] = new[
                        :, lane * LANES : (lane + 1) * LANES
                    ]

        def finish(group):
            def leave(count):
                for f in group:
                    for lane in range(2):
                        copy(f, lane, t, count).start()

            if final == SUB:
                leave(SUB)
            else:
                pl.when(t < tiles - 1)(lambda: leave(SUB))
                pl.when(t == tiles - 1)(lambda: leave(final))

        tendency(lambda f, a: between[f, a], RIM, tall - RIM - 1, tall - 2, emit_second, finish)
        return 0

    def copy(f, lane, t, count):
        size = count * rows
        at = (first_level(chunk) + SUB * t) * rows
        return pltpu.make_async_copy(
            held.at[f, lane, pl.ds(t * (SUB * rows), size)],
            outs[f].at[pl.ds(at, size), pl.ds(lane * LANES, LANES)],
            sems.at[t, f, lane],
        )

    final = levels - SUB * (tiles - 1)
    lax.fori_loop(0, tiles, tile, 0)
    if last:
        depth_levels = first_level(chunk) + levels
        for f in range(2):
            for ref, at in ((sums_a, (1 - odd_y) * RIM), (sums_b, odd_y * RIM)):
                for q in range(RIM):
                    line = jnp.sum(sums[f, at + q], axis=0, keepdims=True) / depth_levels
                    ref[f, pl.ds(q, 1), :] = line
    for t in range(tiles):
        for f in every:
            for lane in range(2):
                copy(f, lane, t, final if t == tiles - 1 else SUB).wait()


def step(chunk, rows, levels, columns, rotate, blocks, kept, news):
    first = chunk == 0
    last = chunk == len(CHUNKS) - 1
    tiles = CHUNKS[chunk]
    wide = columns + LANES
    tall = rows + 2 * RIM
    vmem = pl.BlockSpec(memory_space=pltpu.VMEM)
    hbm = pl.BlockSpec(memory_space=pl.ANY)
    operands = [rotate, *blocks]
    in_specs = [vmem] * 5
    if not first:
        operands += [*kept, *news]
        in_specs += [vmem] * 3 + [hbm] * FIELDS
    carry = (tall - 2 + rows + 2, SUB, wide)
    sums = (2, rows, SUB, wide)
    shapes = [jax.ShapeDtypeStruct((levels * rows, columns), F32)] * FIELDS
    out_specs = [hbm] * FIELDS
    row = pltpu.VMEM((tall, SUB, wide), F32)
    fields = pltpu.VMEM((FIELDS, tall, SUB, wide), F32)
    scratch = [fields] + [row] * 7 + [fields] * 3
    scratch += [pltpu.VMEM((FIELDS, 2, tiles * SUB * rows, LANES), F32)]
    if first:
        shapes += [jax.ShapeDtypeStruct((4, tall, SUB, wide), F32)]
        shapes += [jax.ShapeDtypeStruct((tall, wide), F32)] * 2
        scratch += [pltpu.VMEM((2, tall, SUB, wide), F32)]
    if last:
        shapes += [jax.ShapeDtypeStruct((2, RIM, wide), F32)] * 2
        scratch += [pltpu.VMEM(carry, F32), pltpu.VMEM(sums, F32)]
    else:
        shapes += [jax.ShapeDtypeStruct(carry, F32), jax.ShapeDtypeStruct(sums, F32)]
    out_specs += [vmem] * (len(shapes) - FIELDS)
    scratch += [pltpu.SemaphoreType.DMA((tiles, FIELDS, 2))]
    aliases = {} if first else {len(operands) - FIELDS + f: f for f in range(FIELDS)}
    return pl.pallas_call(
        functools.partial(step_kernel, chunk, rows),
        out_shape=shapes,
        in_specs=in_specs,
        out_specs=out_specs,
        scratch_shapes=scratch,
        input_output_aliases=aliases,
        compiler_params=pltpu.CompilerParams(vmem_limit_bytes=16 * 1024 * 1024),
        name="step",
    )(*operands)


def shift_rows(x, count):
    return pltpu.roll(x, count % x.shape[0], 0)


def weighed(weights, e):
    east, west = east_of(e), west_of(e)
    return (
        weights[0] * shift_rows(east, -1) + weights[1] * shift_rows(west, -1)
    ) + (weights[2] * shift_rows(east, 1) + weights[3] * shift_rows(west, 1))


def prepare_kernel(levels, deep_ref, surface_ref, out):
    deep = deep_ref[...]
    surface = surface_ref[...]
    ocean = jnp.where(deep > 0.0, 1.0, 0.0)
    pair = jnp.minimum(deep, east_of(deep))
    north_east = jnp.minimum(pair, shift_rows(pair, -1)) / levels
    north_west = west_of(north_east)
    corners = (north_east, north_west, shift_rows(north_east, 1), shift_rows(north_west, 1))
    share = 1.0 / (PHI + 0.5 * ((corners[0] + corners[1]) + (corners[2] + corners[3])))
    weights = [(0.5 * share) * corner for corner in corners]
    for k in range(4):
        out[k] = weights[k]
    out[4] = (PHI * ocean * share) * surface - (surface - weighed(weights, surface))
    across = ocean * east_of(ocean)
    along = ocean * shift_rows(ocean, -1)
    scale = (-0.5 * DIVERGE) * share
    out[5] = scale * across
    out[6] = scale * west_of(across)
    out[7] = scale * along
    out[8] = scale * shift_rows(along, 1)
    out[9] = surface


def solve_kernel(rows, ready, met_a, own_a, own_b, met_b, out):
    odd = jnp.broadcast_to(parities()[0], ready.shape[1:]) == 1
    flows = []
    for f in range(2):
        lines = [ref[f] for ref in (met_a, own_a, own_b, met_b)]
        flows.append(
            jnp.where(odd, jnp.concatenate(lines, axis=0), jnp.concatenate(lines[::-1], axis=0))
        )
    weights = [ready[k] for k in range(4)]
    east, north = flows
    scaled = ready[4] + (
        (ready[5] * (east_of(east) - east) + ready[6] * (east - west_of(east)))
        + (
            ready[7] * (shift_rows(north, -1) - north)
            + ready[8] * (north - shift_rows(north, 1))
        )
    )
    opening, updates = chebyshev_weights(ITERS)
    direction = opening * scaled
    total = ready[9]
    for index in range(ITERS):
        total = total + direction
        if index + 1 < ITERS:
            scaled = scaled - (direction - weighed(weights, direction))
            keep, push = updates[index]
            direction = keep * direction + push * scaled
    out[...] = total[RIM : RIM + rows, : out.shape[1]]


def body(
    eastward_flow,
    northward_flow,
    heat_anomaly,
    salt_anomaly,
    air_stress_forcing,
    earlier_sea_height_load,
    ocean_layer_depths,
):
    levels, rows, columns = eastward_flow.shape
    assert rows == 2 * RIM and columns == 2 * LANES and levels + EXTRA == SUB * sum(CHUNKS)
    along_y, along_x = lax.axis_size("by"), lax.axis_size("bx")
    pairs_y = (swaps(along_y, 0, False), swaps(along_y, 1, False))
    pairs_x = (swaps(along_x, 0, True), swaps(along_x, 1, True))
    row_index = lax.axis_index("by") * rows - RIM + jnp.arange(rows + 2 * RIM)
    rotate = 1.2 * jnp.sin(
        0.9 * math.pi * ((row_index.astype(F32) + 0.5) / (rows * along_y) - 0.5)
    )
    rotate = jnp.broadcast_to(rotate[:, None], (rows + 2 * RIM, columns + LANES))

    fields = (eastward_flow, northward_flow, heat_anomaly, salt_anomaly)
    lines = (air_stress_forcing, earlier_sea_height_load, ocean_layer_depths)
    halves, edge_a, edge_b = pack(fields, lines)
    across_a = lax.ppermute(edge_a, "bx", pairs_x[0])
    across_b = lax.ppermute(edge_b, "bx", pairs_x[1])
    halves = put_rims(halves, across_a, across_b)

    def send(own):
        met_b = lax.ppermute(own[1], "by", pairs_y[1])
        return lax.ppermute(own[0], "by", pairs_y[0]), met_b

    rims = [send(halves[chunk]) for chunk in range(AHEAD)]
    kept, news = None, None
    for chunk in range(len(CHUNKS)):
        own_a, own_b = halves[chunk]
        met_a, met_b = rims[chunk]
        blocks = (met_a, own_a, own_b, met_b)
        outs = step(chunk, rows, levels, columns, rotate, blocks, kept, news)
        news, rest = outs[:FIELDS], outs[FIELDS:]
        if chunk == 0:
            deeps, depth_wide, surface_wide = rest[:3]
            rest = rest[3:]
        later = chunk + AHEAD
        if later < len(CHUNKS):
            *halves[later], one, two = lax.optimization_barrier((*halves[later], *rest))
            rest = (one, two)
            rims.append(send(halves[later]))
        kept = (deeps, *rest)
    own_a, own_b = rest
    depth_wide, surface_wide, own_a, own_b = lax.optimization_barrier(
        (depth_wide, surface_wide, own_a, own_b)
    )
    met_a, met_b = send((own_a, own_b))
    vmem = pl.BlockSpec(memory_space=pltpu.VMEM)
    ready = pl.pallas_call(
        functools.partial(prepare_kernel, levels),
        out_shape=jax.ShapeDtypeStruct((10, *depth_wide.shape), F32),
        in_specs=[vmem] * 2,
        out_specs=vmem,
        compiler_params=pltpu.CompilerParams(vmem_limit_bytes=SMALL_VMEM),
        name="prepare",
    )(depth_wide, surface_wide)
    surface_new = pl.pallas_call(
        functools.partial(solve_kernel, rows),
        out_shape=jax.ShapeDtypeStruct((rows, columns), F32),
        in_specs=[vmem] * 5,
        out_specs=vmem,
        compiler_params=pltpu.CompilerParams(vmem_limit_bytes=SMALL_VMEM),
        name="solve",
    )(ready, met_a, own_a, own_b, met_b)
    shaped = [item.reshape(levels, rows, columns) for item in news]
    return (*shaped, surface_new)


def solution(mesh):
    return jax.shard_map(
        body,
        mesh=mesh,
        in_specs=(P(None, "by", "bx"),) * 5 + (P("by", "bx"),) * 2,
        out_specs=(P(None, "by", "bx"),) * 4 + (P("by", "bx"),),
        check_vma=False,
    )
```

```python
import functools
import math

import jax
import jax.numpy as jnp
from jax import lax
from jax.experimental import pallas as pl
from jax.experimental.pallas import tpu as pltpu
from jax.sharding import PartitionSpec as P

ITERS = 4
KAPPA = 0.004
ADVECT = 0.25
PRESS = 0.1
WIND = 0.5
PHI = 0.5
DIVERGE = 2.0
LOWER = 0.2
UPPER = 2.0

SUB = 8
LANES = 128
FIELDS = 4
RIM = 4
EDGE = 8
EXTRA = 2
CHUNKS = (2, 2, 2, 2)
AHEAD = 3
FAR = 1000000
BATCH = 4
GROUPS = ((0,), (1,), (2,), (3,))
SMALL_VMEM = 4 * 1024 * 1024
PACK_VMEM = 8 * 1024 * 1024
F32 = jnp.float32


def chebyshev_weights(count):
    middle = 0.5 * (UPPER + LOWER)
    half_span = 0.5 * (UPPER - LOWER)
    ratio_value = middle / half_span
    rho_now = 1.0 / ratio_value
    updates = []
    for index in range(count - 1):
        rho_next = 1.0 / (2.0 * ratio_value - rho_now)
        updates.append((rho_next * rho_now, 2.0 * rho_next / half_span))
        rho_now = rho_next
    return (1.0 / middle, updates)


def swaps(count, first, ring):
    pairs = []
    for i in range(first, count if ring else count - 1, 2):
        j = (i + 1) % count
        pairs += [(i, j), (j, i)]
    return pairs


def first_level(chunk):
    return SUB * sum(CHUNKS[:chunk]) - (EXTRA if chunk else 0)


def chunk_levels(chunk):
    return SUB * CHUNKS[chunk] - (0 if chunk else EXTRA)


def parities():
    return 1 - (lax.axis_index("by") & 1), lax.axis_index("bx") & 1


def first_rows():
    odd = parities()[0]
    return (1 - odd) * RIM, odd * RIM


def edges_kernel(rows, *refs):
    fields, sources = refs[:FIELDS], refs[FIELDS : FIELDS + 3]
    across_a, across_b, held, lines, mixed, depth, sems, sems_lines = refs[FIELDS + 3 :]
    small = [
        pltpu.make_async_copy(source, into, sems_lines.at[k])
        for k, (source, into) in enumerate(
            zip(sources, (lines.at[pl.ds(EXTRA, EXTRA)], lines.at[1], depth))
        )
    ]

    def copy(f, lane):
        return pltpu.make_async_copy(
            fields[f].at[:, pl.ds(lane * LANES, LANES)], held.at[f, lane], sems.at[f, lane]
        )

    for f in range(FIELDS):
        for lane in range(2):
            copy(f, lane).start()
    for item in small:
        item.start()
    for item in small:
        item.wait()
    lines[0] = depth[...].astype(F32)
    for f in range(FIELDS):
        for lane in range(2):
            copy(f, lane).wait()

    used = SUB - EXTRA
    for f in range(FIELDS):
        for group in range(2):
            for q in range(RIM):
                place_tile(mixed.at[f, group, q], held, lines, rows, group, f, q, 0, CHUNKS[0] - 1)

    lanes = lax.broadcasted_iota(jnp.int32, (SUB, LANES), 1)
    odd = jnp.broadcast_to(parities()[1], (SUB, LANES)) == 1
    slot = 0
    for c in range(len(CHUNKS)):
        for t in range(CHUNKS[c]):
            base = (first_level(c) + SUB * t) * rows
            for group in range(2):
                west = jnp.zeros((SUB, LANES), F32)
                east = jnp.zeros((SUB, LANES), F32)
                for q in range(RIM):
                    for f in range(FIELDS):
                        place = (q * FIELDS + f) * EDGE
                        other = (place - EDGE) % LANES
                        if c == 0 and t == CHUNKS[0] - 1:
                            low = mixed[f, group, q, :, pl.ds(0, LANES)]
                            high = mixed[f, group, q, :, pl.ds(LANES, LANES)]
                        else:
                            row = pl.ds(base + first_rows()[group] + q, SUB, stride=rows)
                            low = held[f, 0, row, :]
                            high = held[f, 1, row, :]
                        if place:
                            low = pltpu.roll(low, place, 1)
                            high = pltpu.roll(high, place, 1)
                        west = jnp.where((lanes >= place) & (lanes < place + EDGE), low, west)
                        east = jnp.where((lanes >= other) & (lanes < other + EDGE), high, east)
                across_a[group, slot] = jnp.where(odd, west, east)
                across_b[group, slot] = jnp.where(odd, east, west)
            slot += 1


def place_tile(ref, held, lines, rows, group, f, q, chunk, t):
    used = min(SUB, chunk_levels(chunk) - SUB * t)
    base = (first_level(chunk) + SUB * t) * rows
    row = first_rows()[group] + q
    for lane in range(2):
        ref[pl.ds(0, used), pl.ds(lane * LANES, LANES)] = held[
            f, lane, pl.ds(base + row, used, stride=rows), :
        ]
    for extra in range(SUB - used):
        if f < 2:
            line = lines[EXTRA * f + extra, pl.ds(row, 1), :]
        else:
            line = jnp.zeros((1, 2 * LANES), F32)
        ref[pl.ds(used + extra, 1), :] = line


def halves_kernel(rows, held, lines, *halves):
    for c in range(len(CHUNKS)):
        for t in range(CHUNKS[c]):
            for f in range(FIELDS):
                for group in range(2):
                    for q in range(RIM):
                        ref = halves[2 * c + group].at[f * RIM + q, t]
                        place_tile(ref, held, lines, rows, group, f, q, c, t)


def pack_edges(fields, wind, surface, depth):
    levels, rows, columns = fields[0].shape
    flat = [item.reshape(levels * rows, columns) for item in fields]
    arguments = [
        pltpu.with_memory_space_constraint(item, pltpu.HBM)
        for item in (*flat, wind, surface, depth)
    ]
    vmem = pl.BlockSpec(memory_space=pltpu.VMEM)
    return pl.pallas_call(
        functools.partial(edges_kernel, rows),
        out_shape=[jax.ShapeDtypeStruct((2, sum(CHUNKS), SUB, LANES), F32)] * 2
        + [
            jax.ShapeDtypeStruct((FIELDS, 2, levels * rows, LANES), F32),
            jax.ShapeDtypeStruct((2 * EXTRA, rows, columns), F32),
        ],
        in_specs=[pl.BlockSpec(memory_space=pltpu.HBM)] * len(arguments),
        out_specs=[vmem] * 4,
        scratch_shapes=[
            pltpu.VMEM((FIELDS, 2, RIM, SUB, columns), F32),
            pltpu.VMEM(depth.shape, depth.dtype),
            pltpu.SemaphoreType.DMA((FIELDS, 2)),
            pltpu.SemaphoreType.DMA((3,)),
        ],
        compiler_params=pltpu.CompilerParams(vmem_limit_bytes=PACK_VMEM),
        name="edges",
    )(*arguments)


def pack_halves(rows, held, lines):
    vmem = pl.BlockSpec(memory_space=pltpu.VMEM)
    shapes = [
        jax.ShapeDtypeStruct((FIELDS * RIM + 1, tiles, SUB, lines.shape[-1]), F32)
        for tiles in CHUNKS
        for _ in range(2)
    ]
    return pl.pallas_call(
        functools.partial(halves_kernel, rows),
        out_shape=shapes,
        in_specs=[vmem] * 2,
        out_specs=[vmem] * len(shapes),
        compiler_params=pltpu.CompilerParams(vmem_limit_bytes=PACK_VMEM),
        name="halves",
    )(held, lines)


def rims_kernel(across_a, across_b, *refs):
    count = 2 * len(CHUNKS)
    halves, sems = refs[count : 2 * count], refs[2 * count]
    copies = []
    for k, half in enumerate(halves):
        slots = pl.ds(sum(CHUNKS[: k // 2]), CHUNKS[k // 2])
        for lane, across in enumerate((across_a, across_b)):
            copies.append(
                pltpu.make_async_copy(
                    across.at[k % 2, slots],
                    half.at[FIELDS * RIM, :, :, pl.ds(lane * LANES, LANES)],
                    sems.at[k, lane],
                )
            )
    for copy in copies:
        copy.start()
    for copy in copies:
        copy.wait()


def put_rims(halves, across_a, across_b):
    count = len(halves)
    anywhere = pl.BlockSpec(memory_space=pl.ANY)
    outs = pl.pallas_call(
        rims_kernel,
        out_shape=[jax.ShapeDtypeStruct(item.shape, F32) for item in halves],
        in_specs=[anywhere] * (count + 2),
        out_specs=[anywhere] * count,
        scratch_shapes=[pltpu.SemaphoreType.DMA((count, 2))],
        input_output_aliases={2 + k: k for k in range(count)},
        compiler_params=pltpu.CompilerParams(vmem_limit_bytes=SMALL_VMEM),
        name="rims",
    )(across_a, across_b, *halves)
    return [list(outs[k : k + 2]) for k in range(0, count, 2)]


def east_of(value):
    return pltpu.roll(value, value.shape[-1] - 1, value.ndim - 1)


def west_of(value):
    return pltpu.roll(value, 1, value.ndim - 1)


def step_kernel(chunk, rows, *refs):
    first = chunk == 0
    last = chunk == len(CHUNKS) - 1
    tiles = CHUNKS[chunk]
    levels = chunk_levels(chunk)
    tall = rows + 2 * RIM
    refs = list(refs)

    def take(count):
        taken = refs[:count]
        del refs[:count]
        return taken

    (rotate,) = take(1)
    met_a, own_a, own_b, met_b = blocks = take(4)
    if not first:
        deeps_in, carry_in, sums_in = take(3)
        take(FIELDS)
    outs = take(FIELDS)
    if first:
        deeps, depth_out, surface_out = take(3)
    else:
        deeps = deeps_in
    if last:
        sums_a, sums_b = take(2)
    else:
        carry_out, sums_out = take(2)
    cur, wets, wets_x, wets_w, wets_y, press, press_x, press_y, laps, mixes, between, held = take(12)
    if first:
        (winds,) = take(1)
    if last:
        carry, sums = take(2)
    else:
        carry, sums = carry_out, sums_out
    (sems,) = take(1)

    if first:
        carry[...] = jnp.zeros(carry.shape, F32)
        sums[...] = jnp.zeros(sums.shape, F32)
    else:
        carry[...] = carry_in[...]
        sums[...] = sums_in[...]

    lanes = lax.broadcasted_iota(jnp.int32, (SUB, LANES), 1)
    own = own_a.shape[-1]
    wide = own + LANES
    every = range(FIELDS)
    odd_y, odd_x = parities()
    bases = [odd_y * (RIM * k) + (1 - odd_y) * (RIM * (3 - k)) for k in range(4)]
    swapped = ((lanes // EDGE) & 1) != 1 - odd_x

    def rims_of(k, t):
        both = blocks[k][FIELDS * RIM, t]
        one, two = both[:, :LANES], both[:, LANES:]
        mixed = (jnp.where(swapped, one, two), jnp.where(swapped, two, one))

        def rim(f, q):
            place = (q * FIELDS + f) * EDGE
            return pltpu.roll(mixed[f % 2], LANES - place, 1) if place else mixed[f % 2]

        return rim

    if first:
        for k in range(4):
            rim = rims_of(k, tiles - 1)
            for q in range(RIM):
                block = [
                    jnp.concatenate([blocks[k][f * RIM + q, tiles - 1], rim(f, q)], axis=1)
                    for f in range(2)
                ]
                for f, extra, ref in (
                    (0, 0, deeps.at[0]),
                    (0, 1, deeps.at[1]),
                    (1, 0, winds.at[0]),
                    (1, 1, winds.at[1]),
                ):
                    slot = SUB - EXTRA + extra
                    ref[bases[k] + q] = jnp.broadcast_to(block[f][slot : slot + 1, :], (SUB, wide))
        for a in range(tall):
            surface_out[pl.ds(a, 1), :] = deeps[1, a, pl.ds(0, 1), :]
            depth_out[pl.ds(a, 1), :] = deeps[0, a, pl.ds(0, 1), :]
        for a in range(tall):
            here = deeps[0, a]
            deeps[1, a] = jnp.minimum(here, east_of(here))
            deeps[2, a] = jnp.minimum(here, west_of(here))
            deeps[3, a] = jnp.minimum(here, deeps[0, min(a + 1, tall - 1)])

    subs = lax.broadcasted_iota(jnp.int32, (SUB, wide), 0)

    def pressure(get, lowest, highest, carry_at):
        for first_row in range(lowest - 1, highest + 2, BATCH):
            rows_p = range(first_row, min(first_row + BATCH, highest + 2))
            sums_p = [
                ((-0.4 * PRESS) * get(2, a) + (0.3 * PRESS) * get(3, a)) * wets[a] for a in rows_p
            ]
            for shift in (1, 2, 4):
                moved = [pltpu.roll(value, shift, 0) for value in sums_p]
                sums_p = [
                    value + jnp.where(subs >= shift, other, 0.0)
                    for value, other in zip(sums_p, moved)
                ]
            places = [carry_at + a - (lowest - 1) for a in rows_p]
            sums_p = [value + carry[place] for value, place in zip(sums_p, places)]
            ends = [jnp.broadcast_to(value[SUB - 1 : SUB, :], value.shape) for value in sums_p]
            for k, a in enumerate(rows_p):
                press[a] = sums_p[k]
                carry[places[k]] = ends[k]
        slope = wets_y[lowest - 1] * (press[lowest] - press[lowest - 1])
        for first_row in range(lowest, highest + 1, BATCH):
            rows_p = range(first_row, min(first_row + BATCH, highest + 1))
            here = [press[a] for a in rows_p]
            east = [east_of(x) for x in here]
            west = [west_of(x) for x in here]
            across = [
                wets_x[a] * (east[k] - here[k]) + wets_w[a] * (here[k] - west[k])
                for k, a in enumerate(rows_p)
            ]
            here.append(press[rows_p[-1] + 1])
            slopes = [slope] + [
                wets_y[a] * (here[k + 1] - here[k]) for k, a in enumerate(rows_p)
            ]
            slope = slopes[-1]
            for k, a in enumerate(rows_p):
                press_x[a] = across[k]
                press_y[a] = slopes[k + 1] + slopes[k]

    def tendency(get, lowest, highest, carry_at, emit, finish=None):
        pressure(get, lowest, highest, carry_at)
        widths = [own if finish is not None and group[0] > 1 else wide for group in GROUPS]
        for group, width in zip(GROUPS, widths):
            first_pass(get, lowest, highest, group, width)
        for group, width in zip(GROUPS, widths):
            second_pass(lowest, highest, group, emit, width)
            if finish is not None:
                finish(group)

    def turned(get, group, a):
        values = [get(f, a) for f in group]
        return values, [east_of(x) for x in values], [west_of(x) for x in values]

    def first_pass(get, lowest, highest, group, width):
        span = range(len(group))
        below = [get(f, lowest - 2) for f in group]
        here, east, west = turned(get, group, lowest - 1)
        face = wets_y[lowest - 2]
        up = [face * (x - y) for x, y in zip(here, below)]
        for a in range(lowest - 1, highest + 2):
            if a <= highest:
                after, east_after, west_after = turned(get, group, a + 1)
            else:
                after = [get(f, a + 1) for f in group]
            face, side_x, side_w = wets_y[a], wets_x[a], wets_w[a]
            up_before = up
            up = [face * (x - y) for x, y in zip(after, here)]
            right = [side_x * (x - y) for x, y in zip(east, here)]
            left = [side_w * (x - y) for x, y in zip(here, west)]
            lap = [(right[i] - left[i]) + (up[i] - up_before[i]) for i in span]
            if lowest <= a <= highest:
                flows = [here[group.index(f)] if f in group else get(f, a) for f in range(2)]
                u, v = (-0.5 * ADVECT) * flows[0], (-0.5 * ADVECT) * flows[1]
                mixed = [
                    u[:, :width] * (right[i] + left[i])[:, :width]
                    + v[:, :width] * (up[i] + up_before[i])[:, :width]
                    for i in span
                ]
                for i, f in enumerate(group):
                    if f < 2:
                        turn = rotate[pl.ds(a, 1), :] * wets[a]
                    if f == 0:
                        mixed[i] = mixed[i] + (turn * flows[1] - press_x[a])
                    if f == 1:
                        mixed[i] = mixed[i] - (turn * flows[0] + press_y[a])
                for i, f in enumerate(group):
                    mixes[f, a, :, pl.ds(0, width)] = mixed[i]
            for i, f in enumerate(group):
                laps[f, a] = lap[i]
            if a <= highest:
                here, east, west = after, east_after, west_after

    def second_pass(lowest, highest, group, emit, width):
        span = range(len(group))
        part = pl.ds(0, width)

        def get(f, a):
            return laps[f, a]

        below = [laps[f, lowest - 1, :, part] for f in group]
        here, east, west = turned(get, group, lowest)
        face = wets_y[lowest - 1, :, part]
        up = [face * (x[:, :width] - y) for x, y in zip(here, below)]
        for a in range(lowest, highest + 1):
            if a < highest:
                after, east_after, west_after = turned(get, group, a + 1)
            else:
                after = [get(f, a + 1) for f in group]
            face, side_x, side_w = (ref[a, :, part] for ref in (wets_y, wets_x, wets_w))
            near = [x[:, :width] for x in here]
            up_before = up
            up = [face * (x[:, :width] - y) for x, y in zip(after, near)]
            smooth = [
                (side_x * (east[i][:, :width] - near[i]) - side_w * (near[i] - west[i][:, :width]))
                + (up[i] - up_before[i])
                for i in span
            ]
            mixed = [mixes[f, a, :, part] for f in group]
            emit(a, group, [x - KAPPA * y for x, y in zip(mixed, smooth)])
            if a < highest:
                here, east, west = after, east_after, west_after

    def tile(t, _):
        for k in range(4):
            rim = rims_of(k, t)
            for q in range(RIM):
                for f in every:
                    cur[f, bases[k] + q, :, pl.ds(0, own)] = blocks[k][f * RIM + q, t]
                    cur[f, bases[k] + q, :, pl.ds(own, LANES)] = rim(f, q)
        level = subs + (first_level(chunk) + SUB * t)
        if first:
            level = jnp.where(level >= levels, FAR, level)
        level = level.astype(F32)
        top = jnp.where(level == 0.0, WIND, 0.0)
        for a in range(tall):
            for k, ref in enumerate((wets, wets_x, wets_w, wets_y)):
                ref[a] = jnp.where(level < deeps[k, a], 1.0, 0.0)

        def winded(a, group, values):
            if not first:
                return values
            return [
                value + (top * wets[a]) * winds[f, a] if f < 2 else value
                for f, value in zip(group, values)
            ]

        def emit_first(a, group, values):
            values = winded(a, group, values)
            values = [cur[f, a] + value for f, value in zip(group, values)]
            for f, value in zip(group, values):
                between[f, a] = value

        tendency(lambda f, a: cur[f, a], 2, tall - 3, 0, emit_first)

        def emit_second(a, group, values):
            values = winded(a, group, values)
            part = pl.ds(0, values[0].shape[-1])
            news = [
                0.5 * ((cur[f, a, :, part] + between[f, a, :, part]) + value)
                for f, value in zip(group, values)
            ]
            r = a - RIM
            adds = [sums[f, r] + wets[a] * new for f, new in zip(group, news) if f < 2]
            for f, add in zip(group, adds):
                sums[f, r] = add
            for f, new in zip(group, news):
                for lane in range(2):
                    held[f, lane, pl.ds(t * (SUB * rows) + r, SUB, stride=rows), :] = new[
                        :, lane * LANES : (lane + 1) * LANES
                    ]

        def finish(group):
            def leave(count):
                for f in group:
                    for lane in range(2):
                        copy(f, lane, t, count).start()

            if final == SUB:
                leave(SUB)
            else:
                pl.when(t < tiles - 1)(lambda: leave(SUB))
                pl.when(t == tiles - 1)(lambda: leave(final))

        tendency(lambda f, a: between[f, a], RIM, tall - RIM - 1, tall - 2, emit_second, finish)
        return 0

    def copy(f, lane, t, count):
        size = count * rows
        at = (first_level(chunk) + SUB * t) * rows
        return pltpu.make_async_copy(
            held.at[f, lane, pl.ds(t * (SUB * rows), size)],
            outs[f].at[pl.ds(at, size), pl.ds(lane * LANES, LANES)],
            sems.at[t, f, lane],
        )

    final = levels - SUB * (tiles - 1)
    lax.fori_loop(0, tiles, tile, 0)
    if last:
        depth_levels = first_level(chunk) + levels
        for f in range(2):
            for ref, at in ((sums_a, (1 - odd_y) * RIM), (sums_b, odd_y * RIM)):
                for q in range(RIM):
                    line = jnp.sum(sums[f, at + q], axis=0, keepdims=True) / depth_levels
                    ref[f, pl.ds(q, 1), :] = line
    for t in range(tiles):
        for f in every:
            for lane in range(2):
                copy(f, lane, t, final if t == tiles - 1 else SUB).wait()


def step(chunk, rows, levels, columns, rotate, blocks, kept, news):
    first = chunk == 0
    last = chunk == len(CHUNKS) - 1
    tiles = CHUNKS[chunk]
    wide = columns + LANES
    tall = rows + 2 * RIM
    vmem = pl.BlockSpec(memory_space=pltpu.VMEM)
    hbm = pl.BlockSpec(memory_space=pl.ANY)
    operands = [rotate, *blocks]
    in_specs = [vmem] * 5
    if not first:
        operands += [*kept, *news]
        in_specs += [vmem] * 3 + [hbm] * FIELDS
    carry = (tall - 2 + rows + 2, SUB, wide)
    sums = (2, rows, SUB, wide)
    shapes = [jax.ShapeDtypeStruct((levels * rows, columns), F32)] * FIELDS
    out_specs = [hbm] * FIELDS
    row = pltpu.VMEM((tall, SUB, wide), F32)
    fields = pltpu.VMEM((FIELDS, tall, SUB, wide), F32)
    scratch = [fields] + [row] * 7 + [fields] * 3
    scratch += [pltpu.VMEM((FIELDS, 2, tiles * SUB * rows, LANES), F32)]
    if first:
        shapes += [jax.ShapeDtypeStruct((4, tall, SUB, wide), F32)]
        shapes += [jax.ShapeDtypeStruct((tall, wide), F32)] * 2
        scratch += [pltpu.VMEM((2, tall, SUB, wide), F32)]
    if last:
        shapes += [jax.ShapeDtypeStruct((2, RIM, wide), F32)] * 2
        scratch += [pltpu.VMEM(carry, F32), pltpu.VMEM(sums, F32)]
    else:
        shapes += [jax.ShapeDtypeStruct(carry, F32), jax.ShapeDtypeStruct(sums, F32)]
    out_specs += [vmem] * (len(shapes) - FIELDS)
    scratch += [pltpu.SemaphoreType.DMA((tiles, FIELDS, 2))]
    aliases = {} if first else {len(operands) - FIELDS + f: f for f in range(FIELDS)}
    return pl.pallas_call(
        functools.partial(step_kernel, chunk, rows),
        out_shape=shapes,
        in_specs=in_specs,
        out_specs=out_specs,
        scratch_shapes=scratch,
        input_output_aliases=aliases,
        compiler_params=pltpu.CompilerParams(vmem_limit_bytes=16 * 1024 * 1024),
        name="step",
    )(*operands)


def shift_rows(x, count):
    return pltpu.roll(x, count % x.shape[0], 0)


def weighed(weights, e):
    east, west = east_of(e), west_of(e)
    return (
        weights[0] * shift_rows(east, -1) + weights[1] * shift_rows(west, -1)
    ) + (weights[2] * shift_rows(east, 1) + weights[3] * shift_rows(west, 1))


def prepare_kernel(levels, deep_ref, surface_ref, out):
    deep = deep_ref[...]
    surface = surface_ref[...]
    ocean = jnp.where(deep > 0.0, 1.0, 0.0)
    pair = jnp.minimum(deep, east_of(deep))
    north_east = jnp.minimum(pair, shift_rows(pair, -1)) / levels
    north_west = west_of(north_east)
    corners = (north_east, north_west, shift_rows(north_east, 1), shift_rows(north_west, 1))
    share = 1.0 / (PHI + 0.5 * ((corners[0] + corners[1]) + (corners[2] + corners[3])))
    weights = [(0.5 * share) * corner for corner in corners]
    for k in range(4):
        out[k] = weights[k]
    out[4] = (PHI * ocean * share) * surface - (surface - weighed(weights, surface))
    across = ocean * east_of(ocean)
    along = ocean * shift_rows(ocean, -1)
    scale = (-0.5 * DIVERGE) * share
    out[5] = scale * across
    out[6] = scale * west_of(across)
    out[7] = scale * along
    out[8] = scale * shift_rows(along, 1)
    out[9] = surface


def solve_kernel(rows, ready, met_a, own_a, own_b, met_b, out):
    odd = jnp.broadcast_to(parities()[0], ready.shape[1:]) == 1
    flows = []
    for f in range(2):
        lines = [ref[f] for ref in (met_a, own_a, own_b, met_b)]
        flows.append(
            jnp.where(odd, jnp.concatenate(lines, axis=0), jnp.concatenate(lines[::-1], axis=0))
        )
    weights = [ready[k] for k in range(4)]
    east, north = flows
    scaled = ready[4] + (
        (ready[5] * (east_of(east) - east) + ready[6] * (east - west_of(east)))
        + (
            ready[7] * (shift_rows(north, -1) - north)
            + ready[8] * (north - shift_rows(north, 1))
        )
    )
    opening, updates = chebyshev_weights(ITERS)
    direction = opening * scaled
    total = ready[9]
    for index in range(ITERS):
        total = total + direction
        if index + 1 < ITERS:
            scaled = scaled - (direction - weighed(weights, direction))
            keep, push = updates[index]
            direction = keep * direction + push * scaled
    out[...] = total[RIM : RIM + rows, : out.shape[1]]


def body(
    eastward_flow,
    northward_flow,
    heat_anomaly,
    salt_anomaly,
    air_stress_forcing,
    earlier_sea_height_load,
    ocean_layer_depths,
):
    levels, rows, columns = eastward_flow.shape
    assert rows == 2 * RIM and columns == 2 * LANES and levels + EXTRA == SUB * sum(CHUNKS)
    along_y, along_x = lax.axis_size("by"), lax.axis_size("bx")
    pairs_y = (swaps(along_y, 1, False), swaps(along_y, 0, False))
    pairs_x = (swaps(along_x, 0, True), swaps(along_x, 1, True))
    row_index = lax.axis_index("by") * rows - RIM + jnp.arange(rows + 2 * RIM)
    rotate = 1.2 * jnp.sin(
        0.9 * math.pi * ((row_index.astype(F32) + 0.5) / (rows * along_y) - 0.5)
    )
    rotate = jnp.broadcast_to(rotate[:, None], (rows + 2 * RIM, columns + LANES))

    fields = (eastward_flow, northward_flow, heat_anomaly, salt_anomaly)
    edge_a, edge_b, held, lines = pack_edges(
        fields, air_stress_forcing, earlier_sea_height_load, ocean_layer_depths
    )
    halves = pack_halves(rows, held, lines)
    across_a = lax.ppermute(edge_a, "bx", pairs_x[0])
    across_b = lax.ppermute(edge_b, "bx", pairs_x[1])
    halves = put_rims(halves, across_a, across_b)

    def send(own):
        return [lax.ppermute(item, "by", pairs) for item, pairs in zip(own, pairs_y)]

    rims = [send(halves[chunk]) for chunk in range(AHEAD)]
    kept, news = None, None
    for chunk in range(len(CHUNKS)):
        own_a, own_b = halves[chunk]
        met_a, met_b = rims[chunk]
        blocks = (met_a, own_a, own_b, met_b)
        outs = step(chunk, rows, levels, columns, rotate, blocks, kept, news)
        news, rest = outs[:FIELDS], outs[FIELDS:]
        if chunk == 0:
            deeps, depth_wide, surface_wide = rest[:3]
            rest = rest[3:]
        later = chunk + AHEAD
        if later < len(CHUNKS):
            *halves[later], one, two = lax.optimization_barrier((*halves[later], *rest))
            rest = (one, two)
            rims.append(send(halves[later]))
        kept = (deeps, *rest)
    own_a, own_b = rest
    depth_wide, surface_wide, own_a, own_b = lax.optimization_barrier(
        (depth_wide, surface_wide, own_a, own_b)
    )
    met_a, met_b = send((own_a, own_b))
    vmem = pl.BlockSpec(memory_space=pltpu.VMEM)
    ready = pl.pallas_call(
        functools.partial(prepare_kernel, levels),
        out_shape=jax.ShapeDtypeStruct((10, *depth_wide.shape), F32),
        in_specs=[vmem] * 2,
        out_specs=vmem,
        compiler_params=pltpu.CompilerParams(vmem_limit_bytes=SMALL_VMEM),
        name="prepare",
    )(depth_wide, surface_wide)
    surface_new = pl.pallas_call(
        functools.partial(solve_kernel, rows),
        out_shape=jax.ShapeDtypeStruct((rows, columns), F32),
        in_specs=[vmem] * 5,
        out_specs=vmem,
        compiler_params=pltpu.CompilerParams(vmem_limit_bytes=SMALL_VMEM),
        name="solve",
    )(ready, met_a, own_a, own_b, met_b)
    shaped = [item.reshape(levels, rows, columns) for item in news]
    return (*shaped, surface_new)


def solution(mesh):
    return jax.shard_map(
        body,
        mesh=mesh,
        in_specs=(P(None, "by", "bx"),) * 5 + (P("by", "bx"),) * 2,
        out_specs=(P(None, "by", "bx"),) * 4 + (P("by", "bx"),),
        check_vma=False,
    )
```

```python
import functools
import math

import jax
import jax.numpy as jnp
from jax import lax
from jax.experimental import pallas as pl
from jax.experimental.pallas import tpu as pltpu
from jax.sharding import PartitionSpec as P

ITERS = 4
KAPPA = 0.004
ADVECT = 0.25
PRESS = 0.1
WIND = 0.5
PHI = 0.5
DIVERGE = 2.0
LOWER = 0.2
UPPER = 2.0

SUB = 8
LANES = 128
FIELDS = 4
RIM = 4
EDGE = 8
EXTRA = 2
CHUNKS = (3, 3, 2)
AHEAD = 3
FAR = 1000000
BATCH = 4
GROUPS = ((0,), (1,), (2,), (3,))
SMALL_VMEM = 4 * 1024 * 1024
PACK_VMEM = 8 * 1024 * 1024
F32 = jnp.float32


def chebyshev_weights(count):
    middle = 0.5 * (UPPER + LOWER)
    half_span = 0.5 * (UPPER - LOWER)
    ratio_value = middle / half_span
    rho_now = 1.0 / ratio_value
    updates = []
    for index in range(count - 1):
        rho_next = 1.0 / (2.0 * ratio_value - rho_now)
        updates.append((rho_next * rho_now, 2.0 * rho_next / half_span))
        rho_now = rho_next
    return (1.0 / middle, updates)


def swaps(count, first, ring):
    pairs = []
    for i in range(first, count if ring else count - 1, 2):
        j = (i + 1) % count
        pairs += [(i, j), (j, i)]
    return pairs


def first_level(chunk):
    return SUB * sum(CHUNKS[:chunk]) - (EXTRA if chunk else 0)


def chunk_levels(chunk):
    return SUB * CHUNKS[chunk] - (0 if chunk else EXTRA)


def parities():
    return 1 - (lax.axis_index("by") & 1), lax.axis_index("bx") & 1


def first_rows():
    odd = parities()[0]
    return (1 - odd) * RIM, odd * RIM


def edges_kernel(rows, *refs):
    fields, sources = refs[:FIELDS], refs[FIELDS : FIELDS + 3]
    across_a, across_b, held, lines, mixed, depth, sems, sems_lines = refs[FIELDS + 3 :]
    small = [
        pltpu.make_async_copy(source, into, sems_lines.at[k])
        for k, (source, into) in enumerate(
            zip(sources, (lines.at[pl.ds(EXTRA, EXTRA)], lines.at[1], depth))
        )
    ]

    def copy(f, lane):
        return pltpu.make_async_copy(
            fields[f].at[:, pl.ds(lane * LANES, LANES)], held.at[f, lane], sems.at[f, lane]
        )

    for f in range(FIELDS):
        for lane in range(2):
            copy(f, lane).start()
    for item in small:
        item.start()
    for item in small:
        item.wait()
    lines[0] = depth[...].astype(F32)
    for f in range(FIELDS):
        for lane in range(2):
            copy(f, lane).wait()

    used = SUB - EXTRA
    for f in range(FIELDS):
        for group in range(2):
            for q in range(RIM):
                place_tile(mixed.at[f, group, q], held, lines, rows, group, f, q, 0, CHUNKS[0] - 1)

    lanes = lax.broadcasted_iota(jnp.int32, (SUB, LANES), 1)
    odd = jnp.broadcast_to(parities()[1], (SUB, LANES)) == 1
    slot = 0
    for c in range(len(CHUNKS)):
        for t in range(CHUNKS[c]):
            base = (first_level(c) + SUB * t) * rows
            for group in range(2):
                west = jnp.zeros((SUB, LANES), F32)
                east = jnp.zeros((SUB, LANES), F32)
                for q in range(RIM):
                    for f in range(FIELDS):
                        place = (q * FIELDS + f) * EDGE
                        other = (place - EDGE) % LANES
                        if c == 0 and t == CHUNKS[0] - 1:
                            low = mixed[f, group, q, :, pl.ds(0, LANES)]
                            high = mixed[f, group, q, :, pl.ds(LANES, LANES)]
                        else:
                            row = pl.ds(base + first_rows()[group] + q, SUB, stride=rows)
                            low = held[f, 0, row, :]
                            high = held[f, 1, row, :]
                        if place:
                            low = pltpu.roll(low, place, 1)
                            high = pltpu.roll(high, place, 1)
                        west = jnp.where((lanes >= place) & (lanes < place + EDGE), low, west)
                        east = jnp.where((lanes >= other) & (lanes < other + EDGE), high, east)
                across_a[group, slot] = jnp.where(odd, west, east)
                across_b[group, slot] = jnp.where(odd, east, west)
            slot += 1


def place_tile(ref, held, lines, rows, group, f, q, chunk, t):
    used = min(SUB, chunk_levels(chunk) - SUB * t)
    base = (first_level(chunk) + SUB * t) * rows
    row = first_rows()[group] + q
    for lane in range(2):
        ref[pl.ds(0, used), pl.ds(lane * LANES, LANES)] = held[
            f, lane, pl.ds(base + row, used, stride=rows), :
        ]
    for extra in range(SUB - used):
        if f < 2:
            line = lines[EXTRA * f + extra, pl.ds(row, 1), :]
        else:
            line = jnp.zeros((1, 2 * LANES), F32)
        ref[pl.ds(used + extra, 1), :] = line


def halves_kernel(rows, held, lines, *halves):
    for c in range(len(CHUNKS)):
        for t in range(CHUNKS[c]):
            for f in range(FIELDS):
                for group in range(2):
                    for q in range(RIM):
                        ref = halves[2 * c + group].at[f * RIM + q, t]
                        place_tile(ref, held, lines, rows, group, f, q, c, t)


def pack_edges(fields, wind, surface, depth):
    levels, rows, columns = fields[0].shape
    flat = [item.reshape(levels * rows, columns) for item in fields]
    arguments = [
        pltpu.with_memory_space_constraint(item, pltpu.HBM)
        for item in (*flat, wind, surface, depth)
    ]
    vmem = pl.BlockSpec(memory_space=pltpu.VMEM)
    return pl.pallas_call(
        functools.partial(edges_kernel, rows),
        out_shape=[jax.ShapeDtypeStruct((2, sum(CHUNKS), SUB, LANES), F32)] * 2
        + [
            jax.ShapeDtypeStruct((FIELDS, 2, levels * rows, LANES), F32),
            jax.ShapeDtypeStruct((2 * EXTRA, rows, columns), F32),
        ],
        in_specs=[pl.BlockSpec(memory_space=pltpu.HBM)] * len(arguments),
        out_specs=[vmem] * 4,
        scratch_shapes=[
            pltpu.VMEM((FIELDS, 2, RIM, SUB, columns), F32),
            pltpu.VMEM(depth.shape, depth.dtype),
            pltpu.SemaphoreType.DMA((FIELDS, 2)),
            pltpu.SemaphoreType.DMA((3,)),
        ],
        compiler_params=pltpu.CompilerParams(vmem_limit_bytes=PACK_VMEM),
        name="edges",
    )(*arguments)


def pack_halves(rows, held, lines):
    vmem = pl.BlockSpec(memory_space=pltpu.VMEM)
    shapes = [
        jax.ShapeDtypeStruct((FIELDS * RIM + 1, tiles, SUB, lines.shape[-1]), F32)
        for tiles in CHUNKS
        for _ in range(2)
    ]
    return pl.pallas_call(
        functools.partial(halves_kernel, rows),
        out_shape=shapes,
        in_specs=[vmem] * 2,
        out_specs=[vmem] * len(shapes),
        compiler_params=pltpu.CompilerParams(vmem_limit_bytes=PACK_VMEM),
        name="halves",
    )(held, lines)


def rims_kernel(across_a, across_b, *refs):
    count = 2 * len(CHUNKS)
    halves, sems = refs[count : 2 * count], refs[2 * count]
    copies = []
    for k, half in enumerate(halves):
        slots = pl.ds(sum(CHUNKS[: k // 2]), CHUNKS[k // 2])
        for lane, across in enumerate((across_a, across_b)):
            copies.append(
                pltpu.make_async_copy(
                    across.at[k % 2, slots],
                    half.at[FIELDS * RIM, :, :, pl.ds(lane * LANES, LANES)],
                    sems.at[k, lane],
                )
            )
    for copy in copies:
        copy.start()
    for copy in copies:
        copy.wait()


def put_rims(halves, across_a, across_b):
    count = len(halves)
    anywhere = pl.BlockSpec(memory_space=pl.ANY)
    outs = pl.pallas_call(
        rims_kernel,
        out_shape=[jax.ShapeDtypeStruct(item.shape, F32) for item in halves],
        in_specs=[anywhere] * (count + 2),
        out_specs=[anywhere] * count,
        scratch_shapes=[pltpu.SemaphoreType.DMA((count, 2))],
        input_output_aliases={2 + k: k for k in range(count)},
        compiler_params=pltpu.CompilerParams(vmem_limit_bytes=SMALL_VMEM),
        name="rims",
    )(across_a, across_b, *halves)
    return [list(outs[k : k + 2]) for k in range(0, count, 2)]


def east_of(value):
    return pltpu.roll(value, value.shape[-1] - 1, value.ndim - 1)


def west_of(value):
    return pltpu.roll(value, 1, value.ndim - 1)


def step_kernel(chunk, rows, *refs):
    first = chunk == 0
    last = chunk == len(CHUNKS) - 1
    tiles = CHUNKS[chunk]
    levels = chunk_levels(chunk)
    tall = rows + 2 * RIM
    refs = list(refs)

    def take(count):
        taken = refs[:count]
        del refs[:count]
        return taken

    (rotate,) = take(1)
    met_a, own_a, own_b, met_b = blocks = take(4)
    if not first:
        deeps_in, carry_in, sums_in = take(3)
        take(FIELDS)
    outs = take(FIELDS)
    if first:
        deeps, depth_out, surface_out = take(3)
    else:
        deeps = deeps_in
    if last:
        sums_a, sums_b = take(2)
    else:
        carry_out, sums_out = take(2)
    cur, wets, wets_x, wets_w, wets_y, press, press_x, press_y, laps, mixes, between, held = take(12)
    if first:
        (winds,) = take(1)
    if last:
        carry, sums = take(2)
    else:
        carry, sums = carry_out, sums_out
    (sems,) = take(1)

    if first:
        carry[...] = jnp.zeros(carry.shape, F32)
        sums[...] = jnp.zeros(sums.shape, F32)
    else:
        carry[...] = carry_in[...]
        sums[...] = sums_in[...]

    lanes = lax.broadcasted_iota(jnp.int32, (SUB, LANES), 1)
    own = own_a.shape[-1]
    wide = own + LANES
    every = range(FIELDS)
    odd_y, odd_x = parities()
    bases = [odd_y * (RIM * k) + (1 - odd_y) * (RIM * (3 - k)) for k in range(4)]
    swapped = ((lanes // EDGE) & 1) != 1 - odd_x

    def rims_of(k, t):
        both = blocks[k][FIELDS * RIM, t]
        one, two = both[:, :LANES], both[:, LANES:]
        mixed = (jnp.where(swapped, one, two), jnp.where(swapped, two, one))

        def rim(f, q):
            place = (q * FIELDS + f) * EDGE
            return pltpu.roll(mixed[f % 2], LANES - place, 1) if place else mixed[f % 2]

        return rim

    if first:
        for k in range(4):
            rim = rims_of(k, tiles - 1)
            for q in range(RIM):
                block = [
                    jnp.concatenate([blocks[k][f * RIM + q, tiles - 1], rim(f, q)], axis=1)
                    for f in range(2)
                ]
                for f, extra, ref in (
                    (0, 0, deeps.at[0]),
                    (0, 1, deeps.at[1]),
                    (1, 0, winds.at[0]),
                    (1, 1, winds.at[1]),
                ):
                    slot = SUB - EXTRA + extra
                    ref[bases[k] + q] = jnp.broadcast_to(block[f][slot : slot + 1, :], (SUB, wide))
        for a in range(tall):
            surface_out[pl.ds(a, 1), :] = deeps[1, a, pl.ds(0, 1), :]
            depth_out[pl.ds(a, 1), :] = deeps[0, a, pl.ds(0, 1), :]
        for a in range(tall):
            here = deeps[0, a]
            deeps[1, a] = jnp.minimum(here, east_of(here))
            deeps[2, a] = jnp.minimum(here, west_of(here))
            deeps[3, a] = jnp.minimum(here, deeps[0, min(a + 1, tall - 1)])

    subs = lax.broadcasted_iota(jnp.int32, (SUB, wide), 0)

    def pressure(get, lowest, highest, carry_at):
        for first_row in range(lowest - 1, highest + 2, BATCH):
            rows_p = range(first_row, min(first_row + BATCH, highest + 2))
            sums_p = [
                ((-0.4 * PRESS) * get(2, a) + (0.3 * PRESS) * get(3, a)) * wets[a] for a in rows_p
            ]
            for shift in (1, 2, 4):
                moved = [pltpu.roll(value, shift, 0) for value in sums_p]
                sums_p = [
                    value + jnp.where(subs >= shift, other, 0.0)
                    for value, other in zip(sums_p, moved)
                ]
            places = [carry_at + a - (lowest - 1) for a in rows_p]
            sums_p = [value + carry[place] for value, place in zip(sums_p, places)]
            ends = [jnp.broadcast_to(value[SUB - 1 : SUB, :], value.shape) for value in sums_p]
            for k, a in enumerate(rows_p):
                press[a] = sums_p[k]
                carry[places[k]] = ends[k]
        slope = wets_y[lowest - 1] * (press[lowest] - press[lowest - 1])
        for first_row in range(lowest, highest + 1, BATCH):
            rows_p = range(first_row, min(first_row + BATCH, highest + 1))
            here = [press[a] for a in rows_p]
            east = [east_of(x) for x in here]
            west = [west_of(x) for x in here]
            across = [
                wets_x[a] * (east[k] - here[k]) + wets_w[a] * (here[k] - west[k])
                for k, a in enumerate(rows_p)
            ]
            here.append(press[rows_p[-1] + 1])
            slopes = [slope] + [
                wets_y[a] * (here[k + 1] - here[k]) for k, a in enumerate(rows_p)
            ]
            slope = slopes[-1]
            for k, a in enumerate(rows_p):
                press_x[a] = across[k]
                press_y[a] = slopes[k + 1] + slopes[k]

    def tendency(get, lowest, highest, carry_at, emit, finish=None):
        pressure(get, lowest, highest, carry_at)
        widths = [own if finish is not None and group[0] > 1 else wide for group in GROUPS]
        for group, width in zip(GROUPS, widths):
            first_pass(get, lowest, highest, group, width)
        for group, width in zip(GROUPS, widths):
            second_pass(lowest, highest, group, emit, width)
            if finish is not None:
                finish(group)

    def turned(get, group, a):
        values = [get(f, a) for f in group]
        return values, [east_of(x) for x in values], [west_of(x) for x in values]

    def first_pass(get, lowest, highest, group, width):
        span = range(len(group))
        below = [get(f, lowest - 2) for f in group]
        here, east, west = turned(get, group, lowest - 1)
        face = wets_y[lowest - 2]
        up = [face * (x - y) for x, y in zip(here, below)]
        for a in range(lowest - 1, highest + 2):
            if a <= highest:
                after, east_after, west_after = turned(get, group, a + 1)
            else:
                after = [get(f, a + 1) for f in group]
            face, side_x, side_w = wets_y[a], wets_x[a], wets_w[a]
            up_before = up
            up = [face * (x - y) for x, y in zip(after, here)]
            right = [side_x * (x - y) for x, y in zip(east, here)]
            left = [side_w * (x - y) for x, y in zip(here, west)]
            lap = [(right[i] - left[i]) + (up[i] - up_before[i]) for i in span]
            if lowest <= a <= highest:
                flows = [here[group.index(f)] if f in group else get(f, a) for f in range(2)]
                u, v = (-0.5 * ADVECT) * flows[0], (-0.5 * ADVECT) * flows[1]
                mixed = [
                    u[:, :width] * (right[i] + left[i])[:, :width]
                    + v[:, :width] * (up[i] + up_before[i])[:, :width]
                    for i in span
                ]
                for i, f in enumerate(group):
                    if f < 2:
                        turn = rotate[pl.ds(a, 1), :] * wets[a]
                    if f == 0:
                        mixed[i] = mixed[i] + (turn * flows[1] - press_x[a])
                    if f == 1:
                        mixed[i] = mixed[i] - (turn * flows[0] + press_y[a])
                for i, f in enumerate(group):
                    mixes[f, a, :, pl.ds(0, width)] = mixed[i]
            for i, f in enumerate(group):
                laps[f, a] = lap[i]
            if a <= highest:
                here, east, west = after, east_after, west_after

    def second_pass(lowest, highest, group, emit, width):
        span = range(len(group))
        part = pl.ds(0, width)

        def get(f, a):
            return laps[f, a]

        below = [laps[f, lowest - 1, :, part] for f in group]
        here, east, west = turned(get, group, lowest)
        face = wets_y[lowest - 1, :, part]
        up = [face * (x[:, :width] - y) for x, y in zip(here, below)]
        for a in range(lowest, highest + 1):
            if a < highest:
                after, east_after, west_after = turned(get, group, a + 1)
            else:
                after = [get(f, a + 1) for f in group]
            face, side_x, side_w = (ref[a, :, part] for ref in (wets_y, wets_x, wets_w))
            near = [x[:, :width] for x in here]
            up_before = up
            up = [face * (x[:, :width] - y) for x, y in zip(after, near)]
            smooth = [
                (side_x * (east[i][:, :width] - near[i]) - side_w * (near[i] - west[i][:, :width]))
                + (up[i] - up_before[i])
                for i in span
            ]
            mixed = [mixes[f, a, :, part] for f in group]
            emit(a, group, [x - KAPPA * y for x, y in zip(mixed, smooth)])
            if a < highest:
                here, east, west = after, east_after, west_after

    def tile(t, _):
        for k in range(4):
            rim = rims_of(k, t)
            for q in range(RIM):
                for f in every:
                    cur[f, bases[k] + q, :, pl.ds(0, own)] = blocks[k][f * RIM + q, t]
                    cur[f, bases[k] + q, :, pl.ds(own, LANES)] = rim(f, q)
        level = subs + (first_level(chunk) + SUB * t)
        if first:
            level = jnp.where(level >= levels, FAR, level)
        level = level.astype(F32)
        top = jnp.where(level == 0.0, WIND, 0.0)
        for a in range(tall):
            for k, ref in enumerate((wets, wets_x, wets_w, wets_y)):
                ref[a] = jnp.where(level < deeps[k, a], 1.0, 0.0)

        def winded(a, group, values):
            if not first:
                return values
            return [
                value + (top * wets[a]) * winds[f, a] if f < 2 else value
                for f, value in zip(group, values)
            ]

        def emit_first(a, group, values):
            values = winded(a, group, values)
            values = [cur[f, a] + value for f, value in zip(group, values)]
            for f, value in zip(group, values):
                between[f, a] = value

        tendency(lambda f, a: cur[f, a], 2, tall - 3, 0, emit_first)

        def emit_second(a, group, values):
            values = winded(a, group, values)
            part = pl.ds(0, values[0].shape[-1])
            news = [
                0.5 * ((cur[f, a, :, part] + between[f, a, :, part]) + value)
                for f, value in zip(group, values)
            ]
            r = a - RIM
            adds = [sums[f, r] + wets[a] * new for f, new in zip(group, news) if f < 2]
            for f, add in zip(group, adds):
                sums[f, r] = add
            for f, new in zip(group, news):
                for lane in range(2):
                    held[f, lane, pl.ds(t * (SUB * rows) + r, SUB, stride=rows), :] = new[
                        :, lane * LANES : (lane + 1) * LANES
                    ]

        def finish(group):
            def leave(count):
                for f in group:
                    for lane in range(2):
                        copy(f, lane, t, count).start()

            if final == SUB:
                leave(SUB)
            else:
                pl.when(t < tiles - 1)(lambda: leave(SUB))
                pl.when(t == tiles - 1)(lambda: leave(final))

        tendency(lambda f, a: between[f, a], RIM, tall - RIM - 1, tall - 2, emit_second, finish)
        return 0

    def copy(f, lane, t, count):
        size = count * rows
        at = (first_level(chunk) + SUB * t) * rows
        return pltpu.make_async_copy(
            held.at[f, lane, pl.ds(t * (SUB * rows), size)],
            outs[f].at[pl.ds(at, size), pl.ds(lane * LANES, LANES)],
            sems.at[t, f, lane],
        )

    final = levels - SUB * (tiles - 1)
    lax.fori_loop(0, tiles, tile, 0)
    if last:
        depth_levels = first_level(chunk) + levels
        for f in range(2):
            for ref, at in ((sums_a, (1 - odd_y) * RIM), (sums_b, odd_y * RIM)):
                for q in range(RIM):
                    line = jnp.sum(sums[f, at + q], axis=0, keepdims=True) / depth_levels
                    ref[f, pl.ds(q, 1), :] = line
    for t in range(tiles):
        for f in every:
            for lane in range(2):
                copy(f, lane, t, final if t == tiles - 1 else SUB).wait()


def step(chunk, rows, levels, columns, rotate, blocks, kept, news):
    first = chunk == 0
    last = chunk == len(CHUNKS) - 1
    tiles = CHUNKS[chunk]
    wide = columns + LANES
    tall = rows + 2 * RIM
    vmem = pl.BlockSpec(memory_space=pltpu.VMEM)
    hbm = pl.BlockSpec(memory_space=pl.ANY)
    operands = [rotate, *blocks]
    in_specs = [vmem] * 5
    if not first:
        operands += [*kept, *news]
        in_specs += [vmem] * 3 + [hbm] * FIELDS
    carry = (tall - 2 + rows + 2, SUB, wide)
    sums = (2, rows, SUB, wide)
    shapes = [jax.ShapeDtypeStruct((levels * rows, columns), F32)] * FIELDS
    out_specs = [hbm] * FIELDS
    row = pltpu.VMEM((tall, SUB, wide), F32)
    fields = pltpu.VMEM((FIELDS, tall, SUB, wide), F32)
    scratch = [fields] + [row] * 7 + [fields] * 3
    scratch += [pltpu.VMEM((FIELDS, 2, tiles * SUB * rows, LANES), F32)]
    if first:
        shapes += [jax.ShapeDtypeStruct((4, tall, SUB, wide), F32)]
        shapes += [jax.ShapeDtypeStruct((tall, wide), F32)] * 2
        scratch += [pltpu.VMEM((2, tall, SUB, wide), F32)]
    if last:
        shapes += [jax.ShapeDtypeStruct((2, RIM, wide), F32)] * 2
        scratch += [pltpu.VMEM(carry, F32), pltpu.VMEM(sums, F32)]
    else:
        shapes += [jax.ShapeDtypeStruct(carry, F32), jax.ShapeDtypeStruct(sums, F32)]
    out_specs += [vmem] * (len(shapes) - FIELDS)
    scratch += [pltpu.SemaphoreType.DMA((tiles, FIELDS, 2))]
    aliases = {} if first else {len(operands) - FIELDS + f: f for f in range(FIELDS)}
    return pl.pallas_call(
        functools.partial(step_kernel, chunk, rows),
        out_shape=shapes,
        in_specs=in_specs,
        out_specs=out_specs,
        scratch_shapes=scratch,
        input_output_aliases=aliases,
        compiler_params=pltpu.CompilerParams(vmem_limit_bytes=16 * 1024 * 1024),
        name="step",
    )(*operands)


def shift_rows(x, count):
    return pltpu.roll(x, count % x.shape[0], 0)


def weighed(weights, e):
    east, west = east_of(e), west_of(e)
    return (
        weights[0] * shift_rows(east, -1) + weights[1] * shift_rows(west, -1)
    ) + (weights[2] * shift_rows(east, 1) + weights[3] * shift_rows(west, 1))


def prepare_kernel(levels, deep_ref, surface_ref, out):
    deep = deep_ref[...]
    surface = surface_ref[...]
    ocean = jnp.where(deep > 0.0, 1.0, 0.0)
    pair = jnp.minimum(deep, east_of(deep))
    north_east = jnp.minimum(pair, shift_rows(pair, -1)) / levels
    north_west = west_of(north_east)
    corners = (north_east, north_west, shift_rows(north_east, 1), shift_rows(north_west, 1))
    share = 1.0 / (PHI + 0.5 * ((corners[0] + corners[1]) + (corners[2] + corners[3])))
    weights = [(0.5 * share) * corner for corner in corners]
    for k in range(4):
        out[k] = weights[k]
    out[4] = (PHI * ocean * share) * surface - (surface - weighed(weights, surface))
    across = ocean * east_of(ocean)
    along = ocean * shift_rows(ocean, -1)
    scale = (-0.5 * DIVERGE) * share
    out[5] = scale * across
    out[6] = scale * west_of(across)
    out[7] = scale * along
    out[8] = scale * shift_rows(along, 1)
    out[9] = surface


def solve_kernel(rows, ready, met_a, own_a, own_b, met_b, out):
    odd = jnp.broadcast_to(parities()[0], ready.shape[1:]) == 1
    flows = []
    for f in range(2):
        lines = [ref[f] for ref in (met_a, own_a, own_b, met_b)]
        flows.append(
            jnp.where(odd, jnp.concatenate(lines, axis=0), jnp.concatenate(lines[::-1], axis=0))
        )
    weights = [ready[k] for k in range(4)]
    east, north = flows
    scaled = ready[4] + (
        (ready[5] * (east_of(east) - east) + ready[6] * (east - west_of(east)))
        + (
            ready[7] * (shift_rows(north, -1) - north)
            + ready[8] * (north - shift_rows(north, 1))
        )
    )
    opening, updates = chebyshev_weights(ITERS)
    direction = opening * scaled
    total = ready[9]
    for index in range(ITERS):
        total = total + direction
        if index + 1 < ITERS:
            scaled = scaled - (direction - weighed(weights, direction))
            keep, push = updates[index]
            direction = keep * direction + push * scaled
    out[...] = total[RIM : RIM + rows, : out.shape[1]]


def body(
    eastward_flow,
    northward_flow,
    heat_anomaly,
    salt_anomaly,
    air_stress_forcing,
    earlier_sea_height_load,
    ocean_layer_depths,
):
    levels, rows, columns = eastward_flow.shape
    assert rows == 2 * RIM and columns == 2 * LANES and levels + EXTRA == SUB * sum(CHUNKS)
    along_y, along_x = lax.axis_size("by"), lax.axis_size("bx")
    pairs_y = (swaps(along_y, 1, False), swaps(along_y, 0, False))
    pairs_x = (swaps(along_x, 0, True), swaps(along_x, 1, True))
    row_index = lax.axis_index("by") * rows - RIM + jnp.arange(rows + 2 * RIM)
    rotate = 1.2 * jnp.sin(
        0.9 * math.pi * ((row_index.astype(F32) + 0.5) / (rows * along_y) - 0.5)
    )
    rotate = jnp.broadcast_to(rotate[:, None], (rows + 2 * RIM, columns + LANES))

    fields = (eastward_flow, northward_flow, heat_anomaly, salt_anomaly)
    edge_a, edge_b, held, lines = pack_edges(
        fields, air_stress_forcing, earlier_sea_height_load, ocean_layer_depths
    )
    halves = pack_halves(rows, held, lines)
    across_a = lax.ppermute(edge_a, "bx", pairs_x[0])
    across_b = lax.ppermute(edge_b, "bx", pairs_x[1])
    halves = put_rims(halves, across_a, across_b)

    def send(own):
        return [lax.ppermute(item, "by", pairs) for item, pairs in zip(own, pairs_y)]

    rims = [send(halves[chunk]) for chunk in range(AHEAD)]
    kept, news = None, None
    for chunk in range(len(CHUNKS)):
        own_a, own_b = halves[chunk]
        met_a, met_b = rims[chunk]
        blocks = (met_a, own_a, own_b, met_b)
        outs = step(chunk, rows, levels, columns, rotate, blocks, kept, news)
        news, rest = outs[:FIELDS], outs[FIELDS:]
        if chunk == 0:
            deeps, depth_wide, surface_wide = rest[:3]
            rest = rest[3:]
        later = chunk + AHEAD
        if later < len(CHUNKS):
            *halves[later], one, two = lax.optimization_barrier((*halves[later], *rest))
            rest = (one, two)
            rims.append(send(halves[later]))
        kept = (deeps, *rest)
    own_a, own_b = rest
    depth_wide, surface_wide, own_a, own_b = lax.optimization_barrier(
        (depth_wide, surface_wide, own_a, own_b)
    )
    met_a, met_b = send((own_a, own_b))
    vmem = pl.BlockSpec(memory_space=pltpu.VMEM)
    ready = pl.pallas_call(
        functools.partial(prepare_kernel, levels),
        out_shape=jax.ShapeDtypeStruct((10, *depth_wide.shape), F32),
        in_specs=[vmem] * 2,
        out_specs=vmem,
        compiler_params=pltpu.CompilerParams(vmem_limit_bytes=SMALL_VMEM),
        name="prepare",
    )(depth_wide, surface_wide)
    surface_new = pl.pallas_call(
        functools.partial(solve_kernel, rows),
        out_shape=jax.ShapeDtypeStruct((rows, columns), F32),
        in_specs=[vmem] * 5,
        out_specs=vmem,
        compiler_params=pltpu.CompilerParams(vmem_limit_bytes=SMALL_VMEM),
        name="solve",
    )(ready, met_a, own_a, own_b, met_b)
    shaped = [item.reshape(levels, rows, columns) for item in news]
    return (*shaped, surface_new)


def solution(mesh):
    return jax.shard_map(
        body,
        mesh=mesh,
        in_specs=(P(None, "by", "bx"),) * 5 + (P("by", "bx"),) * 2,
        out_specs=(P(None, "by", "bx"),) * 4 + (P("by", "bx"),),
        check_vma=False,
    )
```

```python
import functools
import math

import jax
import jax.numpy as jnp
from jax import lax
from jax.experimental import pallas as pl
from jax.experimental.pallas import tpu as pltpu
from jax.sharding import PartitionSpec as P

ITERS = 4
KAPPA = 0.004
ADVECT = 0.25
PRESS = 0.1
WIND = 0.5
PHI = 0.5
DIVERGE = 2.0
LOWER = 0.2
UPPER = 2.0

SUB = 8
LANES = 128
FIELDS = 4
RIM = 4
EDGE = 8
EXTRA = 2
CHUNKS = (2, 2, 2, 2)
AHEAD = 3
FAR = 1000000
BATCH = 4
GROUPS = ((0,), (1,), (2,), (3,))
SMALL_VMEM = 4 * 1024 * 1024
PACK_VMEM = 8 * 1024 * 1024
F32 = jnp.float32


def chebyshev_weights(count):
    middle = 0.5 * (UPPER + LOWER)
    half_span = 0.5 * (UPPER - LOWER)
    ratio_value = middle / half_span
    rho_now = 1.0 / ratio_value
    updates = []
    for index in range(count - 1):
        rho_next = 1.0 / (2.0 * ratio_value - rho_now)
        updates.append((rho_next * rho_now, 2.0 * rho_next / half_span))
        rho_now = rho_next
    return (1.0 / middle, updates)


def swaps(count, first, ring):
    pairs = []
    for i in range(first, count if ring else count - 1, 2):
        j = (i + 1) % count
        pairs += [(i, j), (j, i)]
    return pairs


def first_level(chunk):
    return SUB * sum(CHUNKS[:chunk]) - (EXTRA if chunk else 0)


def chunk_levels(chunk):
    return SUB * CHUNKS[chunk] - (0 if chunk else EXTRA)


def parities():
    return lax.axis_index("by") & 1, lax.axis_index("bx") & 1


def first_rows():
    odd = parities()[0]
    return (1 - odd) * RIM, odd * RIM


def edges_kernel(rows, *refs):
    fields, sources = refs[:FIELDS], refs[FIELDS : FIELDS + 3]
    across_a, across_b, held, lines, mixed, depth, sems, sems_lines = refs[FIELDS + 3 :]
    small = [
        pltpu.make_async_copy(source, into, sems_lines.at[k])
        for k, (source, into) in enumerate(
            zip(sources, (lines.at[pl.ds(EXTRA, EXTRA)], lines.at[1], depth))
        )
    ]

    def copy(f, lane):
        return pltpu.make_async_copy(
            fields[f].at[:, pl.ds(lane * LANES, LANES)], held.at[f, lane], sems.at[f, lane]
        )

    for f in range(FIELDS):
        for lane in range(2):
            copy(f, lane).start()
    for item in small:
        item.start()
    across_a[...] = jnp.zeros(across_a.shape, F32)
    across_b[...] = jnp.zeros(across_b.shape, F32)
    for item in small:
        item.wait()
    lines[0] = depth[...].astype(F32)
    lanes = lax.broadcasted_iota(jnp.int32, (SUB, LANES), 1)
    odd = jnp.broadcast_to(parities()[1], (SUB, LANES)) == 1
    tiles = [(c, t) for c in range(len(CHUNKS)) for t in range(CHUNKS[c])]
    for f in range(FIELDS):
        for lane in range(2):
            copy(f, lane).wait()
        for group in range(2):
            for q in range(RIM):
                place_tile(mixed.at[f, group, q], held, lines, rows, group, f, q, 0, CHUNKS[0] - 1)
        for slot, (c, t) in enumerate(tiles):
            base = (first_level(c) + SUB * t) * rows
            for group in range(2):
                west, east = across_a[group, slot], across_b[group, slot]
                for q in range(RIM):
                    place = (q * FIELDS + f) * EDGE
                    other = (place - EDGE) % LANES
                    if c == 0 and t == CHUNKS[0] - 1:
                        low = mixed[f, group, q, :, pl.ds(0, LANES)]
                        high = mixed[f, group, q, :, pl.ds(LANES, LANES)]
                    else:
                        row = pl.ds(base + first_rows()[group] + q, SUB, stride=rows)
                        low = held[f, 0, row, :]
                        high = held[f, 1, row, :]
                    if place:
                        low = pltpu.roll(low, place, 1)
                        high = pltpu.roll(high, place, 1)
                    west = jnp.where((lanes >= place) & (lanes < place + EDGE), low, west)
                    east = jnp.where((lanes >= other) & (lanes < other + EDGE), high, east)
                if f == FIELDS - 1:
                    west, east = jnp.where(odd, west, east), jnp.where(odd, east, west)
                across_a[group, slot] = west
                across_b[group, slot] = east


def place_tile(ref, held, lines, rows, group, f, q, chunk, t):
    used = min(SUB, chunk_levels(chunk) - SUB * t)
    base = (first_level(chunk) + SUB * t) * rows
    row = first_rows()[group] + q
    for lane in range(2):
        ref[pl.ds(0, used), pl.ds(lane * LANES, LANES)] = held[
            f, lane, pl.ds(base + row, used, stride=rows), :
        ]
    for extra in range(SUB - used):
        if f < 2:
            line = lines[EXTRA * f + extra, pl.ds(row, 1), :]
        else:
            line = jnp.zeros((1, 2 * LANES), F32)
        ref[pl.ds(used + extra, 1), :] = line


def halves_kernel(rows, chunks, held, lines, across_a, across_b, *halves):
    for k, c in enumerate(chunks):
        for t in range(CHUNKS[c]):
            slot = sum(CHUNKS[:c]) + t
            for group in range(2):
                half = halves[2 * k + group]
                for f in range(FIELDS):
                    for q in range(RIM):
                        ref = half.at[f * RIM + q, t]
                        place_tile(ref, held, lines, rows, group, f, q, c, t)
                half[FIELDS * RIM, t, :, pl.ds(0, LANES)] = across_a[group, slot]
                half[FIELDS * RIM, t, :, pl.ds(LANES, LANES)] = across_b[group, slot]


def pack_edges(fields, wind, surface, depth):
    levels, rows, columns = fields[0].shape
    flat = [item.reshape(levels * rows, columns) for item in fields]
    arguments = [
        pltpu.with_memory_space_constraint(item, pltpu.HBM)
        for item in (*flat, wind, surface, depth)
    ]
    vmem = pl.BlockSpec(memory_space=pltpu.VMEM)
    return pl.pallas_call(
        functools.partial(edges_kernel, rows),
        out_shape=[jax.ShapeDtypeStruct((2, sum(CHUNKS), SUB, LANES), F32)] * 2
        + [
            jax.ShapeDtypeStruct((FIELDS, 2, levels * rows, LANES), F32),
            jax.ShapeDtypeStruct((2 * EXTRA, rows, columns), F32),
        ],
        in_specs=[pl.BlockSpec(memory_space=pltpu.HBM)] * len(arguments),
        out_specs=[vmem] * 4,
        scratch_shapes=[
            pltpu.VMEM((FIELDS, 2, RIM, SUB, columns), F32),
            pltpu.VMEM(depth.shape, depth.dtype),
            pltpu.SemaphoreType.DMA((FIELDS, 2)),
            pltpu.SemaphoreType.DMA((3,)),
        ],
        compiler_params=pltpu.CompilerParams(vmem_limit_bytes=PACK_VMEM),
        name="edges",
    )(*arguments)


def pack_halves(rows, chunks, held, lines, across_a, across_b):
    vmem = pl.BlockSpec(memory_space=pltpu.VMEM)
    shapes = [
        jax.ShapeDtypeStruct((FIELDS * RIM + 1, CHUNKS[c], SUB, lines.shape[-1]), F32)
        for c in chunks
        for _ in range(2)
    ]
    outs = pl.pallas_call(
        functools.partial(halves_kernel, rows, chunks),
        out_shape=shapes,
        in_specs=[vmem] * 4,
        out_specs=[vmem] * len(shapes),
        compiler_params=pltpu.CompilerParams(vmem_limit_bytes=SMALL_VMEM),
        name="halves",
    )(held, lines, across_a, across_b)
    return [list(outs[k : k + 2]) for k in range(0, len(outs), 2)]


def east_of(value):
    return pltpu.roll(value, value.shape[-1] - 1, value.ndim - 1)


def west_of(value):
    return pltpu.roll(value, 1, value.ndim - 1)


def step_kernel(chunk, rows, *refs):
    first = chunk == 0
    last = chunk == len(CHUNKS) - 1
    tiles = CHUNKS[chunk]
    levels = chunk_levels(chunk)
    tall = rows + 2 * RIM
    refs = list(refs)

    def take(count):
        taken = refs[:count]
        del refs[:count]
        return taken

    (rotate,) = take(1)
    blocks = take(4)
    if not first:
        deeps_in, carry_in, sums_in = take(3)
        take(FIELDS)
    outs = take(FIELDS)
    if first:
        deeps, depth_out, surface_out = take(3)
    else:
        deeps = deeps_in
    if last:
        sums_a, sums_b = take(2)
    else:
        carry_out, sums_out = take(2)
    cur, wets, wets_x, wets_w, wets_y, press, press_x, press_y, laps, mixes, between, held = take(12)
    if first:
        (winds,) = take(1)
    if last:
        carry, sums = take(2)
    else:
        carry, sums = carry_out, sums_out
    (sems,) = take(1)

    if first:
        carry[...] = jnp.zeros(carry.shape, F32)
        sums[...] = jnp.zeros(sums.shape, F32)
    else:
        carry[...] = carry_in[...]
        sums[...] = sums_in[...]

    lanes = lax.broadcasted_iota(jnp.int32, (SUB, LANES), 1)
    own = blocks[0].shape[-1]
    wide = own + LANES
    every = range(FIELDS)
    odd_y, odd_x = parities()
    bases = [odd_y * (RIM * k) + (1 - odd_y) * (RIM * (3 - k)) for k in range(4)]
    swapped = ((lanes // EDGE) & 1) != 1 - odd_x

    def rims_of(k, t):
        both = blocks[k][FIELDS * RIM, t]
        one, two = both[:, :LANES], both[:, LANES:]
        mixed = (jnp.where(swapped, one, two), jnp.where(swapped, two, one))

        def rim(f, q):
            place = (q * FIELDS + f) * EDGE
            return pltpu.roll(mixed[f % 2], LANES - place, 1) if place else mixed[f % 2]

        return rim

    if first:
        for k in range(4):
            rim = rims_of(k, tiles - 1)
            for q in range(RIM):
                block = [
                    jnp.concatenate([blocks[k][f * RIM + q, tiles - 1], rim(f, q)], axis=1)
                    for f in range(2)
                ]
                for f, extra, ref in (
                    (0, 0, deeps.at[0]),
                    (0, 1, deeps.at[1]),
                    (1, 0, winds.at[0]),
                    (1, 1, winds.at[1]),
                ):
                    slot = SUB - EXTRA + extra
                    ref[bases[k] + q] = jnp.broadcast_to(block[f][slot : slot + 1, :], (SUB, wide))
        for a in range(tall):
            surface_out[pl.ds(a, 1), :] = deeps[1, a, pl.ds(0, 1), :]
            depth_out[pl.ds(a, 1), :] = deeps[0, a, pl.ds(0, 1), :]
        for a in range(tall):
            here = deeps[0, a]
            deeps[1, a] = jnp.minimum(here, east_of(here))
            deeps[2, a] = jnp.minimum(here, west_of(here))
            deeps[3, a] = jnp.minimum(here, deeps[0, min(a + 1, tall - 1)])

    subs = lax.broadcasted_iota(jnp.int32, (SUB, wide), 0)

    def pressure(get, lowest, highest, carry_at):
        for first_row in range(lowest - 1, highest + 2, BATCH):
            rows_p = range(first_row, min(first_row + BATCH, highest + 2))
            sums_p = [
                ((-0.4 * PRESS) * get(2, a) + (0.3 * PRESS) * get(3, a)) * wets[a] for a in rows_p
            ]
            for shift in (1, 2, 4):
                moved = [pltpu.roll(value, shift, 0) for value in sums_p]
                sums_p = [
                    value + jnp.where(subs >= shift, other, 0.0)
                    for value, other in zip(sums_p, moved)
                ]
            places = [carry_at + a - (lowest - 1) for a in rows_p]
            sums_p = [value + carry[place] for value, place in zip(sums_p, places)]
            ends = [jnp.broadcast_to(value[SUB - 1 : SUB, :], value.shape) for value in sums_p]
            for k, a in enumerate(rows_p):
                press[a] = sums_p[k]
                carry[places[k]] = ends[k]
        slope = wets_y[lowest - 1] * (press[lowest] - press[lowest - 1])
        for first_row in range(lowest, highest + 1, BATCH):
            rows_p = range(first_row, min(first_row + BATCH, highest + 1))
            here = [press[a] for a in rows_p]
            east = [east_of(x) for x in here]
            west = [west_of(x) for x in here]
            across = [
                wets_x[a] * (east[k] - here[k]) + wets_w[a] * (here[k] - west[k])
                for k, a in enumerate(rows_p)
            ]
            here.append(press[rows_p[-1] + 1])
            slopes = [slope] + [
                wets_y[a] * (here[k + 1] - here[k]) for k, a in enumerate(rows_p)
            ]
            slope = slopes[-1]
            for k, a in enumerate(rows_p):
                press_x[a] = across[k]
                press_y[a] = slopes[k + 1] + slopes[k]

    def tendency(get, lowest, highest, carry_at, emit, finish=None):
        pressure(get, lowest, highest, carry_at)
        widths = [own if finish is not None and group[0] > 1 else wide for group in GROUPS]
        for group, width in zip(GROUPS, widths):
            first_pass(get, lowest, highest, group, width)
        for group, width in zip(GROUPS, widths):
            second_pass(lowest, highest, group, emit, width)
            if finish is not None:
                finish(group)

    def turned(get, group, a):
        values = [get(f, a) for f in group]
        return values, [east_of(x) for x in values], [west_of(x) for x in values]

    def first_pass(get, lowest, highest, group, width):
        span = range(len(group))
        below = [get(f, lowest - 2) for f in group]
        here, east, west = turned(get, group, lowest - 1)
        face = wets_y[lowest - 2]
        up = [face * (x - y) for x, y in zip(here, below)]
        for a in range(lowest - 1, highest + 2):
            if a <= highest:
                after, east_after, west_after = turned(get, group, a + 1)
            else:
                after = [get(f, a + 1) for f in group]
            face, side_x, side_w = wets_y[a], wets_x[a], wets_w[a]
            up_before = up
            up = [face * (x - y) for x, y in zip(after, here)]
            right = [side_x * (x - y) for x, y in zip(east, here)]
            left = [side_w * (x - y) for x, y in zip(here, west)]
            lap = [(right[i] - left[i]) + (up[i] - up_before[i]) for i in span]
            if lowest <= a <= highest:
                flows = [here[group.index(f)] if f in group else get(f, a) for f in range(2)]
                u, v = (-0.5 * ADVECT) * flows[0], (-0.5 * ADVECT) * flows[1]
                mixed = [
                    u[:, :width] * (right[i] + left[i])[:, :width]
                    + v[:, :width] * (up[i] + up_before[i])[:, :width]
                    for i in span
                ]
                for i, f in enumerate(group):
                    if f < 2:
                        turn = rotate[pl.ds(a, 1), :] * wets[a]
                    if f == 0:
                        mixed[i] = mixed[i] + (turn * flows[1] - press_x[a])
                    if f == 1:
                        mixed[i] = mixed[i] - (turn * flows[0] + press_y[a])
                for i, f in enumerate(group):
                    mixes[f, a, :, pl.ds(0, width)] = mixed[i]
            for i, f in enumerate(group):
                laps[f, a] = lap[i]
            if a <= highest:
                here, east, west = after, east_after, west_after

    def second_pass(lowest, highest, group, emit, width):
        span = range(len(group))
        part = pl.ds(0, width)

        def get(f, a):
            return laps[f, a]

        below = [laps[f, lowest - 1, :, part] for f in group]
        here, east, west = turned(get, group, lowest)
        face = wets_y[lowest - 1, :, part]
        up = [face * (x[:, :width] - y) for x, y in zip(here, below)]
        for a in range(lowest, highest + 1):
            if a < highest:
                after, east_after, west_after = turned(get, group, a + 1)
            else:
                after = [get(f, a + 1) for f in group]
            face, side_x, side_w = (ref[a, :, part] for ref in (wets_y, wets_x, wets_w))
            near = [x[:, :width] for x in here]
            up_before = up
            up = [face * (x[:, :width] - y) for x, y in zip(after, near)]
            smooth = [
                (side_x * (east[i][:, :width] - near[i]) - side_w * (near[i] - west[i][:, :width]))
                + (up[i] - up_before[i])
                for i in span
            ]
            mixed = [mixes[f, a, :, part] for f in group]
            emit(a, group, [x - KAPPA * y for x, y in zip(mixed, smooth)])
            if a < highest:
                here, east, west = after, east_after, west_after

    def tile(t, _):
        for k in range(4):
            rim = rims_of(k, t)
            for q in range(RIM):
                for f in every:
                    cur[f, bases[k] + q, :, pl.ds(0, own)] = blocks[k][f * RIM + q, t]
                    cur[f, bases[k] + q, :, pl.ds(own, LANES)] = rim(f, q)
        level = subs + (first_level(chunk) + SUB * t)
        if first:
            level = jnp.where(level >= levels, FAR, level)
        level = level.astype(F32)
        top = jnp.where(level == 0.0, WIND, 0.0)
        for a in range(tall):
            for k, ref in enumerate((wets, wets_x, wets_w, wets_y)):
                ref[a] = jnp.where(level < deeps[k, a], 1.0, 0.0)

        def winded(a, group, values):
            if not first:
                return values
            return [
                value + (top * wets[a]) * winds[f, a] if f < 2 else value
                for f, value in zip(group, values)
            ]

        def emit_first(a, group, values):
            values = winded(a, group, values)
            values = [cur[f, a] + value for f, value in zip(group, values)]
            for f, value in zip(group, values):
                between[f, a] = value

        tendency(lambda f, a: cur[f, a], 2, tall - 3, 0, emit_first)

        def emit_second(a, group, values):
            values = winded(a, group, values)
            part = pl.ds(0, values[0].shape[-1])
            news = [
                0.5 * ((cur[f, a, :, part] + between[f, a, :, part]) + value)
                for f, value in zip(group, values)
            ]
            r = a - RIM
            adds = [sums[f, r] + wets[a] * new for f, new in zip(group, news) if f < 2]
            for f, add in zip(group, adds):
                sums[f, r] = add
            for f, new in zip(group, news):
                for lane in range(2):
                    held[f, lane, pl.ds(t * (SUB * rows) + r, SUB, stride=rows), :] = new[
                        :, lane * LANES : (lane + 1) * LANES
                    ]

        def finish(group):
            def leave(count):
                for f in group:
                    for lane in range(2):
                        copy(f, lane, t, count).start()

            if final == SUB:
                leave(SUB)
            else:
                pl.when(t < tiles - 1)(lambda: leave(SUB))
                pl.when(t == tiles - 1)(lambda: leave(final))

        tendency(lambda f, a: between[f, a], RIM, tall - RIM - 1, tall - 2, emit_second, finish)
        return 0

    def copy(f, lane, t, count):
        size = count * rows
        at = (first_level(chunk) + SUB * t) * rows
        return pltpu.make_async_copy(
            held.at[f, lane, pl.ds(t * (SUB * rows), size)],
            outs[f].at[pl.ds(at, size), pl.ds(lane * LANES, LANES)],
            sems.at[t, f, lane],
        )

    final = levels - SUB * (tiles - 1)
    lax.fori_loop(0, tiles, tile, 0)
    if last:
        depth_levels = first_level(chunk) + levels
        for f in range(2):
            for ref, at in ((sums_a, (1 - odd_y) * RIM), (sums_b, odd_y * RIM)):
                for q in range(RIM):
                    line = jnp.sum(sums[f, at + q], axis=0, keepdims=True) / depth_levels
                    ref[f, pl.ds(q, 1), :] = line
    for t in range(tiles):
        for f in every:
            for lane in range(2):
                copy(f, lane, t, final if t == tiles - 1 else SUB).wait()


def step(chunk, rows, levels, columns, rotate, blocks, kept, news):
    first = chunk == 0
    last = chunk == len(CHUNKS) - 1
    tiles = CHUNKS[chunk]
    wide = columns + LANES
    tall = rows + 2 * RIM
    vmem = pl.BlockSpec(memory_space=pltpu.VMEM)
    hbm = pl.BlockSpec(memory_space=pl.ANY)
    operands = [rotate, *blocks]
    in_specs = [vmem] * 5
    if not first:
        operands += [*kept, *news]
        in_specs += [vmem] * 3 + [hbm] * FIELDS
    carry = (tall - 2 + rows + 2, SUB, wide)
    sums = (2, rows, SUB, wide)
    shapes = [jax.ShapeDtypeStruct((levels * rows, columns), F32)] * FIELDS
    out_specs = [hbm] * FIELDS
    row = pltpu.VMEM((tall, SUB, wide), F32)
    fields = pltpu.VMEM((FIELDS, tall, SUB, wide), F32)
    scratch = [fields] + [row] * 7 + [fields] * 3
    scratch += [pltpu.VMEM((FIELDS, 2, tiles * SUB * rows, LANES), F32)]
    if first:
        shapes += [jax.ShapeDtypeStruct((4, tall, SUB, wide), F32)]
        shapes += [jax.ShapeDtypeStruct((tall, wide), F32)] * 2
        scratch += [pltpu.VMEM((2, tall, SUB, wide), F32)]
    if last:
        shapes += [jax.ShapeDtypeStruct((2, RIM, wide), F32)] * 2
        scratch += [pltpu.VMEM(carry, F32), pltpu.VMEM(sums, F32)]
    else:
        shapes += [jax.ShapeDtypeStruct(carry, F32), jax.ShapeDtypeStruct(sums, F32)]
    out_specs += [vmem] * (len(shapes) - FIELDS)
    scratch += [pltpu.SemaphoreType.DMA((tiles, FIELDS, 2))]
    aliases = {} if first else {len(operands) - FIELDS + f: f for f in range(FIELDS)}
    return pl.pallas_call(
        functools.partial(step_kernel, chunk, rows),
        out_shape=shapes,
        in_specs=in_specs,
        out_specs=out_specs,
        scratch_shapes=scratch,
        input_output_aliases=aliases,
        compiler_params=pltpu.CompilerParams(vmem_limit_bytes=16 * 1024 * 1024),
        name="step",
    )(*operands)


def shift_rows(x, count):
    return pltpu.roll(x, count % x.shape[0], 0)


def weighed(weights, e):
    east, west = east_of(e), west_of(e)
    return (
        weights[0] * shift_rows(east, -1) + weights[1] * shift_rows(west, -1)
    ) + (weights[2] * shift_rows(east, 1) + weights[3] * shift_rows(west, 1))


def prepare_kernel(levels, deep_ref, surface_ref, out):
    deep = deep_ref[...]
    surface = surface_ref[...]
    ocean = jnp.where(deep > 0.0, 1.0, 0.0)
    pair = jnp.minimum(deep, east_of(deep))
    north_east = jnp.minimum(pair, shift_rows(pair, -1)) / levels
    north_west = west_of(north_east)
    corners = (north_east, north_west, shift_rows(north_east, 1), shift_rows(north_west, 1))
    share = 1.0 / (PHI + 0.5 * ((corners[0] + corners[1]) + (corners[2] + corners[3])))
    weights = [(0.5 * share) * corner for corner in corners]
    for k in range(4):
        out[k] = weights[k]
    out[4] = (PHI * ocean * share) * surface - (surface - weighed(weights, surface))
    across = ocean * east_of(ocean)
    along = ocean * shift_rows(ocean, -1)
    scale = (-0.5 * DIVERGE) * share
    out[5] = scale * across
    out[6] = scale * west_of(across)
    out[7] = scale * along
    out[8] = scale * shift_rows(along, 1)
    out[9] = surface


def solve_kernel(rows, ready, met_a, own_a, own_b, met_b, out):
    odd = jnp.broadcast_to(parities()[0], ready.shape[1:]) == 1
    flows = []
    for f in range(2):
        lines = [ref[f] for ref in (met_a, own_a, own_b, met_b)]
        flows.append(
            jnp.where(odd, jnp.concatenate(lines, axis=0), jnp.concatenate(lines[::-1], axis=0))
        )
    weights = [ready[k] for k in range(4)]
    east, north = flows
    scaled = ready[4] + (
        (ready[5] * (east_of(east) - east) + ready[6] * (east - west_of(east)))
        + (
            ready[7] * (shift_rows(north, -1) - north)
            + ready[8] * (north - shift_rows(north, 1))
        )
    )
    opening, updates = chebyshev_weights(ITERS)
    direction = opening * scaled
    total = ready[9]
    for index in range(ITERS):
        total = total + direction
        if index + 1 < ITERS:
            scaled = scaled - (direction - weighed(weights, direction))
            keep, push = updates[index]
            direction = keep * direction + push * scaled
    out[...] = total[RIM : RIM + rows, : out.shape[1]]


def body(
    eastward_flow,
    northward_flow,
    heat_anomaly,
    salt_anomaly,
    air_stress_forcing,
    earlier_sea_height_load,
    ocean_layer_depths,
):
    levels, rows, columns = eastward_flow.shape
    assert rows == 2 * RIM and columns == 2 * LANES and levels + EXTRA == SUB * sum(CHUNKS)
    along_y, along_x = lax.axis_size("by"), lax.axis_size("bx")
    pairs_y = (swaps(along_y, 0, False), swaps(along_y, 1, False))
    pairs_x = (swaps(along_x, 0, True), swaps(along_x, 1, True))
    row_index = lax.axis_index("by") * rows - RIM + jnp.arange(rows + 2 * RIM)
    rotate = 1.2 * jnp.sin(
        0.9 * math.pi * ((row_index.astype(F32) + 0.5) / (rows * along_y) - 0.5)
    )
    rotate = jnp.broadcast_to(rotate[:, None], (rows + 2 * RIM, columns + LANES))

    fields = (eastward_flow, northward_flow, heat_anomaly, salt_anomaly)
    edge_a, edge_b, held, lines = pack_edges(
        fields, air_stress_forcing, earlier_sea_height_load, ocean_layer_depths
    )
    across_a = lax.ppermute(edge_a, "bx", pairs_x[0])
    across_b = lax.ppermute(edge_b, "bx", pairs_x[1])
    made = (held, lines, across_a, across_b)
    halves = pack_halves(rows, (0,), *made)
    halves += pack_halves(rows, tuple(range(1, len(CHUNKS))), *made)

    def send(own):
        return [lax.ppermute(item, "by", pairs) for item, pairs in zip(own, pairs_y)]

    rims = [send(halves[chunk]) for chunk in range(AHEAD)]
    kept, news = None, None
    for chunk in range(len(CHUNKS)):
        own_a, own_b = halves[chunk]
        met_a, met_b = rims[chunk]
        blocks = [met_a, own_a, own_b, met_b]
        outs = step(chunk, rows, levels, columns, rotate, blocks, kept, news)
        news, rest = outs[:FIELDS], outs[FIELDS:]
        if chunk == 0:
            deeps, depth_wide, surface_wide = rest[:3]
            rest = rest[3:]
        later = chunk + AHEAD
        if later < len(CHUNKS):
            *halves[later], one, two = lax.optimization_barrier((*halves[later], *rest))
            rest = (one, two)
            rims.append(send(halves[later]))
        kept = (deeps, *rest)
    own_a, own_b = rest
    depth_wide, surface_wide, own_a, own_b = lax.optimization_barrier(
        (depth_wide, surface_wide, own_a, own_b)
    )
    met_a, met_b = send((own_a, own_b))
    vmem = pl.BlockSpec(memory_space=pltpu.VMEM)
    ready = pl.pallas_call(
        functools.partial(prepare_kernel, levels),
        out_shape=jax.ShapeDtypeStruct((10, *depth_wide.shape), F32),
        in_specs=[vmem] * 2,
        out_specs=vmem,
        compiler_params=pltpu.CompilerParams(vmem_limit_bytes=SMALL_VMEM),
        name="prepare",
    )(depth_wide, surface_wide)
    surface_new = pl.pallas_call(
        functools.partial(solve_kernel, rows),
        out_shape=jax.ShapeDtypeStruct((rows, columns), F32),
        in_specs=[vmem] * 5,
        out_specs=vmem,
        compiler_params=pltpu.CompilerParams(vmem_limit_bytes=SMALL_VMEM),
        name="solve",
    )(ready, met_a, own_a, own_b, met_b)
    shaped = [item.reshape(levels, rows, columns) for item in news]
    return (*shaped, surface_new)


def solution(mesh):
    return jax.shard_map(
        body,
        mesh=mesh,
        in_specs=(P(None, "by", "bx"),) * 5 + (P("by", "bx"),) * 2,
        out_specs=(P(None, "by", "bx"),) * 4 + (P("by", "bx"),),
        check_vma=False,
    )
```

```python
import functools
import math

import jax
import jax.numpy as jnp
from jax import lax
from jax.experimental import pallas as pl
from jax.experimental.pallas import tpu as pltpu
from jax.sharding import PartitionSpec as P

ITERS = 4
KAPPA = 0.004
ADVECT = 0.25
PRESS = 0.1
WIND = 0.5
PHI = 0.5
DIVERGE = 2.0
LOWER = 0.2
UPPER = 2.0

SUB = 8
LANES = 128
FIELDS = 4
RIM = 4
EDGE = 8
EXTRA = 2
CHUNKS = (2, 2, 2, 2)
AHEAD = 3
FAR = 1000000
BATCH = 7
GROUPS = ((0,), (1,), (2,), (3,))
SMALL_VMEM = 4 * 1024 * 1024
PACK_VMEM = 8 * 1024 * 1024
F32 = jnp.float32


def chebyshev_weights(count):
    middle = 0.5 * (UPPER + LOWER)
    half_span = 0.5 * (UPPER - LOWER)
    ratio_value = middle / half_span
    rho_now = 1.0 / ratio_value
    updates = []
    for index in range(count - 1):
        rho_next = 1.0 / (2.0 * ratio_value - rho_now)
        updates.append((rho_next * rho_now, 2.0 * rho_next / half_span))
        rho_now = rho_next
    return (1.0 / middle, updates)


def swaps(count, first, ring):
    pairs = []
    for i in range(first, count if ring else count - 1, 2):
        j = (i + 1) % count
        pairs += [(i, j), (j, i)]
    return pairs


def first_level(chunk):
    return SUB * sum(CHUNKS[:chunk]) - (EXTRA if chunk else 0)


def chunk_levels(chunk):
    return SUB * CHUNKS[chunk] - (0 if chunk else EXTRA)


def parities():
    return lax.axis_index("by") & 1, lax.axis_index("bx") & 1


def first_rows():
    odd = parities()[0]
    return (1 - odd) * RIM, odd * RIM


def edges_kernel(rows, *refs):
    fields, sources = refs[:FIELDS], refs[FIELDS : FIELDS + 3]
    across_a, across_b, held, lines, mixed, depth, sems, sems_lines = refs[FIELDS + 3 :]
    small = [
        pltpu.make_async_copy(source, into, sems_lines.at[k])
        for k, (source, into) in enumerate(
            zip(sources, (lines.at[pl.ds(EXTRA, EXTRA)], lines.at[1], depth))
        )
    ]

    def copy(f, lane):
        return pltpu.make_async_copy(
            fields[f].at[:, pl.ds(lane * LANES, LANES)], held.at[f, lane], sems.at[f, lane]
        )

    for f in range(FIELDS):
        for lane in range(2):
            copy(f, lane).start()
    for item in small:
        item.start()
    across_a[...] = jnp.zeros(across_a.shape, F32)
    across_b[...] = jnp.zeros(across_b.shape, F32)
    for item in small:
        item.wait()
    lines[0] = depth[...].astype(F32)
    lanes = lax.broadcasted_iota(jnp.int32, (SUB, LANES), 1)
    odd = jnp.broadcast_to(parities()[1], (SUB, LANES)) == 1
    tiles = [(c, t) for c in range(len(CHUNKS)) for t in range(CHUNKS[c])]
    for f in range(FIELDS):
        for lane in range(2):
            copy(f, lane).wait()
        for group in range(2):
            for q in range(RIM):
                place_tile(mixed.at[f, group, q], held, lines, rows, group, f, q, 0, CHUNKS[0] - 1)
        for slot, (c, t) in enumerate(tiles):
            base = (first_level(c) + SUB * t) * rows
            for group in range(2):
                west, east = across_a[group, slot], across_b[group, slot]
                for q in range(RIM):
                    place = (q * FIELDS + f) * EDGE
                    other = (place - EDGE) % LANES
                    if c == 0 and t == CHUNKS[0] - 1:
                        low = mixed[f, group, q, :, pl.ds(0, LANES)]
                        high = mixed[f, group, q, :, pl.ds(LANES, LANES)]
                    else:
                        row = pl.ds(base + first_rows()[group] + q, SUB, stride=rows)
                        low = held[f, 0, row, :]
                        high = held[f, 1, row, :]
                    if place:
                        low = pltpu.roll(low, place, 1)
                        high = pltpu.roll(high, place, 1)
                    west = jnp.where((lanes >= place) & (lanes < place + EDGE), low, west)
                    east = jnp.where((lanes >= other) & (lanes < other + EDGE), high, east)
                if f == FIELDS - 1:
                    west, east = jnp.where(odd, west, east), jnp.where(odd, east, west)
                across_a[group, slot] = west
                across_b[group, slot] = east


def place_tile(ref, held, lines, rows, group, f, q, chunk, t):
    used = min(SUB, chunk_levels(chunk) - SUB * t)
    base = (first_level(chunk) + SUB * t) * rows
    row = first_rows()[group] + q
    for lane in range(2):
        ref[pl.ds(0, used), pl.ds(lane * LANES, LANES)] = held[
            f, lane, pl.ds(base + row, used, stride=rows), :
        ]
    for extra in range(SUB - used):
        if f < 2:
            line = lines[EXTRA * f + extra, pl.ds(row, 1), :]
        else:
            line = jnp.zeros((1, 2 * LANES), F32)
        ref[pl.ds(used + extra, 1), :] = line


def halves_kernel(rows, chunks, held, lines, across_a, across_b, *halves):
    for k, c in enumerate(chunks):
        for t in range(CHUNKS[c]):
            slot = sum(CHUNKS[:c]) + t
            for group in range(2):
                half = halves[2 * k + group]
                for f in range(FIELDS):
                    for q in range(RIM):
                        ref = half.at[f * RIM + q, t]
                        place_tile(ref, held, lines, rows, group, f, q, c, t)
                half[FIELDS * RIM, t, :, pl.ds(0, LANES)] = across_a[group, slot]
                half[FIELDS * RIM, t, :, pl.ds(LANES, LANES)] = across_b[group, slot]


def pack_edges(fields, wind, surface, depth):
    levels, rows, columns = fields[0].shape
    flat = [item.reshape(levels * rows, columns) for item in fields]
    arguments = [
        pltpu.with_memory_space_constraint(item, pltpu.HBM)
        for item in (*flat, wind, surface, depth)
    ]
    vmem = pl.BlockSpec(memory_space=pltpu.VMEM)
    return pl.pallas_call(
        functools.partial(edges_kernel, rows),
        out_shape=[jax.ShapeDtypeStruct((2, sum(CHUNKS), SUB, LANES), F32)] * 2
        + [
            jax.ShapeDtypeStruct((FIELDS, 2, levels * rows, LANES), F32),
            jax.ShapeDtypeStruct((2 * EXTRA, rows, columns), F32),
        ],
        in_specs=[pl.BlockSpec(memory_space=pltpu.HBM)] * len(arguments),
        out_specs=[vmem] * 4,
        scratch_shapes=[
            pltpu.VMEM((FIELDS, 2, RIM, SUB, columns), F32),
            pltpu.VMEM(depth.shape, depth.dtype),
            pltpu.SemaphoreType.DMA((FIELDS, 2)),
            pltpu.SemaphoreType.DMA((3,)),
        ],
        compiler_params=pltpu.CompilerParams(vmem_limit_bytes=PACK_VMEM),
        name="edges",
    )(*arguments)


def pack_halves(rows, chunks, held, lines, across_a, across_b):
    vmem = pl.BlockSpec(memory_space=pltpu.VMEM)
    shapes = [
        jax.ShapeDtypeStruct((FIELDS * RIM + 1, CHUNKS[c], SUB, lines.shape[-1]), F32)
        for c in chunks
        for _ in range(2)
    ]
    outs = pl.pallas_call(
        functools.partial(halves_kernel, rows, chunks),
        out_shape=shapes,
        in_specs=[vmem] * 4,
        out_specs=[vmem] * len(shapes),
        compiler_params=pltpu.CompilerParams(vmem_limit_bytes=SMALL_VMEM),
        name="halves",
    )(held, lines, across_a, across_b)
    return [list(outs[k : k + 2]) for k in range(0, len(outs), 2)]


def east_of(value):
    return pltpu.roll(value, value.shape[-1] - 1, value.ndim - 1)


def west_of(value):
    return pltpu.roll(value, 1, value.ndim - 1)


def step_kernel(chunk, rows, *refs):
    first = chunk == 0
    last = chunk == len(CHUNKS) - 1
    tiles = CHUNKS[chunk]
    levels = chunk_levels(chunk)
    tall = rows + 2 * RIM
    refs = list(refs)

    def take(count):
        taken = refs[:count]
        del refs[:count]
        return taken

    (rotate,) = take(1)
    blocks = take(4)
    if not first:
        deeps_in, carry_in, sums_in = take(3)
        take(FIELDS)
    outs = take(FIELDS)
    if first:
        deeps, depth_out, surface_out = take(3)
    else:
        deeps = deeps_in
    if last:
        sums_a, sums_b = take(2)
    else:
        carry_out, sums_out = take(2)
    cur, wets, wets_x, wets_w, wets_y, press, press_x, press_y, laps, mixes, between, held = take(12)
    if first:
        (winds,) = take(1)
    if last:
        carry, sums = take(2)
    else:
        carry, sums = carry_out, sums_out
    (sems,) = take(1)

    if first:
        carry[...] = jnp.zeros(carry.shape, F32)
        sums[...] = jnp.zeros(sums.shape, F32)
    else:
        carry[...] = carry_in[...]
        sums[...] = sums_in[...]

    lanes = lax.broadcasted_iota(jnp.int32, (SUB, LANES), 1)
    own = blocks[0].shape[-1]
    wide = own + LANES
    every = range(FIELDS)
    odd_y, odd_x = parities()
    bases = [odd_y * (RIM * k) + (1 - odd_y) * (RIM * (3 - k)) for k in range(4)]
    swapped = ((lanes // EDGE) & 1) != 1 - odd_x

    def rims_of(k, t):
        both = blocks[k][FIELDS * RIM, t]
        one, two = both[:, :LANES], both[:, LANES:]
        mixed = (jnp.where(swapped, one, two), jnp.where(swapped, two, one))

        def rim(f, q):
            place = (q * FIELDS + f) * EDGE
            return pltpu.roll(mixed[f % 2], LANES - place, 1) if place else mixed[f % 2]

        return rim

    if first:
        for k in range(4):
            rim = rims_of(k, tiles - 1)
            for q in range(RIM):
                block = [
                    jnp.concatenate([blocks[k][f * RIM + q, tiles - 1], rim(f, q)], axis=1)
                    for f in range(2)
                ]
                for f, extra, ref in (
                    (0, 0, deeps.at[0]),
                    (0, 1, deeps.at[1]),
                    (1, 0, winds.at[0]),
                    (1, 1, winds.at[1]),
                ):
                    slot = SUB - EXTRA + extra
                    ref[bases[k] + q] = jnp.broadcast_to(block[f][slot : slot + 1, :], (SUB, wide))
        for a in range(tall):
            surface_out[pl.ds(a, 1), :] = deeps[1, a, pl.ds(0, 1), :]
            depth_out[pl.ds(a, 1), :] = deeps[0, a, pl.ds(0, 1), :]
        for a in range(tall):
            here = deeps[0, a]
            deeps[1, a] = jnp.minimum(here, east_of(here))
            deeps[2, a] = jnp.minimum(here, west_of(here))
            deeps[3, a] = jnp.minimum(here, deeps[0, min(a + 1, tall - 1)])

    subs = lax.broadcasted_iota(jnp.int32, (SUB, wide), 0)

    def pressure(get, lowest, highest, carry_at):
        for first_row in range(lowest - 1, highest + 2, BATCH):
            rows_p = range(first_row, min(first_row + BATCH, highest + 2))
            sums_p = [
                ((-0.4 * PRESS) * get(2, a) + (0.3 * PRESS) * get(3, a)) * wets[a] for a in rows_p
            ]
            for shift in (1, 2, 4):
                moved = [pltpu.roll(value, shift, 0) for value in sums_p]
                sums_p = [
                    value + jnp.where(subs >= shift, other, 0.0)
                    for value, other in zip(sums_p, moved)
                ]
            places = [carry_at + a - (lowest - 1) for a in rows_p]
            sums_p = [value + carry[place] for value, place in zip(sums_p, places)]
            ends = [jnp.broadcast_to(value[SUB - 1 : SUB, :], value.shape) for value in sums_p]
            for k, a in enumerate(rows_p):
                press[a] = sums_p[k]
                carry[places[k]] = ends[k]
        slope = wets_y[lowest - 1] * (press[lowest] - press[lowest - 1])
        for first_row in range(lowest, highest + 1, BATCH):
            rows_p = range(first_row, min(first_row + BATCH, highest + 1))
            here = [press[a] for a in rows_p]
            east = [east_of(x) for x in here]
            west = [west_of(x) for x in here]
            across = [
                wets_x[a] * (east[k] - here[k]) + wets_w[a] * (here[k] - west[k])
                for k, a in enumerate(rows_p)
            ]
            here.append(press[rows_p[-1] + 1])
            slopes = [slope] + [
                wets_y[a] * (here[k + 1] - here[k]) for k, a in enumerate(rows_p)
            ]
            slope = slopes[-1]
            for k, a in enumerate(rows_p):
                press_x[a] = across[k]
                press_y[a] = slopes[k + 1] + slopes[k]

    def tendency(get, lowest, highest, carry_at, emit, finish=None):
        pressure(get, lowest, highest, carry_at)
        widths = [own if finish is not None and group[0] > 1 else wide for group in GROUPS]
        for group, width in zip(GROUPS, widths):
            first_pass(get, lowest, highest, group, width)
        for group, width in zip(GROUPS, widths):
            second_pass(lowest, highest, group, emit, width)
            if finish is not None:
                finish(group)

    def turned(get, group, a):
        values = [get(f, a) for f in group]
        return values, [east_of(x) for x in values], [west_of(x) for x in values]

    def first_pass(get, lowest, highest, group, width):
        span = range(len(group))
        below = [get(f, lowest - 2) for f in group]
        here, east, west = turned(get, group, lowest - 1)
        face = wets_y[lowest - 2]
        up = [face * (x - y) for x, y in zip(here, below)]
        for a in range(lowest - 1, highest + 2):
            if a <= highest:
                after, east_after, west_after = turned(get, group, a + 1)
            else:
                after = [get(f, a + 1) for f in group]
            face, side_x, side_w = wets_y[a], wets_x[a], wets_w[a]
            up_before = up
            up = [face * (x - y) for x, y in zip(after, here)]
            right = [side_x * (x - y) for x, y in zip(east, here)]
            left = [side_w * (x - y) for x, y in zip(here, west)]
            lap = [(right[i] - left[i]) + (up[i] - up_before[i]) for i in span]
            if lowest <= a <= highest:
                flows = [here[group.index(f)] if f in group else get(f, a) for f in range(2)]
                u, v = (-0.5 * ADVECT) * flows[0], (-0.5 * ADVECT) * flows[1]
                mixed = [
                    u[:, :width] * (right[i] + left[i])[:, :width]
                    + v[:, :width] * (up[i] + up_before[i])[:, :width]
                    for i in span
                ]
                for i, f in enumerate(group):
                    if f < 2:
                        turn = rotate[pl.ds(a, 1), :] * wets[a]
                    if f == 0:
                        mixed[i] = mixed[i] + (turn * flows[1] - press_x[a])
                    if f == 1:
                        mixed[i] = mixed[i] - (turn * flows[0] + press_y[a])
                for i, f in enumerate(group):
                    mixes[f, a, :, pl.ds(0, width)] = mixed[i]
            for i, f in enumerate(group):
                laps[f, a] = lap[i]
            if a <= highest:
                here, east, west = after, east_after, west_after

    def second_pass(lowest, highest, group, emit, width):
        span = range(len(group))
        part = pl.ds(0, width)

        def get(f, a):
            return laps[f, a]

        below = [laps[f, lowest - 1, :, part] for f in group]
        here, east, west = turned(get, group, lowest)
        face = wets_y[lowest - 1, :, part]
        up = [face * (x[:, :width] - y) for x, y in zip(here, below)]
        for a in range(lowest, highest + 1):
            if a < highest:
                after, east_after, west_after = turned(get, group, a + 1)
            else:
                after = [get(f, a + 1) for f in group]
            face, side_x, side_w = (ref[a, :, part] for ref in (wets_y, wets_x, wets_w))
            near = [x[:, :width] for x in here]
            up_before = up
            up = [face * (x[:, :width] - y) for x, y in zip(after, near)]
            smooth = [
                (side_x * (east[i][:, :width] - near[i]) - side_w * (near[i] - west[i][:, :width]))
                + (up[i] - up_before[i])
                for i in span
            ]
            mixed = [mixes[f, a, :, part] for f in group]
            emit(a, group, [x - KAPPA * y for x, y in zip(mixed, smooth)])
            if a < highest:
                here, east, west = after, east_after, west_after

    def tile(t, _):
        for k in range(4):
            rim = rims_of(k, t)
            for q in range(RIM):
                for f in every:
                    cur[f, bases[k] + q, :, pl.ds(0, own)] = blocks[k][f * RIM + q, t]
                    cur[f, bases[k] + q, :, pl.ds(own, LANES)] = rim(f, q)
        level = subs + (first_level(chunk) + SUB * t)
        if first:
            level = jnp.where(level >= levels, FAR, level)
        level = level.astype(F32)
        top = jnp.where(level == 0.0, WIND, 0.0)
        for a in range(tall):
            for k, ref in enumerate((wets, wets_x, wets_w, wets_y)):
                ref[a] = jnp.where(level < deeps[k, a], 1.0, 0.0)

        def winded(a, group, values):
            if not first:
                return values
            return [
                value + (top * wets[a]) * winds[f, a] if f < 2 else value
                for f, value in zip(group, values)
            ]

        def emit_first(a, group, values):
            values = winded(a, group, values)
            values = [cur[f, a] + value for f, value in zip(group, values)]
            for f, value in zip(group, values):
                between[f, a] = value

        tendency(lambda f, a: cur[f, a], 2, tall - 3, 0, emit_first)

        def emit_second(a, group, values):
            values = winded(a, group, values)
            part = pl.ds(0, values[0].shape[-1])
            news = [
                0.5 * ((cur[f, a, :, part] + between[f, a, :, part]) + value)
                for f, value in zip(group, values)
            ]
            r = a - RIM
            adds = [sums[f, r] + wets[a] * new for f, new in zip(group, news) if f < 2]
            for f, add in zip(group, adds):
                sums[f, r] = add
            for f, new in zip(group, news):
                for lane in range(2):
                    held[f, lane, pl.ds(t * (SUB * rows) + r, SUB, stride=rows), :] = new[
                        :, lane * LANES : (lane + 1) * LANES
                    ]

        def finish(group):
            def leave(count):
                for f in group:
                    for lane in range(2):
                        copy(f, lane, t, count).start()

            if final == SUB:
                leave(SUB)
            else:
                pl.when(t < tiles - 1)(lambda: leave(SUB))
                pl.when(t == tiles - 1)(lambda: leave(final))

        tendency(lambda f, a: between[f, a], RIM, tall - RIM - 1, tall - 2, emit_second, finish)
        return 0

    def copy(f, lane, t, count):
        size = count * rows
        at = (first_level(chunk) + SUB * t) * rows
        return pltpu.make_async_copy(
            held.at[f, lane, pl.ds(t * (SUB * rows), size)],
            outs[f].at[pl.ds(at, size), pl.ds(lane * LANES, LANES)],
            sems.at[t, f, lane],
        )

    final = levels - SUB * (tiles - 1)
    lax.fori_loop(0, tiles, tile, 0)
    if last:
        depth_levels = first_level(chunk) + levels
        for f in range(2):
            for ref, at in ((sums_a, (1 - odd_y) * RIM), (sums_b, odd_y * RIM)):
                for q in range(RIM):
                    line = jnp.sum(sums[f, at + q], axis=0, keepdims=True) / depth_levels
                    ref[f, pl.ds(q, 1), :] = line
    for t in range(tiles):
        for f in every:
            for lane in range(2):
                copy(f, lane, t, final if t == tiles - 1 else SUB).wait()


def step(chunk, rows, levels, columns, rotate, blocks, kept, news):
    first = chunk == 0
    last = chunk == len(CHUNKS) - 1
    tiles = CHUNKS[chunk]
    wide = columns + LANES
    tall = rows + 2 * RIM
    vmem = pl.BlockSpec(memory_space=pltpu.VMEM)
    hbm = pl.BlockSpec(memory_space=pl.ANY)
    operands = [rotate, *blocks]
    in_specs = [vmem] * 5
    if not first:
        operands += [*kept, *news]
        in_specs += [vmem] * 3 + [hbm] * FIELDS
    carry = (tall - 2 + rows + 2, SUB, wide)
    sums = (2, rows, SUB, wide)
    shapes = [jax.ShapeDtypeStruct((levels * rows, columns), F32)] * FIELDS
    out_specs = [hbm] * FIELDS
    row = pltpu.VMEM((tall, SUB, wide), F32)
    fields = pltpu.VMEM((FIELDS, tall, SUB, wide), F32)
    scratch = [fields] + [row] * 7 + [fields] * 3
    scratch += [pltpu.VMEM((FIELDS, 2, tiles * SUB * rows, LANES), F32)]
    if first:
        shapes += [jax.ShapeDtypeStruct((4, tall, SUB, wide), F32)]
        shapes += [jax.ShapeDtypeStruct((tall, wide), F32)] * 2
        scratch += [pltpu.VMEM((2, tall, SUB, wide), F32)]
    if last:
        shapes += [jax.ShapeDtypeStruct((2, RIM, wide), F32)] * 2
        scratch += [pltpu.VMEM(carry, F32), pltpu.VMEM(sums, F32)]
    else:
        shapes += [jax.ShapeDtypeStruct(carry, F32), jax.ShapeDtypeStruct(sums, F32)]
    out_specs += [vmem] * (len(shapes) - FIELDS)
    scratch += [pltpu.SemaphoreType.DMA((tiles, FIELDS, 2))]
    aliases = {} if first else {len(operands) - FIELDS + f: f for f in range(FIELDS)}
    return pl.pallas_call(
        functools.partial(step_kernel, chunk, rows),
        out_shape=shapes,
        in_specs=in_specs,
        out_specs=out_specs,
        scratch_shapes=scratch,
        input_output_aliases=aliases,
        compiler_params=pltpu.CompilerParams(vmem_limit_bytes=16 * 1024 * 1024),
        name="step",
    )(*operands)


def shift_rows(x, count):
    return pltpu.roll(x, count % x.shape[0], 0)


def weighed(weights, e):
    east, west = east_of(e), west_of(e)
    return (
        weights[0] * shift_rows(east, -1) + weights[1] * shift_rows(west, -1)
    ) + (weights[2] * shift_rows(east, 1) + weights[3] * shift_rows(west, 1))


def prepare_kernel(levels, deep_ref, surface_ref, out):
    deep = deep_ref[...]
    surface = surface_ref[...]
    ocean = jnp.where(deep > 0.0, 1.0, 0.0)
    pair = jnp.minimum(deep, east_of(deep))
    north_east = jnp.minimum(pair, shift_rows(pair, -1)) / levels
    north_west = west_of(north_east)
    corners = (north_east, north_west, shift_rows(north_east, 1), shift_rows(north_west, 1))
    share = 1.0 / (PHI + 0.5 * ((corners[0] + corners[1]) + (corners[2] + corners[3])))
    weights = [(0.5 * share) * corner for corner in corners]
    for k in range(4):
        out[k] = weights[k]
    out[4] = (PHI * ocean * share) * surface - (surface - weighed(weights, surface))
    across = ocean * east_of(ocean)
    along = ocean * shift_rows(ocean, -1)
    scale = (-0.5 * DIVERGE) * share
    out[5] = scale * across
    out[6] = scale * west_of(across)
    out[7] = scale * along
    out[8] = scale * shift_rows(along, 1)
    out[9] = surface


def solve_kernel(rows, ready, met_a, own_a, own_b, met_b, out):
    odd = jnp.broadcast_to(parities()[0], ready.shape[1:]) == 1
    flows = []
    for f in range(2):
        lines = [ref[f] for ref in (met_a, own_a, own_b, met_b)]
        flows.append(
            jnp.where(odd, jnp.concatenate(lines, axis=0), jnp.concatenate(lines[::-1], axis=0))
        )
    weights = [ready[k] for k in range(4)]
    east, north = flows
    scaled = ready[4] + (
        (ready[5] * (east_of(east) - east) + ready[6] * (east - west_of(east)))
        + (
            ready[7] * (shift_rows(north, -1) - north)
            + ready[8] * (north - shift_rows(north, 1))
        )
    )
    opening, updates = chebyshev_weights(ITERS)
    direction = opening * scaled
    total = ready[9]
    for index in range(ITERS):
        total = total + direction
        if index + 1 < ITERS:
            scaled = scaled - (direction - weighed(weights, direction))
            keep, push = updates[index]
            direction = keep * direction + push * scaled
    out[...] = total[RIM : RIM + rows, : out.shape[1]]


def body(
    eastward_flow,
    northward_flow,
    heat_anomaly,
    salt_anomaly,
    air_stress_forcing,
    earlier_sea_height_load,
    ocean_layer_depths,
):
    levels, rows, columns = eastward_flow.shape
    assert rows == 2 * RIM and columns == 2 * LANES and levels + EXTRA == SUB * sum(CHUNKS)
    along_y, along_x = lax.axis_size("by"), lax.axis_size("bx")
    pairs_y = (swaps(along_y, 0, False), swaps(along_y, 1, False))
    pairs_x = (swaps(along_x, 0, True), swaps(along_x, 1, True))
    row_index = lax.axis_index("by") * rows - RIM + jnp.arange(rows + 2 * RIM)
    rotate = 1.2 * jnp.sin(
        0.9 * math.pi * ((row_index.astype(F32) + 0.5) / (rows * along_y) - 0.5)
    )
    rotate = jnp.broadcast_to(rotate[:, None], (rows + 2 * RIM, columns + LANES))

    fields = (eastward_flow, northward_flow, heat_anomaly, salt_anomaly)
    edge_a, edge_b, held, lines = pack_edges(
        fields, air_stress_forcing, earlier_sea_height_load, ocean_layer_depths
    )
    across_a = lax.ppermute(edge_a, "bx", pairs_x[0])
    across_b = lax.ppermute(edge_b, "bx", pairs_x[1])
    made = (held, lines, across_a, across_b)
    halves = pack_halves(rows, (0,), *made)
    halves += pack_halves(rows, tuple(range(1, len(CHUNKS))), *made)

    def send(own):
        return [lax.ppermute(item, "by", pairs) for item, pairs in zip(own, pairs_y)]

    rims = [send(halves[chunk]) for chunk in range(AHEAD)]
    kept, news = None, None
    for chunk in range(len(CHUNKS)):
        own_a, own_b = halves[chunk]
        met_a, met_b = rims[chunk]
        blocks = [met_a, own_a, own_b, met_b]
        outs = step(chunk, rows, levels, columns, rotate, blocks, kept, news)
        news, rest = outs[:FIELDS], outs[FIELDS:]
        if chunk == 0:
            deeps, depth_wide, surface_wide = rest[:3]
            rest = rest[3:]
        later = chunk + AHEAD
        if later < len(CHUNKS):
            *halves[later], one, two = lax.optimization_barrier((*halves[later], *rest))
            rest = (one, two)
            rims.append(send(halves[later]))
        kept = (deeps, *rest)
    own_a, own_b = rest
    depth_wide, surface_wide, own_a, own_b = lax.optimization_barrier(
        (depth_wide, surface_wide, own_a, own_b)
    )
    met_a, met_b = send((own_a, own_b))
    vmem = pl.BlockSpec(memory_space=pltpu.VMEM)
    ready = pl.pallas_call(
        functools.partial(prepare_kernel, levels),
        out_shape=jax.ShapeDtypeStruct((10, *depth_wide.shape), F32),
        in_specs=[vmem] * 2,
        out_specs=vmem,
        compiler_params=pltpu.CompilerParams(vmem_limit_bytes=SMALL_VMEM),
        name="prepare",
    )(depth_wide, surface_wide)
    surface_new = pl.pallas_call(
        functools.partial(solve_kernel, rows),
        out_shape=jax.ShapeDtypeStruct((rows, columns), F32),
        in_specs=[vmem] * 5,
        out_specs=vmem,
        compiler_params=pltpu.CompilerParams(vmem_limit_bytes=SMALL_VMEM),
        name="solve",
    )(ready, met_a, own_a, own_b, met_b)
    shaped = [item.reshape(levels, rows, columns) for item in news]
    return (*shaped, surface_new)


def solution(mesh):
    return jax.shard_map(
        body,
        mesh=mesh,
        in_specs=(P(None, "by", "bx"),) * 5 + (P("by", "bx"),) * 2,
        out_specs=(P(None, "by", "bx"),) * 4 + (P("by", "bx"),),
        check_vma=False,
    )
```
